32 devices in a mesh: seq: 16 (over z, y, core), fsdp: 2 (over x).
Axes of the slice: x: 2, y: 2, z: 4, core: 2. Of those that a mesh axis runs over, the one named last changes fastest.
Arguments:
- tokens: bfloat16 [2, 4096, 2048], P('fsdp', 'seq'), may hold values from -6 to 6
- seq_lengths: int32 [2, 4], P('fsdp'), may hold values from 1 to 4009, as said below
- norm_gain: bfloat16 [2048], P(('seq', 'fsdp')), may hold values from 0.25 to 1.75
- w_query: bfloat16 [2048, 256], P(('seq', 'fsdp')), may hold values from -0.125 to 0.125
- w_key: bfloat16 [2048, 256], P(('seq', 'fsdp')), may hold values from -0.125 to 0.125
- w_value: bfloat16 [2048, 2048], P(('seq', 'fsdp')), may hold values from -0.125 to 0.125
- w_out: bfloat16 [2048, 2048], P(('seq', 'fsdp')), may hold values from -4 to 4
- mlp_gain: bfloat16 [2048], P(('seq', 'fsdp')), may hold values from 0.25 to 1.75
- w_gate: bfloat16 [2048, 5632], P(('seq', 'fsdp')), may hold values from -0.125 to 0.125
- w_up: bfloat16 [2048, 5632], P(('seq', 'fsdp')), may hold values from -0.125 to 0.125
- w_down: bfloat16 [5632, 2048], P(('seq', 'fsdp')), may hold values from -0.078125 to 0.078125
- cotangent: bfloat16 [2, 4096, 2048], P('fsdp', 'seq'), may hold values from -6 to 6
Outputs:
- block_out: float32 [2, 4096, 2048], P('fsdp', 'seq')
- input_grad: float32 [2, 4096, 2048], P('fsdp', 'seq')
- norm_gain_grad: float32 [2048], P(('seq', 'fsdp'))
- w_query_grad: float32 [2048, 256], P(('seq', 'fsdp'))
- w_key_grad: float32 [2048, 256], P(('seq', 'fsdp'))
- w_value_grad: float32 [2048, 2048], P(('seq', 'fsdp'))
- w_out_grad: float32 [2048, 2048], P(('seq', 'fsdp'))
- mlp_gain_grad: float32 [2048], P(('seq', 'fsdp'))
- w_gate_grad: float32 [2048, 5632], P(('seq', 'fsdp'))
- w_up_grad: float32 [2048, 5632], P(('seq', 'fsdp'))
- w_down_grad: float32 [5632, 2048], P(('seq', 'fsdp'))
The draws below stay inside these ranges and needn't reach their ends.
Inputs may be any that keep to these rules, and one draw needn't show every extreme that they name: `seq_lengths`: each row sums to 4096. In each row all entries but one lie between 1 and (255) // 3, and one of them equals that bound. In some row of every draw all entries but two equal 1.
All inputs are finite; a program needn't handle non-finite values.
Results may differ from the reference program's by a relative error of at most 0.017.
Values may be sent and summed in bfloat16 or wider, within the bound.
No kernel may reach another device: no remote copies, remote signals or barrier semaphores. Data moves between devices by JAX's collectives and lax.ppermute only.
A program may use at most 512 MiB of HBM per device.

```python
import math
import jax
import jax.numpy as jnp
from jax import lax

D = 2048
H = 16
FD = 16
DV = 128
FF = 5632
PHI = 273
TOK_DEV = 256
SEQS = 4
GROUPS = 2
GROUP_TOK = 4096
N_SEQ = 16


def draw_seq_lengths(key, part):
    key = jax.random.fold_in(key, 7)
    key_span, key_short, key_group = jax.random.split(key, 3)
    span_index = jax.random.randint(key_span, (GROUPS,), 0, SEQS)
    short_top = (TOK_DEV - 1) // (SEQS - 1)
    short_rows = jax.random.randint(key_short, (GROUPS, SEQS), 1, short_top + 1)
    chosen_group = jax.random.randint(key_group, (), 0, GROUPS)
    group_ids = jnp.arange(GROUPS)
    short_rows = jnp.where((group_ids == chosen_group)[:, None], 1, short_rows)
    columns = jnp.arange(SEQS)
    is_span = columns[None, :] == span_index[:, None]
    is_top = columns[None, :] == ((span_index + 1) % SEQS)[:, None]
    others = jnp.where(is_span, 0, jnp.where(is_top, short_top, short_rows))
    remaining = GROUP_TOK - jnp.sum(others, axis=1, keepdims=True)
    return jnp.where(is_span, remaining, others).astype(jnp.int32)


def block_scale(rng, extent, cuts, least, top_value):
    def one(dim, blocks):
        heights = jax.random.uniform(jax.random.fold_in(jax.random.fold_in(rng, 6), dim), (blocks,), jnp.float32, least / len(cuts), top_value / len(cuts))
        return jnp.repeat(jnp.exp(heights), extent[dim] // blocks).reshape((-1,) + (1,) * (len(extent) - dim - 1))

    gain = one(*cuts[0])
    for cut in cuts[1:]:
        gain = gain * one(*cut)
    return gain


def centred(rng, dims, spread, reach, pieces=(), kind=jnp.bfloat16):
    gain = block_scale(rng, dims, pieces, -0.22, 0.18) if pieces else 1.0
    result = jax.random.normal(rng, dims, jnp.float32) * spread * gain
    return jnp.minimum(jnp.maximum(result, -reach), reach).astype(kind)


def setup_inputs(seed: int = 0) -> dict:
    seeds = jax.random.split(jax.random.key(seed), 13)
    return {
        "tokens": centred(seeds[0], (GROUPS, GROUP_TOK, D), 1.0, 6.0, ((0, 2), (1, 16))),
        "seq_lengths": draw_seq_lengths(jax.random.fold_in(seeds[12], 71), 0),
        "norm_gain": jnp.clip(1.0 + 0.15 * jax.random.normal(seeds[2], (D,), jnp.float32), 0.25, 1.75).astype(jnp.bfloat16),
        "w_query": centred(seeds[3], (D, H * FD), D ** -0.5, 0.125, ((0, 32),)),
        "w_key": centred(seeds[4], (D, H * FD), D ** -0.5, 0.125, ((0, 32),)),
        "w_value": centred(seeds[5], (D, H * DV), D ** -0.5, 0.125, ((0, 32),)),
        "w_out": centred(seeds[6], (H * DV, D), (max(1, (H * DV) // (GROUP_TOK // 4))) ** -0.5, 4.0, ((0, 32),)),
        "mlp_gain": jnp.clip(1.0 + 0.15 * jax.random.normal(seeds[7], (D,), jnp.float32), 0.25, 1.75).astype(jnp.bfloat16),
        "w_gate": centred(seeds[8], (D, FF), D ** -0.5, 0.125, ((0, 32),)),
        "w_up": centred(seeds[9], (D, FF), D ** -0.5, 0.125, ((0, 32),)),
        "w_down": centred(seeds[10], (FF, D), FF ** -0.5, 0.078125, ((0, 32),)),
        "cotangent": centred(seeds[11], (GROUPS, GROUP_TOK, D), 1.0, 6.0, ((0, 2), (1, 16))),
    }


@jax.custom_vjp
def low(v):
    return lax.optimization_barrier(v.astype(jnp.bfloat16)).astype(jnp.float32)

@jax.custom_vjp
def low_back(v):
    return v

def low_keep(v):
    return (low(v), None)

def low_pass(kept, grad):
    return (grad,)

def back_keep(v):
    return (v, None)

def back_low(kept, grad):
    return (low(grad),)
low.defvjp(low_keep, low_pass)
low_back.defvjp(back_keep, back_low)

def matmul(left, right):
    return jnp.dot(left, right, precision=lax.Precision.HIGHEST, preferred_element_type=jnp.float32)

def rms_scale(values, gain_vec):
    return values * lax.rsqrt(lax.optimization_barrier(jnp.mean(values * values, axis=-1, keepdims=True)) + 1e-05) * gain_vec

def taylor(values):
    feat_width = values.shape[-1]
    outer_prod = (values[..., :, None] * values[..., None, :]).reshape(values.shape[:-1] + (feat_width * feat_width,))
    ones_col = jnp.ones(values.shape[:-1] + (1,), values.dtype)
    return jnp.concatenate([ones_col, values / math.sqrt(math.sqrt(feat_width)), outer_prod / (math.sqrt(2.0) * math.sqrt(feat_width))], axis=-1)

def block_masks(lengths):
    seq_ends = jnp.cumsum(lengths).astype(jnp.int32)
    places = jnp.arange(GROUP_TOK, dtype=jnp.int32)
    segment = lax.optimization_barrier(jnp.sum((places[:, None] >= seq_ends[None, :]).astype(jnp.int32), axis=1)).astype(jnp.int32)
    blocks = segment.reshape(N_SEQ, TOK_DEV)
    before = jnp.concatenate([jnp.full((1,), -1, jnp.int32), blocks[:-1, -1]])
    continues = (blocks == before[:, None]).astype(jnp.float32)
    tail_rows = (blocks == blocks[:, -1:]).astype(jnp.float32)
    return (blocks, continues, tail_rows)

def forward(hidden_in, norm_gain, w_query, w_key, w_value, w_out, mlp_gain, w_gate, w_up, w_down, blocks, continues, tail_rows):
    normed = low(rms_scale(hidden_in, norm_gain))
    queries = low_back(matmul(normed, w_query))
    key_rows = low_back(matmul(normed, w_key))
    value_rows = low_back(matmul(normed, w_value))
    feat_query = low(taylor(queries.reshape(N_SEQ, TOK_DEV, H, FD)))
    feat_key = low(taylor(key_rows.reshape(N_SEQ, TOK_DEV, H, FD)))
    values_low = low(value_rows.reshape(N_SEQ, TOK_DEV, H, DV))
    index_row = jnp.arange(TOK_DEV)
    causal = index_row[:, None] >= index_row[None, :]
    highest = lax.Precision.HIGHEST

    def block_step(carried, inputs):
        state_sum, den_state = carried
        query_blk, key_blk, value_blk, seg_row, cont_row, tail_row = inputs
        pair_mask = ((seg_row[:, None] == seg_row[None, :]) & causal).astype(jnp.float32)
        scores = low_back(jnp.einsum('thp,shp->hts', query_blk, key_blk, precision=highest) * pair_mask[None])
        scores_low = low(scores)
        state_low = low(state_sum)
        numerator = jnp.einsum('hts,shv->thv', scores_low, value_blk, precision=highest)
        numerator = numerator + cont_row[:, None, None] * jnp.einsum('thp,hpv->thv', query_blk, state_low, precision=highest)
        numerator = low_back(numerator)
        denominator = lax.optimization_barrier(jnp.sum(scores, axis=2)).T + cont_row[:, None] * jnp.einsum('thp,hp->th', query_blk, den_state, precision=highest)
        attn_blk = numerator / denominator[:, :, None]
        added_state = low_back(jnp.einsum('thp,thv->hpv', key_blk, value_blk * tail_row[:, None, None], precision=highest))
        carry_on = cont_row[-1]
        new_state = carry_on * state_sum + added_state
        new_den = carry_on * den_state + jnp.einsum('thp,t->hp', key_blk, tail_row, precision=highest)
        return ((new_state, new_den), attn_blk)
    initial = (jnp.zeros((H, PHI, DV), jnp.float32), jnp.zeros((H, PHI), jnp.float32))
    _, attn_all = lax.scan(jax.checkpoint(block_step), initial, (feat_query, feat_key, values_low, blocks, continues, tail_rows))
    mixed_heads = low(attn_all.reshape(GROUP_TOK, H * DV))
    residual = hidden_in + low_back(matmul(mixed_heads, w_out))
    normed_two = low(rms_scale(residual, mlp_gain))
    gate_rows = low_back(matmul(normed_two, w_gate))
    up_rows = low_back(matmul(normed_two, w_up))
    hidden = low(jax.nn.silu(gate_rows) * up_rows)
    return residual + low_back(matmul(hidden, w_down))

def reference(tokens, seq_lengths, norm_gain, w_query, w_key, w_value, w_out, mlp_gain, w_gate, w_up, w_down, cotangent):
    weight_args = tuple((weight_arg.astype(jnp.float32) for weight_arg in (norm_gain, w_query, w_key, w_value, w_out, mlp_gain, w_gate, w_up, w_down)))

    def one_group(grad_sums, inputs):
        group_tokens, lengths, group_cot = inputs
        blocks, continues, tail_rows = block_masks(lengths)

        def wrapped(hidden_in, *params):
            return forward(hidden_in, *params, blocks, continues, tail_rows)
        out_vals, pull = jax.vjp(wrapped, group_tokens.astype(jnp.float32), *weight_args)
        pulled = pull(group_cot.astype(jnp.float32))
        new_sums = tuple((running + piece for running, piece in zip(grad_sums, pulled[1:])))
        return (new_sums, (out_vals, pulled[0]))
    zero_grads = tuple((jnp.zeros_like(weight_arg) for weight_arg in weight_args))
    grad_sums, (block_outs, input_grads) = lax.scan(one_group, zero_grads, (tokens, seq_lengths, cotangent))
    return (block_outs, input_grads, grad_sums[0], grad_sums[1], grad_sums[2], grad_sums[3], grad_sums[4], grad_sums[5], grad_sums[6], grad_sums[7], grad_sums[8])
```

```python
import jax
import jax.numpy as jnp
import numpy as np
from jax import lax
from jax.sharding import Mesh
from jax.sharding import PartitionSpec as P

H = 16
FD = 16
DV = 128
HP = 2
TP = ("l", "y", "c")
DP = ("h", "x")
EPS = 1e-5
F32, BF16 = jnp.float32, jnp.bfloat16
HIGH = lax.Precision.HIGHEST


def dot(a, b, dims):
    return lax.dot_general(a, b, (dims, ((), ())), preferred_element_type=F32)


def mm(a, b):
    return dot(a, b, ((1,), (0,)))


def mm_nt(a, b):
    return dot(a, b, ((1,), (1,)))


def mm_tn(a, b):
    return dot(a, b, ((0,), (0,)))


def swap(a, axis):
    return lax.ppermute(a, axis, [(0, 1), (1, 0)])


def gather_tokens(own):
    half = own.shape[0] // 2
    from_l, from_y = swap(own, "l"), swap(own, "y")
    far = jnp.concatenate([swap(from_y[:half], "l"), swap(from_l[half:], "y")], 0)
    same = [own, from_y, from_l, far]
    return [b for s in same for b in (s, swap(s, "c"))]


def scatter_tokens(parts):
    half = parts[0].shape[0] // 2
    pair = lambda r: parts[r].astype(F32) + swap(parts[r ^ 1], "c").astype(F32)
    far = pair(6).astype(BF16)
    via_l, via_y = swap(far[:half], "l").astype(F32), swap(far[half:], "y").astype(F32)
    for_y, for_l = pair(2), pair(4)
    for_y = jnp.concatenate([for_y[:half] + via_l, for_y[half:]], 0).astype(BF16)
    for_l = jnp.concatenate([for_l[:half], for_l[half:] + via_y], 0).astype(BF16)
    return pair(0) + swap(for_l, "l").astype(F32) + swap(for_y, "y").astype(F32)


def reorder(blocks):
    me = lax.axis_index(TP)
    return jnp.stack([lax.dynamic_index_in_dim(blocks, p ^ me, 0, keepdims=False) for p in range(8)])


def flips(a):
    a = jnp.where(lax.axis_index("h") == 0, a, a[::-1])
    return jnp.where(lax.axis_index("x") == 0, a, a[:, ::-1])


def gather_weights(a):
    if lax.axis_size("h") == 2 and lax.axis_size("x") == 2:
        over_h = swap(a, "h")
        rel = jnp.stack([jnp.stack([a, swap(a, "x")]), jnp.stack([over_h, swap(over_h, "x")])])
        return flips(rel)
    full = lax.all_gather(a, DP)
    return full.reshape((lax.axis_size("h"), lax.axis_size("x")) + a.shape)


def scatter_weights(parts):
    if parts.shape[:2] == (2, 2):
        rel = flips(parts)
        near = rel[0, 0].astype(F32) + swap(rel[0, 1], "x").astype(F32)
        over = rel[1, 0].astype(F32) + swap(rel[1, 1], "x").astype(F32)
        return near + swap(over.astype(BF16), "h").astype(F32)
    flat = parts.reshape((-1,) + parts.shape[2:])
    return lax.psum_scatter(flat, DP, scatter_dimension=0, tiled=False).astype(F32)


def sub_head():
    return lax.axis_size(DP + TP) // H == 2 * lax.axis_size("x")


def split_heads(w, width):
    rows = w.shape[0]
    if sub_head():
        w = w.reshape(rows, 2, HP, 2, 2, width).transpose(3, 4, 1, 0, 2, 5)
    else:
        w = w.reshape(rows, HP, 8, width).transpose(2, 0, 1, 3)
    return w.reshape(8, rows, HP * width)


def join_heads(w, width):
    rows = w.shape[1]
    if sub_head():
        w = w.reshape(2, 2, 2, rows, HP, width).transpose(3, 2, 4, 0, 1, 5)
    else:
        w = w.reshape(8, rows, HP, width).transpose(1, 2, 0, 3)
    return w.reshape(rows, H * width)


def split_hidden(w):
    h, x = lax.axis_size("h"), lax.axis_size("x")
    rows = w.shape[0]
    w = w.reshape(rows, h, 8, x, -1).transpose(2, 0, 1, 3, 4)
    return w.reshape(8, rows, -1)


def join_hidden(w):
    h, x = lax.axis_size("h"), lax.axis_size("x")
    rows = w.shape[1]
    w = w.reshape(8, rows, h, x, -1).transpose(1, 2, 0, 3, 4)
    return w.reshape(rows, -1)


def columns_in(w):
    rows, n = w.shape[1:]
    mine = lax.all_to_all(w, TP, 0, 0, tiled=True)
    full = gather_weights(mine.reshape(8 * rows, n))
    h, x = full.shape[:2]
    return full.reshape(h, x, 8, rows, n).transpose(0, 2, 1, 3, 4).reshape(-1, n)


def columns_out(grad):
    h, x = lax.axis_size("h"), lax.axis_size("x")
    n = grad.shape[1]
    parts = grad.reshape(h, 8, x, -1, n).transpose(0, 2, 1, 3, 4)
    mine = scatter_weights(parts).astype(BF16)
    return lax.all_to_all(mine, TP, 0, 0, tiled=True)


def out_rows_in(w):
    full = gather_weights(w)
    if sub_head():
        h, x, rows, d = full.shape
        full = lax.all_to_all(full.reshape(2, h // 2, x, rows, d), "c", 0, 0, tiled=True)
        full = full.transpose(1, 0, 2, 3, 4)
    return full.reshape(HP * DV, -1)


def out_rows_out(grad):
    h, x = lax.axis_size("h"), lax.axis_size("x")
    d = grad.shape[1]
    if sub_head():
        grad = grad.reshape(HP, 2, x, -1, d).transpose(1, 0, 2, 3, 4)
        grad = lax.all_to_all(grad, "c", 0, 0, tiled=True)
    return scatter_weights(grad.reshape(h, x, -1, d))


def entering(total, reverse):
    n = lax.axis_size("h")
    low = total.astype(BF16)
    got = jnp.zeros_like(total)
    for s in range(1, n):
        route = [(i + s, i) if reverse else (i, i + s) for i in range(n - s)]
        got = got + lax.ppermute(low, "h", route).astype(F32)
    return got


PAIRS = [(i, j) for i in range(FD + 1) for j in range(i, FD + 1)]
LEFT = np.zeros((FD + 1, len(PAIRS)), np.float32)
RIGHT = np.zeros((FD + 1, len(PAIRS)), np.float32)
for col, (i, j) in enumerate(PAIRS):
    LEFT[i, col] = 1.0
    RIGHT[j, col] = 2.0**-0.5 if i == j < FD else 1.0


def features(u):
    wide = jnp.concatenate([u * 0.5, jnp.ones(u.shape[:-1] + (1,), u.dtype)], -1)
    return jnp.dot(wide, LEFT, precision=HIGH) * jnp.dot(wide, RIGHT, precision=HIGH)


def ein(spec, a, b):
    return jnp.einsum(spec, a, b, preferred_element_type=F32)


def masks(lengths, tokens, chunk):
    ends = jnp.cumsum(lengths)
    places = lax.axis_index("h") * tokens + jnp.arange(tokens, dtype=jnp.int32)
    segment = jnp.sum((places[:, None] >= ends[None, :]).astype(jnp.int32), 1).reshape(-1, chunk)
    crosses = (segment == jnp.argmax(lengths)).astype(F32)
    row = jnp.arange(chunk)
    pairs = (segment[:, :, None] == segment[:, None, :]) & (row[:, None] >= row[None, :])
    return crosses, pairs.astype(F32)


def attention(queries, keys, values, crosses, pairs):
    taylor_q, pull_q = jax.vjp(features, queries)
    taylor_k, pull_k = jax.vjp(features, keys)
    feat_q = (taylor_q * crosses[:, :, None, None]).astype(BF16)
    feat_k = (taylor_k * crosses[:, :, None, None]).astype(BF16)
    flat = jnp.einsum("cthe,cshe->chts", queries, keys, precision=HIGH) * 0.25
    scores = (1.0 + flat + 0.5 * flat * flat) * pairs[:, None]
    low = scores.astype(BF16)
    added = ein("cshf,cshv->chfv", feat_k, values)
    added_den = jnp.sum(feat_k.astype(F32), 1)
    both = jnp.concatenate([added, added_den[..., None]], -1)
    state = entering(jnp.sum(both, 0), False) + jnp.cumsum(both, 0) - both
    state_low, den_state = state[..., :DV].astype(BF16), state[..., DV].astype(BF16)
    numer = ein("chts,cshv->cthv", low, values) + ein("cthf,chfv->cthv", feat_q, state_low)
    denom = jnp.sum(scores, -1).transpose(0, 2, 1) + ein("cthf,chf->cth", feat_q, den_state)
    attn = numer / denom[..., None]

    def back(d_attn):
        d_numer = (d_attn / denom[..., None]).astype(BF16)
        d_denom = -jnp.sum(d_attn * attn, -1) / denom
        use = ein("cthf,cthv->chfv", feat_q, d_numer)
        use_den = ein("cthf,cth->chf", feat_q, d_denom.astype(BF16))
        both = jnp.concatenate([use, use_den[..., None]], -1)
        total = jnp.sum(both, 0)
        later = entering(total, True) + total - jnp.cumsum(both, 0)
        back_low, back_den = later[..., :DV].astype(BF16), later[..., DV]
        d_scores = ein("cthv,cshv->chts", d_numer, values) + d_denom.transpose(0, 2, 1)[..., None]
        d_flat = (d_scores * pairs[:, None] * (1.0 + flat) * 0.25).astype(BF16)
        d_feat_q = ein("cthv,chfv->cthf", d_numer, state_low) + d_denom[..., None] * den_state.astype(F32)[:, None]
        d_feat_k = ein("cshv,chfv->cshf", values, back_low) + back_den[:, None]
        d_q = ein("chts,cshe->cthe", d_flat, keys.astype(BF16)) + pull_q(d_feat_q * crosses[:, :, None, None])[0]
        d_k = ein("chts,cthe->cshe", d_flat, queries.astype(BF16)) + pull_k(d_feat_k * crosses[:, :, None, None])[0]
        d_v = ein("chts,cthv->cshv", low, d_numer) + ein("cshf,chfv->cshv", feat_k, back_low)
        return d_q, d_k, d_v

    return attn, back


def stack(blocks):
    return jnp.concatenate(blocks, 0)


def unstack(rows):
    return list(rows.reshape(8, -1, rows.shape[-1]))


def on_device(
    tokens, seq_lengths, norm_gain, w_query, w_key, w_value, w_out, mlp_gain, w_gate, w_up, w_down, cotangent
):
    x_low = tokens[0]
    x_own, dy_own = x_low.astype(F32), cotangent[0].astype(F32)
    size, d_model = x_own.shape
    gain_one = norm_gain.astype(F32)[:, None]
    gain_two = mlp_gain.astype(F32)[:, None]
    crosses, pairs = masks(seq_lengths[0], 8 * size, size)

    gained = lambda gain, w: (gain * w.astype(F32)).astype(BF16)
    w_qkv = columns_in(
        jnp.concatenate(
            [
                split_heads(gained(gain_one, w_value), DV),
                split_heads(gained(gain_one, w_query), FD),
                split_heads(gained(gain_one, w_key), FD),
            ],
            -1,
        )
    )
    x_all = stack(gather_tokens(x_low))
    w_out_mine = out_rows_in(w_out)
    w_gu = columns_in(
        jnp.concatenate([split_hidden(gained(gain_two, w_gate)), split_hidden(gained(gain_two, w_up))], -1)
    )
    w_down_mine = gather_weights(w_down).reshape(-1, d_model)
    ff = w_down_mine.shape[0]

    r_all = lax.rsqrt(jnp.mean(jnp.square(x_all.astype(F32)), -1, keepdims=True) + EPS)
    qkv = reorder((mm(x_all, w_qkv) * r_all).reshape(8, size, -1))
    nv, nq = HP * DV, HP * FD
    values = qkv[..., :nv].astype(BF16).reshape(8, size, HP, DV)
    queries = qkv[..., nv : nv + nq].reshape(8, size, HP, FD)
    keys = qkv[..., nv + nq :].reshape(8, size, HP, FD)
    attn, attention_back = attention(queries, keys, values, crosses, pairs)
    mixed = reorder(attn.astype(BF16).reshape(8, size, nv)).reshape(8 * size, nv)
    branch = scatter_tokens(unstack(mm(mixed, w_out_mine).astype(BF16)))
    resid = x_own + branch
    r_two = lax.rsqrt(jnp.mean(resid * resid, -1, keepdims=True) + EPS)
    n_two = resid * r_two

    n_all = stack(gather_tokens(n_two.astype(BF16)))
    dy_all = stack(gather_tokens(cotangent[0]))
    gu = mm(n_all, w_gu)
    gate, up = gu[:, :ff], gu[:, ff:]
    sig = jax.nn.sigmoid(gate)
    silu = gate * sig
    hidden = (silu * up).astype(BF16)
    d_hidden = mm_nt(dy_all, w_down_mine)
    d_gate = d_hidden * up * sig * (1.0 + gate * (1.0 - sig))
    d_gu = jnp.concatenate([d_gate, d_hidden * silu], 1).astype(BF16)
    d_n_two = scatter_tokens(unstack(mm_nt(d_gu, w_gu).astype(BF16)))
    block_out = resid + scatter_tokens(unstack(mm(hidden, w_down_mine).astype(BF16)))
    g_gu = columns_out(mm_tn(n_all, d_gu).astype(BF16))
    g_down = scatter_weights(
        mm_tn(hidden, dy_all).astype(BF16).reshape(lax.axis_size("h"), lax.axis_size("x"), -1, d_model)
    )
    d_resid = dy_own + r_two * (d_n_two - n_two * jnp.mean(d_n_two * n_two, -1, keepdims=True))

    db_all = stack(gather_tokens(d_resid.astype(BF16)))
    d_attn = reorder(mm_nt(db_all, w_out_mine).reshape(8, size, nv)).reshape(8, size, HP, DV)
    g_out = out_rows_out(mm_tn(mixed, db_all).astype(BF16))
    d_q, d_k, d_v = attention_back(d_attn)
    d_qkv = jnp.concatenate([t.reshape(8, size, -1) for t in (d_v, d_q, d_k)], -1)
    d_qkv = (reorder(d_qkv).reshape(8 * size, -1) * r_all).astype(BF16)
    d_x = scatter_tokens(unstack(mm_nt(d_qkv, w_qkv).astype(BF16)))
    g_qkv = columns_out(mm_tn(x_all, d_qkv).astype(BF16)).astype(F32)
    n_one = x_own * lax.rsqrt(jnp.mean(x_own * x_own, -1, keepdims=True) + EPS)
    input_grad = d_resid + d_x - n_one * jnp.mean(d_x * n_one, -1, keepdims=True)

    g_gu = g_gu.astype(F32)
    g_gate, g_up = join_hidden(g_gu[..., :ff]), join_hidden(g_gu[..., ff:])
    g_value = join_heads(g_qkv[..., :nv], DV)
    g_query = join_heads(g_qkv[..., nv : nv + nq], FD)
    g_key = join_heads(g_qkv[..., nv + nq :], FD)
    along = lambda w, g: jnp.sum(w.astype(F32) * g, -1)
    g_gain_one = along(w_query, g_query) + along(w_key, g_key) + along(w_value, g_value)
    g_gain_two = along(w_gate, g_gate) + along(w_up, g_up)
    return (
        block_out[None],
        input_grad[None],
        g_gain_one,
        gain_one * g_query,
        gain_one * g_key,
        gain_one * g_value,
        g_out,
        g_gain_two,
        gain_two * g_gate,
        gain_two * g_up,
        g_down,
    )


def solution(mesh):
    seq, fsdp = mesh.shape["seq"], mesh.shape["fsdp"]
    fine = Mesh(mesh.devices.reshape(seq // 8, 2, 2, 2, fsdp), ("h", "l", "y", "c", "x"))
    along = ("h", "l", "y", "c")
    token, vec, mat = P("x", along, None), P(along + ("x",)), P(along + ("x",), None)
    return jax.shard_map(
        on_device,
        mesh=fine,
        in_specs=(token, P("x", None), vec, mat, mat, mat, mat, vec, mat, mat, mat, token),
        out_specs=(token, token, vec, mat, mat, mat, mat, vec, mat, mat, mat),
        check_vma=False,
    )
```

```python
import functools

import jax
import jax.numpy as jnp
import numpy as np
from jax import lax
from jax.experimental import pallas as pl
from jax.experimental.pallas import tpu as pltpu
from jax.sharding import Mesh
from jax.sharding import PartitionSpec as P

H = 16
FD = 16
DV = 128
HP = 2
ROWS = DV + 2 * FD
WIDE = 384
QK = 2 * DV
LANE_R, LANE_ONE = 64, 65
FEAT = 256
SENT = 160
SEQS = 4
TP = ("l", "y", "c")
DP = ("h", "x")
EPS = 1e-5
F32, BF16 = jnp.float32, jnp.bfloat16


def dot(a, b, dims):
    return lax.dot_general(a, b, (dims, ((), ())), preferred_element_type=F32)


def mm(a, b):
    return dot(a, b, ((1,), (0,)))


def mm_nt(a, b):
    return dot(a, b, ((1,), (1,)))


def mm_tn(a, b):
    return dot(a, b, ((0,), (0,)))


def swap(a, axis):
    return lax.ppermute(a, axis, [(0, 1), (1, 0)])


class Order:
    def __init__(self, info):
        self.info = info

    def at(self, *values):
        flat, tree = jax.tree.flatten(values)
        got = lax.optimization_barrier((self.info, *flat))
        self.info = got[0]
        return jax.tree.unflatten(tree, got[1:])


SLOTS = ((0, 0, 256), (1, 0, 256), (2, 0, 256), (3, 0, 256), (4, 0, 256), (5, 0, 256))
SLOTS += ((6, 0, 128), (6, 128, 128), (7, 0, 128), (7, 128, 128))


def near_tokens(own):
    return [own, swap(own, "l"), swap(own, "y"), swap(own, "c")]


def far_tokens(near):
    own, from_l, from_y, _ = near
    half = own.shape[0] // 2
    return [swap(from_y[:half], "l"), swap(from_l[half:], "y"), swap(from_y, "c"), swap(from_l, "c")]


def last_tokens(far):
    return [swap(far[0], "c"), swap(far[1], "c")]


def in_slots(near, far, last):
    return [near[0], near[3], near[2], far[2], near[1], far[3], far[0], far[1], *last]


def far_cores(p):
    return [swap(p[8], "c"), swap(p[9], "c")]


def near_cores(p):
    return [swap(p[1], "c"), swap(p[3], "c"), swap(p[5], "c")]


def plus(*terms):
    return functools.reduce(jnp.add, [t.astype(F32) for t in terms]).astype(BF16)


def send_far(p, fars):
    return [swap(plus(p[6], fars[0]), "l"), swap(plus(p[7], fars[1]), "y")]


def send_first(p, nears):
    half = p[6].shape[0]
    return [swap(plus(p[2][half:], nears[1][half:]), "y"), swap(plus(p[4][:half], nears[2][:half]), "l")]


def send_second(p, nears, via):
    half = p[6].shape[0]
    y_a = plus(p[2][:half], nears[1][:half], via[0])
    l_b = plus(p[4][half:], nears[2][half:], via[1])
    return [swap(y_a, "y"), swap(l_b, "l")]


def terms(p, nears, first, second):
    return [p[0], nears[0], second[0], first[1], first[0], second[1]]


def flips(a):
    a = jnp.where(lax.axis_index("h") == 0, a, a[::-1])
    return jnp.where(lax.axis_index("x") == 0, a, a[:, ::-1])


def small_mesh():
    return lax.axis_size("h") == 2 and lax.axis_size("x") == 2


def over_both(a):
    if small_mesh():
        over_h = swap(a, "h")
        rel = [jnp.stack([a, swap(a, "x")]), jnp.stack([over_h, swap(over_h, "x")])]
        return flips(jnp.stack(rel))
    full = lax.all_gather(a, DP)
    return full.reshape((lax.axis_size("h"), lax.axis_size("x")) + a.shape)


def sum_both(parts):
    flat = parts.reshape((-1,) + parts.shape[2:])
    return lax.psum_scatter(flat, DP, scatter_dimension=0, tiled=False).astype(F32)


def cut(a, n):
    step = a.shape[0] // n
    return [a[i * step : (i + 1) * step] for i in range(n)]


def sub_head():
    return lax.axis_size(DP + TP) // H == 2 * lax.axis_size("x")


def split_heads(w, width):
    rows = w.shape[0]
    w = w.T
    if sub_head():
        w = w.reshape(2, HP, 2, 2, width, rows).transpose(2, 3, 0, 1, 4, 5)
    else:
        w = w.reshape(HP, 8, width, rows).transpose(1, 0, 2, 3)
    return w.reshape(8, HP, width, rows)


def join_heads(w, width):
    rows = w.shape[-1]
    if sub_head():
        w = w.reshape(2, 2, 2, HP, width, rows).transpose(2, 3, 0, 1, 4, 5)
    else:
        w = w.transpose(1, 0, 2, 3)
    return w.reshape(H * width, rows).T


def split_hidden(first, second):
    h, x = lax.axis_size("h"), lax.axis_size("x")
    w = jnp.concatenate([first, second], 0).T
    cols = w.shape[1]
    return w.reshape(h, 8, x, -1, cols).transpose(1, 0, 2, 3, 4).reshape(8, -1, cols)


def join_hidden(w):
    h, x = lax.axis_size("h"), lax.axis_size("x")
    cols = w.shape[-1]
    w = w.reshape(8, h, x, -1, cols).transpose(1, 0, 2, 3, 4).reshape(-1, cols).T
    return w[: cols // 2], w[cols // 2 :]


LAYOUT_HEADS = ((0, 0, 0, DV), (1, 0, DV, DV), (0, DV, QK, FD), (1, DV, QK + FD, FD))
LAYOUT_HEADS += ((0, DV + FD, QK + 2 * FD, FD), (1, DV + FD, QK + 3 * FD, FD))


def layout_hidden(n):
    return ((0, 0, 0, n), (1, 0, n, n))


def slabs_to_rows(full, layout, height):
    h, x, _, n, cols = full.shape
    pair = full.reshape(h, x, 8, n, 2, cols // 2).transpose(4, 3, 0, 2, 1, 5).reshape(2, n, -1)
    rows = [pair[m, src : src + count] for m, src, _, count in layout]
    have = sum(count for *_, count in layout)
    return jnp.concatenate(rows + [jnp.zeros((height - have, pair.shape[2]), BF16)], 0)


def unpack(info, chunks, layout, height):
    k = len(chunks[0])
    args = [c for piece in chunks for c in piece]
    return call(functools.partial(unpack_kernel, layout, k), [info, *args], [((height, 16 * 128), BF16)], vmem=20)[0]


def rows_to_slabs(rows, layout):
    h, x = lax.axis_size("h"), lax.axis_size("x")
    pair = [jnp.concatenate([rows[dst : dst + c] for m, _, dst, c in layout if m == k], 0) for k in (0, 1)]
    n = pair[0].shape[0]
    parts = jnp.stack(pair).reshape(2, n, h, 8, x, -1).transpose(2, 4, 3, 1, 0, 5)
    return parts.reshape(h, x, 8, n, -1)


def exchange(slabs):
    return lax.all_to_all(slabs, TP, 0, 0, tiled=True)


def out_rows_in(full):
    if sub_head():
        h, x, rows, d = full.shape
        full = lax.all_to_all(full.reshape(2, h // 2, x, rows, d), "c", 0, 0, tiled=True)
        full = full.transpose(1, 0, 2, 3, 4)
    return full.reshape(HP * DV, -1)


def out_rows_out(grad):
    h, x = lax.axis_size("h"), lax.axis_size("x")
    d = grad.shape[1]
    if sub_head():
        grad = grad.reshape(HP, 2, x, -1, d).transpose(1, 0, 2, 3, 4)
        grad = lax.all_to_all(grad, "c", 0, 0, tiled=True)
    return grad.reshape(h, x, -1, d)


def entering(total, reverse):
    n = lax.axis_size("h")
    got = jnp.zeros_like(total)
    for s in range(1, n):
        route = [(i + s, i) if reverse else (i, i + s) for i in range(n - s)]
        came = lax.ppermute(total, "h", route)
        got = came if s == 1 else (got.astype(F32) + came.astype(F32)).astype(BF16)
    return got


def feature_maps():
    maps = np.zeros((4, 2, 128, FEAT), np.float32)
    for kind in range(4):
        where = [kind * FD + i for i in range(FD)] + [LANE_ONE]
        size = [0.5] * FD + [1.0]
        col = 0
        for i in range(FD + 1):
            for j in range(i, FD + 1):
                maps[kind, 0, where[i], col] = size[i]
                maps[kind, 1, where[j], col] = size[j] * (0.5 if kind >= 2 and i == j < FD else 1.0)
                col += 1
    return maps


MAPS = feature_maps()


def lanes(shape):
    return lax.broadcasted_iota(jnp.int32, shape, len(shape) - 1)


def segments(info, places):
    end, found = 0, jnp.zeros(places.shape, jnp.int32)
    for i in range(SEQS):
        end = end + info[2 + i]
        found = found + (places >= end).astype(jnp.int32)
    return found


def long_bounds(info):
    start, end, best, total = 0, info[2], info[2], info[2]
    for i in range(1, SEQS):
        more = info[2 + i] > best
        start = jnp.where(more, total, start)
        total = total + info[2 + i]
        end = jnp.where(more, total, end)
        best = jnp.where(more, info[2 + i], best)
    return start, end


def crossing(info, base):
    start, end = long_bounds(info)
    places = base + lax.broadcasted_iota(jnp.int32, (256, 1), 0)
    return ((places >= start) & (places < end)).astype(F32)


def pair_mask(info, base):
    row = lax.broadcasted_iota(jnp.int32, (256, 256), 0)
    col = lax.broadcasted_iota(jnp.int32, (256, 256), 1)
    down = segments(info, base + lax.broadcasted_iota(jnp.int32, (256, 1), 0))
    across = segments(info, base + lax.broadcasted_iota(jnp.int32, (1, 256), 1))
    return ((down == across) & (row >= col)).astype(F32)


def maps_of(tile, maps, kind):
    return mm(tile, maps[kind, 0]), mm(tile, maps[kind, 1])


def feats_t(tile, maps_t, kind):
    return (mm_nt(maps_t[kind, 0], tile) * mm_nt(maps_t[kind, 1], tile)).astype(BF16)


def feats(tile, maps, kind):
    a, b = maps_of(tile, maps, kind)
    return (a * b).astype(BF16)


def with_ones(values):
    one = (lanes((256, 128)) == 0).astype(BF16)
    return jnp.concatenate([values, one], 1)


def head_mask(h):
    at = lanes((256, 128))
    return ((at >= h * FD) & (at < (h + 1) * FD)).astype(F32)


def keys_on_queries(tile):
    return pltpu.roll(tile, 128 - HP * FD, 1)


def load(refs, r):
    if r < 6:
        return refs[r][...]
    return jnp.concatenate([refs[2 * r - 6][...], refs[2 * r - 5][...]], 0)


def store(refs, r, value):
    if r < 6:
        refs[r][...] = value
    else:
        refs[2 * r - 6][...] = value[:128]
        refs[2 * r - 5][...] = value[128:]


def project_kernel(info, *refs):
    xs, (w, maps_t, tile_ref, val_ref, state_ref, sums) = refs[:10], refs[10:]
    me, first = info[0], info[1]
    sums[...] = jnp.zeros_like(sums)
    at = lanes((256, 128))
    for r in range(8):
        p = jnp.bitwise_xor(me, r)
        x = load(xs, r)
        wide = x.astype(F32)
        scale = lax.rsqrt(jnp.mean(wide * wide, 1, keepdims=True) + EPS)
        y = mm_nt(x, w[...]) * scale
        values = y[:, :QK].astype(BF16)
        tile = jnp.where(at == LANE_R, scale, jnp.where(at == LANE_ONE, 1.0, y[:, QK:]))
        tile_ref[p] = tile
        val_ref[p] = values
        cross = crossing(info, first + p * 256).astype(BF16)
        low = tile.astype(BF16)
        for h in range(HP):
            feat = feats_t(low, maps_t, 2 + h)
            sums[h] += mm(feat, with_ones(values[:, h * DV : (h + 1) * DV]) * cross)
    state_ref[...] = sums[:, :SENT].astype(BF16)


def attend_kernel(info, tile_ref, val_ref, enter, maps, maps_t, w, *refs):
    mixed_ref, den_ref, before_ref = refs[:3]
    outs, sums = refs[3:13], refs[13]
    me, first = info[0], info[1]
    sums[...] = jnp.zeros_like(sums)
    sums[:, :SENT] = enter[...].astype(F32)

    def step(p, carry):
        tile = tile_ref[p]
        low = tile.astype(BF16)
        keys = keys_on_queries(tile).astype(BF16)
        cross = crossing(info, first + p * 256)
        cross_low = cross.astype(BF16)
        mask = pair_mask(info, first + p * 256)
        den = jnp.zeros((256, 128), F32)
        for h in range(HP):
            flat = mm_nt((tile * (head_mask(h) * 0.25)).astype(BF16), keys)
            low_scores = ((1.0 + flat + 0.5 * flat * flat) * mask).astype(BF16)
            values = with_ones(val_ref[p, :, h * DV : (h + 1) * DV])
            state = sums[h].astype(BF16)
            before_ref[p, h] = state
            both = mm(low_scores, values) + cross * mm(feats(low, maps, h), state)
            here = both[:, DV : DV + 1]
            mixed_ref[p, :, h * DV : (h + 1) * DV] = (both[:, :DV] / here).astype(BF16)
            den = jnp.where(lanes((256, 128)) == h, here, den)
            sums[h] += mm(feats_t(low, maps_t, 2 + h), values * cross_low)
        den_ref[p] = den
        return carry

    lax.fori_loop(0, 8, step, 0, unroll=True)
    for r in range(8):
        store(outs, r, mm(mixed_ref[jnp.bitwise_xor(me, r)], w[...]).astype(BF16))


def back_state_kernel(info, *refs):
    dbs = refs[:10]
    w, mixed_ref, den_ref, tile_ref, maps_t, d_num_ref, d_den_ref, state_ref, sums = refs[10:]
    me, first = info[0], info[1]
    sums[...] = jnp.zeros_like(sums)
    at = lanes((256, 128))
    for r in range(8):
        p = jnp.bitwise_xor(me, r)
        d_attn = mm_nt(load(dbs, r), w[...])
        low = tile_ref[p].astype(BF16)
        cross = crossing(info, first + p * 256).astype(BF16)
        den = den_ref[p]
        d_den = jnp.zeros((256, 128), F32)
        for h in range(HP):
            cols = slice(h * DV, (h + 1) * DV)
            inv = 1.0 / den[:, h : h + 1]
            d_num = (d_attn[:, cols] * inv).astype(BF16)
            d_num_ref[p, :, cols] = d_num
            total = -jnp.sum(d_attn[:, cols] * mixed_ref[p, :, cols].astype(F32), 1, keepdims=True) * inv
            d_den = jnp.where(at == h, total, d_den)
            grad = jnp.concatenate([d_num, jnp.where(at == 0, total, 0.0).astype(BF16)], 1)
            sums[h] += mm(feats_t(low, maps_t, h), grad * cross)
        d_den_ref[p] = d_den
    state_ref[...] = sums[:, :SENT].astype(BF16)


def back_kernel(info, tile_ref, val_ref, d_num_ref, d_den_ref, before_ref, enter, maps, w, *refs):
    e_ref, outs, sums = refs[0], refs[1:11], refs[11]
    me, first = info[0], info[1]
    sums[...] = jnp.zeros_like(sums)
    sums[:, :SENT] = enter[...].astype(F32)
    at = lanes((256, 128))

    def through(d_feat, a, b, kind):
        return mm_nt((d_feat * b).astype(BF16), maps[kind, 0]) + mm_nt((d_feat * a).astype(BF16), maps[kind, 1])

    def step(i, carry):
        p = 7 - i
        tile = tile_ref[p]
        low = tile.astype(BF16)
        keys = keys_on_queries(tile)
        keys_low = keys.astype(BF16)
        cross = crossing(info, first + p * 256)
        cross_low = cross.astype(BF16)
        mask = pair_mask(info, first + p * 256)
        d_tile = jnp.zeros((256, 128), F32)
        d_keys = jnp.zeros((256, 128), F32)
        scale = tile[:, LANE_R : LANE_R + 1]
        for h in range(HP):
            cols = slice(h * DV, (h + 1) * DV)
            here = head_mask(h)
            flat = mm_nt((tile * (here * 0.25)).astype(BF16), keys_low)
            low_scores = ((1.0 + flat + 0.5 * flat * flat) * mask).astype(BF16)
            values = val_ref[p, :, cols]
            d_num = d_num_ref[p, :, cols]
            d_den = d_den_ref[p][:, h : h + 1]
            back = sums[h].astype(BF16)
            d_flat = ((mm_nt(d_num, values) + d_den) * mask * (0.25 + 0.25 * flat)).astype(BF16)
            qa, qb = maps_of(low, maps, h)
            ka, kb = maps_of(low, maps, 2 + h)
            grad = jnp.concatenate([d_num, jnp.where(at == 0, d_den, 0.0).astype(BF16)], 1)
            d_feat_q = mm_nt(grad, before_ref[p, h]) * cross
            d_feat_k = mm_nt(with_ones(values), back) * cross
            d_tile += mm(d_flat, (keys * here).astype(BF16)) + through(d_feat_q, qa, qb, h)
            d_tile += through(d_feat_k, ka, kb, 2 + h)
            d_keys += mm_tn(d_flat, (tile * here).astype(BF16))
            d_val = mm_tn(low_scores, d_num) + cross * mm((ka * kb).astype(BF16), back[:, :DV])
            e_ref[p, :, cols] = (d_val * scale).astype(BF16)
            sums[h] += mm_tn((qa * qb).astype(BF16), grad * cross_low)
        d_tile = jnp.where(at < 2 * HP * FD, d_tile + pltpu.roll(d_keys, HP * FD, 1), 0.0)
        e_ref[p, :, QK:] = (d_tile * scale).astype(BF16)
        return carry

    lax.fori_loop(0, 8, step, 0)
    for r in range(8):
        store(outs, r, mm(e_ref[jnp.bitwise_xor(me, r)], w[...]).astype(BF16))


def unpack_kernel(layout, k, info, *refs):
    pieces, out = [refs[i * k : (i + 1) * k] for i in range(4)], refs[4 * k]
    have = sum(count for *_, count in layout)
    if have < out.shape[0]:
        out[have:] = jnp.zeros((out.shape[0] - have, out.shape[1]), BF16)
    even = info[7] == 0
    each = 8 // k
    for dh in range(2):
        for s in range(8):
            near, far = pieces[dh][s // each][s % each], pieces[2 + dh][s // each][s % each]
            first, second = lax.select(even, near, far), lax.select(even, far, near)
            pair = [jnp.concatenate([first[:, c : c + 64], second[:, c : c + 64]], 1) for c in (0, 64)]
            at = pl.multiple_of((jnp.bitwise_xor(info[6], dh) * 8 + s) * 128, 128)
            for m, src, dst, count in layout:
                out[dst : dst + count, pl.ds(at, 128)] = pair[m][src : src + count]


def rows_kernel(k, info, *refs):
    pieces, out = [refs[i * k : (i + 1) * k] for i in range(4)], refs[4 * k]
    block = sum(c.shape[0] for c in pieces[0])
    even = info[7] == 0
    for dh in range(2):
        start = 0
        for c in range(k):
            near, far = pieces[dh][c][...], pieces[2 + dh][c][...]
            for x, value in enumerate((lax.select(even, near, far), lax.select(even, far, near))):
                at = (jnp.bitwise_xor(info[6], dh) * 2 + x) * block + start
                out[pl.ds(pl.multiple_of(at, 16), near.shape[0])] = value
            start += near.shape[0]


def total_kernel(groups, *refs):
    total, at = 0.0, 0
    for k in groups:
        term = [refs[at + c][...].astype(F32) for c in range(k)]
        total = total + (term[0] if k == 1 else jnp.concatenate(term, 0))
        at += k
    refs[-1][...] = total.astype(refs[-1].dtype)


def summed(pieces):
    total = pieces[0][...].astype(F32) + pieces[1][...].astype(F32)
    upper = pieces[2][...].astype(F32) + pieces[3][...].astype(F32)
    lower = pieces[4][...].astype(F32) + pieces[5][...].astype(F32)
    return total + jnp.concatenate([upper, lower], 0)


def scale_of(v):
    return lax.rsqrt(jnp.mean(v * v, 1, keepdims=True) + EPS)


def residual_kernel(x, *refs):
    resid = x[...].astype(F32) + summed(refs[:6])
    refs[6][...] = resid
    refs[7][...] = (resid * scale_of(resid)).astype(BF16)


def d_residual_kernel(dy, resid_ref, *refs):
    resid, d_n = resid_ref[...], summed(refs[:6])
    r = scale_of(resid)
    n = resid * r
    d = dy[...].astype(F32) + r * (d_n - n * jnp.mean(d_n * n, 1, keepdims=True))
    refs[6][...] = d
    refs[7][...] = d.astype(BF16)


def input_kernel(x_ref, d_resid, *refs):
    x, d_x = x_ref[...].astype(F32), summed(refs[:6])
    n = x * scale_of(x)
    refs[6][0] = d_resid[...] + d_x - n * jnp.mean(d_x * n, 1, keepdims=True)


def output_kernel(resid, *refs):
    refs[6][0] = resid[...] + summed(refs[:6])


def sort_by_x(info, zero, one):
    even = info[7] == 0
    return lax.select(even, zero, one), lax.select(even, one, zero)


def pack_tile(info, first, second):
    zero = jnp.concatenate([first[:, :64], second[:, :64]], 1)
    one = jnp.concatenate([first[:, 64:], second[:, 64:]], 1)
    return sort_by_x(info, zero, one)


def qkv_grads_kernel(info, *refs):
    xs, (e_ref, total) = refs[:10], (refs[10], refs[-1])
    me = info[0]
    for r in range(8):
        more = mm_tn(e_ref[jnp.bitwise_xor(me, r)], load(xs, r))
        total[...] = more if r == 0 else total[...] + more
    if len(refs) == 13:
        refs[11][...] = total[...].astype(BF16)
        return
    outs = refs[11:15]
    for dh in range(2):
        for s in range(8):
            at = pl.multiple_of((jnp.bitwise_xor(info[6], dh) * 8 + s) * 128, 128)
            tile = total[:, pl.ds(at, 128)].astype(BF16)
            pair = [
                jnp.concatenate([tile[dst : dst + c] for m, _, dst, c in LAYOUT_HEADS if m == k], 0) for k in (0, 1)
            ]
            outs[dh][s], outs[2 + dh][s] = pack_tile(info, *pair)


def out_grads_kernel(info, *refs):
    dbs, (mixed_ref, total) = refs[:10], (refs[10], refs[-1])
    me = info[0]
    for r in range(8):
        more = mm_tn(mixed_ref[jnp.bitwise_xor(me, r)], load(dbs, r))
        total[...] = more if r == 0 else total[...] + more
    if len(refs) == 13:
        refs[11][...] = total[...].astype(BF16)
        return
    outs = refs[11:15]
    for dh in range(2):
        at = pl.multiple_of(jnp.bitwise_xor(info[6], dh) * DV, DV)
        rows = total[pl.ds(at, DV), :].astype(BF16)
        outs[dh][...], outs[2 + dh][...] = sort_by_x(info, rows[:64], rows[64:])


def mlp_kernel(pieces, *refs):
    ns, dys, (w_gu, wd) = refs[:pieces], refs[pieces : 2 * pieces], refs[2 * pieces : 2 * pieces + 2]
    outs, dns = refs[2 * pieces + 2 : 3 * pieces + 2], refs[3 * pieces + 2 : 4 * pieces + 2]
    hid_ref, dg_ref, du_ref = refs[4 * pieces + 2 :]
    ff = wd.shape[0]
    at = 0
    for i in range(pieces):
        rows = ns[i].shape[0]
        n, dy = ns[i][...], dys[i][...]
        gate, up, d_hid = mm_nt(n, w_gu[:ff]), mm_nt(n, w_gu[ff:]), mm_nt(dy, wd[...])
        sig = 1.0 / (1.0 + jnp.exp(-gate))
        silu = gate * sig
        hid = (silu * up).astype(BF16)
        dg = (d_hid * up * sig * (1.0 + gate * (1.0 - sig))).astype(BF16)
        du = (d_hid * silu).astype(BF16)
        hid_ref[at : at + rows] = hid
        dg_ref[at : at + rows] = dg
        du_ref[at : at + rows] = du
        outs[i][...] = mm(hid, wd[...]).astype(BF16)
        dns[i][...] = (mm(dg, w_gu[:ff]) + mm(du, w_gu[ff:])).astype(BF16)
        at += rows


QUARTERS = ((0, 1), (2, 3), (4, 5), (6, 7, 8, 9))


def over_tokens(lefts, rights, scratch):
    @pl.when(pl.program_id(0) == 0)
    def _():
        for q in range(4):
            scratch[:, q * 512 : (q + 1) * 512] = lefts[q][...].T

    total = 0.0
    for q, at in enumerate(QUARTERS):
        total += mm(scratch[:, q * 512 : (q + 1) * 512], jnp.concatenate([rights[i][...] for i in at], 0))
    return total.astype(BF16)


def hidden_grads_kernel(info, *refs):
    ns, dgs, dus, (near, far, dg_t, du_t) = refs[:10], refs[10:14], refs[14:18], refs[18:]
    gate, up = over_tokens(dgs, ns, dg_t), over_tokens(dus, ns, du_t)
    for s in range(gate.shape[1] // 128):
        cols = slice(s * 128, (s + 1) * 128)
        near[s], far[s] = pack_tile(info, gate[:, cols], up[:, cols])


def down_grads_kernel(info, *refs):
    dys, hids, outs = refs[:10], refs[10:14], refs[14:18]
    grad = over_tokens(hids, dys, refs[18])
    rows = grad.shape[0] // 4
    cut = lambda i: grad[i * rows : (i + 1) * rows]
    even = info[6] == 0
    for k, (zero, one) in enumerate(((cut(0), cut(1)), (cut(2), cut(3)))):
        stays, goes = sort_by_x(info, zero, one)
        if k == 0:
            first = stays, goes
    for i in range(2):
        outs[2 * i][...] = lax.select(even, first[i], (stays, goes)[i])
        outs[2 * i + 1][...] = lax.select(even, (stays, goes)[i], first[i])


def plain_grads_kernel(info, *refs):
    rights, lefts, (out, left_t) = refs[:10], refs[10:14], refs[14:]
    out[...] = over_tokens(lefts, rights, left_t)


SMEM = pl.BlockSpec(memory_space=pltpu.SMEM)
VMEM = pl.BlockSpec(memory_space=pltpu.VMEM)


def call(kernel, args, outs, scratch=(), flops=0, vmem=24, grid=None):
    shapes = tuple(jax.ShapeDtypeStruct(s, t) for s, t in outs)
    moved = sum(a.size * a.dtype.itemsize for a in args) + sum(s.size * s.dtype.itemsize for s in shapes)
    if grid is None:
        grid = {
            "in_specs": [SMEM if a.dtype == jnp.int32 else VMEM for a in args],
            "out_specs": [VMEM] * len(outs),
            "scratch_shapes": list(scratch),
        }
    return pl.pallas_call(
        kernel,
        out_shape=shapes,
        compiler_params=pltpu.CompilerParams(vmem_limit_bytes=vmem << 20),
        cost_estimate=pl.CostEstimate(flops=flops, bytes_accessed=moved, transcendentals=0),
        **grid,
    )(*args)


STATE = pltpu.VMEM((HP, FEAT, 2 * DV), F32)
TOKENS = [((n, 2048), BF16) for _, _, n in SLOTS]


QUARTER_SLICES = (slice(0, 2), slice(2, 4), slice(4, 6), slice(6, 10))


def mlp(ns, dys, w_gu, wd):
    ff, d = wd.shape
    k = len(ns)
    blocks = [((n.shape[0], d), BF16) for n in ns]
    rows = sum(n.shape[0] for n in ns)
    got = call(
        functools.partial(mlp_kernel, k),
        [*ns, *dys, w_gu, wd],
        blocks + blocks + [((rows, ff), BF16)] * 3,
        flops=12 * rows * ff * d,
    )
    return got[:k], got[k : 2 * k], got[2 * k :]


CUT = 256


def tall(n, at=lambda i, info: i):
    return pl.BlockSpec((n, CUT), lambda i, info: (0, at(i, info)))


def whole(a):
    return pl.BlockSpec(a.shape, lambda i, info: (0, 0))


def scalar_grid(steps, in_specs, out_specs, scratch):
    return {
        "grid_spec": pltpu.PrefetchScalarGridSpec(
            num_scalar_prefetch=1, grid=(steps,), in_specs=in_specs, out_specs=out_specs, scratch_shapes=scratch
        )
    }


def turned(ff):
    return pltpu.VMEM((ff, 2048), BF16)


def plain_grads(info, rights, lefts):
    ff, d = lefts[0].shape[1], rights[0].shape[1]
    grid = scalar_grid(d // CUT, [tall(a.shape[0]) for a in rights] + [whole(a) for a in lefts], [tall(ff)], [turned(ff)])
    return call(plain_grads_kernel, [info, *rights, *lefts], [((ff, d), BF16)], grid=grid)[0]


def hidden_grads(info, ns, dgs, dus, dh):
    ff, d = dgs[0].shape[1], ns[0].shape[1]
    steps = d // 2 // CUT
    cols = lambda i, info: jnp.bitwise_xor(info[6], dh) * steps + i
    slab = pl.BlockSpec((CUT // 128, ff, 128), lambda i, info: (i, 0, 0))
    grid = scalar_grid(steps, [tall(a.shape[0], cols) for a in ns] + [whole(a) for a in [*dgs, *dus]], [slab] * 2, [turned(ff)] * 2)
    return call(
        hidden_grads_kernel,
        [info, *ns, *dgs, *dus],
        [((8, ff, 128), BF16)] * 2,
        flops=2 * 2048 * ff * d,
        grid=grid,
        vmem=36,
    )


def down_grads(info, dys, hids):
    ff, d = hids[0].shape[1], dys[0].shape[1]
    out = tall(ff // 4)
    grid = scalar_grid(d // CUT, [tall(a.shape[0]) for a in dys] + [whole(a) for a in hids], [out] * 4, [turned(ff)])
    shapes = [((ff // 4, d), BF16)] * 4
    return call(down_grads_kernel, [info, *dys, *hids], shapes, flops=2 * 2048 * ff * d, grid=grid)


def gained(gain, w):
    return (gain * w.astype(F32)).astype(BF16)


def head_slabs(gain, w_query, w_key, w_value):
    split = [split_heads(gained(gain, w), n) for w, n in ((w_value, DV), (w_query, FD), (w_key, FD))]
    return jnp.concatenate(split, 2).transpose(0, 2, 1, 3).reshape(8, ROWS, -1)


def project(info, xs, w_qkv, maps_t):
    size, d = 256, w_qkv.shape[1]
    return call(
        project_kernel,
        [info, *xs, w_qkv, maps_t],
        [((8, size, 128), F32), ((8, size, QK), BF16), ((HP, SENT, 2 * DV), BF16)],
        [STATE],
        flops=2 * 8 * size * d * WIDE,
    )


def attend(info, tile, values, enter, maps, maps_t, w_out):
    size, d = 256, w_out.shape[1]
    got = call(
        attend_kernel,
        [info, tile, values, enter, maps, maps_t, w_out],
        [((8, size, QK), BF16), ((8, size, 128), F32), ((8, HP, FEAT, 2 * DV), BF16)] + TOKENS,
        [STATE],
        flops=2 * 8 * size * d * QK,
    )
    return got[:3], got[3:]


def back_state(info, dbs, w_out, mixed, den, tile, maps_t):
    size, d = 256, w_out.shape[1]
    return call(
        back_state_kernel,
        [info, *dbs, w_out, mixed, den, tile, maps_t],
        [((8, size, QK), BF16), ((8, size, 128), F32), ((HP, SENT, 2 * DV), BF16)],
        [STATE],
        flops=2 * 8 * size * d * QK,
    )


def back(info, tile, values, d_num, d_den, before, later, maps, w_qkv):
    size, d = 256, w_qkv.shape[1]
    got = call(
        back_kernel,
        [info, tile, values, d_num, d_den, before, later, maps, w_qkv],
        [((8, size, WIDE), BF16)] + TOKENS,
        [STATE],
        flops=2 * 8 * size * d * WIDE,
        vmem=28,
    )
    return got[0], got[1:]


def qkv_grads(info, xs, e, packed):
    d = xs[0].shape[1]
    outs = [((8, ROWS, 128), BF16)] * 4 if packed else [((WIDE, d), BF16)]
    return call(qkv_grads_kernel, [info, *xs, e], outs, [pltpu.VMEM((WIDE, d), F32)], flops=2 * 2048 * d * WIDE)


def out_grads(info, dbs, mixed, packed):
    d = dbs[0].shape[1]
    outs = [((QK // 4, d), BF16)] * 4 if packed else [((QK, d), BF16)]
    return call(out_grads_kernel, [info, *dbs, mixed], outs, [pltpu.VMEM((QK, d), F32)], flops=2 * 2048 * d * QK)


def total(groups, shape, dtype):
    args = [c for g in groups for c in g]
    return call(functools.partial(total_kernel, [len(g) for g in groups]), args, [(shape, dtype)])[0]


def finish_residual(x, pieces):
    return call(residual_kernel, [x, *pieces], [(x.shape, F32), (x.shape, BF16)])


def finish_d_residual(dy, resid, pieces):
    return call(d_residual_kernel, [dy, resid, *pieces], [(dy.shape, F32), (dy.shape, BF16)])


def finish_input(x, d_resid, pieces):
    return call(input_kernel, [x, d_resid, *pieces], [((1,) + x.shape, F32)])[0]


def finish_output(resid, pieces):
    return call(output_kernel, [resid, *pieces], [((1,) + resid.shape, F32)])[0]


def gather_all(own):
    near = near_tokens(own)
    far = far_tokens(near)
    return in_slots(near, far, last_tokens(far))


def scatter_all(p):
    nears = near_cores(p)
    via = send_far(p, far_cores(p))
    return terms(p, nears, send_first(p, nears), send_second(p, nears, via))


def weight_grads(weights, gains, g_heads, g_hid):
    w_query, w_key, w_value, w_gate, w_up = weights
    g_gate, g_up = join_hidden(g_hid.astype(F32))
    g_heads = g_heads.astype(F32).reshape(8, ROWS, HP, -1).transpose(0, 2, 1, 3)
    g_value = join_heads(g_heads[:, :, :DV], DV)
    g_query = join_heads(g_heads[:, :, DV : DV + FD], FD)
    g_key = join_heads(g_heads[:, :, DV + FD :], FD)
    along = lambda w, g: jnp.sum(w.astype(F32) * g, -1)
    g_one = along(w_query, g_query) + along(w_key, g_key) + along(w_value, g_value)
    g_two = along(w_gate, g_gate) + along(w_up, g_up)
    return g_one, gains[0] * g_query, gains[0] * g_key, gains[0] * g_value, g_two, gains[1] * g_gate, gains[1] * g_up


def on_device(
    tokens, seq_lengths, norm_gain, w_query, w_key, w_value, w_out, mlp_gain, w_gate, w_up, w_down, cotangent
):
    x, dy = tokens[0], cotangent[0]
    gains = [g.astype(F32)[:, None] for g in (norm_gain, mlp_gain)]
    h, along_x = lax.axis_index("h"), lax.axis_index("x")
    place = jnp.stack([lax.axis_index(TP), h * 8 * x.shape[0]])
    info = jnp.concatenate([place, seq_lengths[0], jnp.stack([h, along_x])]).astype(jnp.int32)
    maps, maps_t = jnp.asarray(MAPS, BF16), jnp.asarray(MAPS.transpose(0, 1, 3, 2), BF16)
    small = small_mesh() and w_query.shape[0] == 64
    run = scheduled if small else plain
    block_out, input_grad, g_heads, g_out, g_hid, g_down = run(
        info, x, dy, gains, w_query, w_key, w_value, w_out, w_gate, w_up, w_down, maps, maps_t
    )
    g = weight_grads((w_query, w_key, w_value, w_gate, w_up), gains, g_heads, g_hid)
    return block_out, input_grad, *g[:4], g_out, *g[4:], g_down


def plain(info, x, dy, gains, w_query, w_key, w_value, w_out, w_gate, w_up, w_down, maps, maps_t):
    heads = over_both(exchange(head_slabs(gains[0], w_query, w_key, w_value)))
    w_qkv = slabs_to_rows(heads, LAYOUT_HEADS, WIDE)
    w_out_mine = out_rows_in(over_both(w_out))
    hid = over_both(exchange(split_hidden(gained(gains[1], w_gate), gained(gains[1], w_up))))
    wd = over_both(w_down).reshape(-1, x.shape[1])
    ff = wd.shape[0]
    w_gu = slabs_to_rows(hid, layout_hidden(ff), 2 * ff)
    xs = gather_all(x)
    tile, values, state = project(info, xs, w_qkv, maps_t)
    (mixed, den, before), p = attend(info, tile, values, entering(state, False), maps, maps_t, w_out_mine)
    resid, n_low = finish_residual(x, scatter_all(p))
    ns, dys = gather_all(n_low), gather_all(dy)
    ran = [mlp(ns[c], dys[c], w_gu, wd) for c in QUARTER_SLICES]
    hids, dgs, dus = [[r[2][i] for r in ran] for i in range(3)]
    block_out = finish_output(resid, scatter_all([b for r in ran for b in r[0]]))
    d_resid, d_low = finish_d_residual(dy, resid, scatter_all([b for r in ran for b in r[1]]))
    grads = jnp.concatenate([plain_grads(info, ns, dgs), plain_grads(info, ns, dus)], 0)
    g_hid = exchange(sum_both(rows_to_slabs(grads, layout_hidden(ff))).astype(BF16))
    g_down = sum_both(plain_grads(info, dys, hids).reshape(*hid.shape[:2], -1, x.shape[1]))
    dbs = gather_all(d_low)
    d_num, d_den, use = back_state(info, dbs, w_out_mine, mixed, den, tile, maps_t)
    e, p = back(info, tile, values, d_num, d_den, before, entering(use, True), maps, w_qkv)
    input_grad = finish_input(x, d_resid, scatter_all(p))
    g_out = sum_both(out_rows_out(out_grads(info, dbs, mixed, False)[0]))
    g_heads = exchange(sum_both(rows_to_slabs(qkv_grads(info, xs, e, False)[0], LAYOUT_HEADS)).astype(BF16))
    return block_out, input_grad, g_heads, g_out, g_hid, g_down


def scheduled(info, x, dy, gains, w_query, w_key, w_value, w_out, w_gate, w_up, w_down, maps, maps_t):
    d_model = x.shape[1]
    o = Order(info)

    near = near_tokens(x)
    out_h = swap(w_out, "h")
    heads = exchange(head_slabs(gains[0], w_query, w_key, w_value))
    heads, out_h = o.at(heads, out_h)
    hid = split_hidden(gained(gains[1], w_gate), gained(gains[1], w_up))
    heads_h, heads_x = swap(heads, "h"), swap(heads, "x")
    near, heads_h, heads_x, hid = o.at(near, heads_h, heads_x, hid)
    far = far_tokens(near)
    heads_hx = swap(heads_h, "x")
    d0, d1 = w_down[:96], w_down[96:]
    d0_h = swap(d0, "h")
    far, heads_hx, d0_h, hid = o.at(far, heads_hx, d0_h, hid)
    last = last_tokens(far)
    w_qkv = unpack(o.info, [[heads], [heads_h], [heads_x], [heads_hx]], LAYOUT_HEADS, WIDE)
    out_x, out_hx = swap(w_out, "x"), swap(out_h, "x")
    last, w_qkv, out_x, out_hx = o.at(last, w_qkv, out_x, out_hx)
    xs = in_slots(near, far, last)

    hid = exchange(hid)
    d1_h = swap(d1, "h")
    tile, values, state = project(o.info, xs, w_qkv, maps_t)
    tile, values, state, hid, d1_h = o.at(tile, values, state, hid, d1_h)
    enter = entering(state, False)
    d0_x, d1_x = swap(d0, "x"), swap(d1, "x")
    w_out_mine = call(
        functools.partial(rows_kernel, 1), [o.info, w_out, out_h, out_x, out_hx], [((QK, d_model), BF16)]
    )[0]
    enter, d0_x, d1_x, w_out_mine = o.at(enter, d0_x, d1_x, w_out_mine)
    dy_near = near_tokens(dy)
    u = cut(hid, 4)
    u_h, u_x, u_hx = [None] * 4, [None] * 4, [None] * 4
    u_h[0] = swap(u[0], "h")
    d0_hx, d1_hx = swap(d0_h, "x"), swap(d1_h, "x")
    (mixed, den, before), p = attend(o.info, tile, values, enter, maps, maps_t, w_out_mine)
    p, mixed, den, before, u_h[0], d0_hx, d1_hx = o.at(p, mixed, den, before, u_h[0], d0_hx, d1_hx)
    fars = far_cores(p)
    u_x[0] = swap(u[0], "x")
    fars, dy_near, u_x[0] = o.at(fars, dy_near, u_x[0])
    via = send_far(p, fars)
    nears = near_cores(p)
    u_h[1], u_x[1], u_hx[0] = swap(u[1], "h"), swap(u[1], "x"), swap(u_h[0], "x")
    via, nears, u_h[1], u_x[1], u_hx[0] = o.at(via, nears, u_h[1], u_x[1], u_hx[0])
    first = send_first(p, nears)
    u_h[2], u_x[2], u_hx[1] = swap(u[2], "h"), swap(u[2], "x"), swap(u_h[1], "x")
    first, u_h[2], u_x[2], u_hx[1] = o.at(first, u_h[2], u_x[2], u_hx[1])
    second = send_second(p, nears, via)
    u_h[3], u_x[3], u_hx[2] = swap(u[3], "h"), swap(u[3], "x"), swap(u_h[2], "x")
    wd = call(
        functools.partial(rows_kernel, 2),
        [o.info, d0, d1, d0_h, d1_h, d0_x, d1_x, d0_hx, d1_hx],
        [((4 * w_down.shape[0], d_model), BF16)],
    )[0]
    ff = wd.shape[0]
    second, u_h[3], u_x[3], u_hx[2], wd = o.at(second, u_h[3], u_x[3], u_hx[2], wd)
    resid, n_low = finish_residual(x, terms(p, nears, first, second))
    resid, n_low = o.at(resid, n_low)

    near = near_tokens(n_low)
    u_hx[3] = swap(u_h[3], "x")
    w_gu = unpack(o.info, [u, u_h, u_x, u_hx], layout_hidden(ff), 2 * ff)
    near, w_gu = o.at(near, w_gu)
    far = far_tokens(near)
    quarter = lambda i, ns, dys: mlp(ns[QUARTER_SLICES[i]], dys[QUARTER_SLICES[i]], w_gu, wd)
    ns, dys = in_slots(near, far, [None] * 2), in_slots(dy_near, [None] * 4, [None] * 2)
    ran = [quarter(0, ns, dys)]
    far, ran = o.at(far, ran)
    last = last_tokens(far)
    dy_far = far_tokens(dy_near)
    ns, dys = in_slots(near, far, last), in_slots(dy_near, dy_far, [None] * 2)
    dy_ready = dy_far[2:]
    last, dy_ready = o.at(last, dy_ready)
    dy_far = dy_far[:2] + dy_ready
    ns, dys = in_slots(near, far, last), in_slots(dy_near, dy_far, [None] * 2)
    ran.append(quarter(1, ns, dys))
    ran, dy_far = o.at(ran, dy_far)
    dy_last = last_tokens(dy_far)
    dys = in_slots(dy_near, dy_far, dy_last)
    ran.append(quarter(2, ns, dys))
    ran, dy_last = o.at(ran, dy_last)
    dys = in_slots(dy_near, dy_far, dy_last)
    p = [b for r in ran for b in r[1]]
    nears = near_cores(p)
    ran.append(quarter(3, ns, dys))
    nears, ran = o.at(nears, ran)
    p = [b for r in ran for b in r[1]]
    outs = [b for r in ran for b in r[0]]
    hids, dgs, dus = [[r[2][i] for r in ran] for i in range(3)]
    fars = far_cores(p)
    fars, = o.at(fars)
    via = send_far(p, fars)
    near_1, far_1 = hidden_grads(o.info, ns, dgs, dus, 1)
    via, near_1, far_1 = o.at(via, near_1, far_1)
    first = send_first(p, nears)
    near_0, far_0 = hidden_grads(o.info, ns, dgs, dus, 0)
    f1, f0 = cut(far_1, 2), cut(far_0, 2)
    f1[0] = swap(f1[0], "x")
    first, near_0, far_0, f1[0] = o.at(first, near_0, far_0, f1[0])
    second = send_second(p, nears, via)
    f1[1] = swap(f1[1], "x")
    n1 = cut(near_1, 2)
    go = cut(plus(n1[0], f1[0]), 2)
    came = [swap(go[0], "h")]
    down = down_grads(o.info, dys, hids)
    second, f1[1], came, down = o.at(second, f1[1], came, down)
    d_resid, d_low = finish_d_residual(dy, resid, terms(p, nears, first, second))
    d_resid, d_low = o.at(d_resid, d_low)

    near = near_tokens(d_low)
    came.append(swap(go[1], "h"))
    go += cut(plus(n1[1], f1[1]), 2)
    down_f1 = swap(down[3], "x")
    near, came, go, down_f1 = o.at(near, came, go, down_f1)
    far = far_tokens(near)
    f0[0] = swap(f0[0], "x")
    came.append(swap(go[2], "h"))
    o_nears = near_cores(outs)
    far, f0[0], came, o_nears = o.at(far, f0[0], came, o_nears)
    last = last_tokens(far)
    o_fars = far_cores(outs)
    last, o_fars = o.at(last, o_fars)
    dbs = in_slots(near, far, last)
    f0[1] = swap(f0[1], "x")
    came.append(swap(go[3], "h"))
    o_via = send_far(outs, o_fars)
    d_num, d_den, use = back_state(o.info, dbs, w_out_mine, mixed, den, tile, maps_t)
    d_num, d_den, use, f0[1], came, o_via = o.at(d_num, d_den, use, f0[1], came, o_via)
    later = entering(use, True)
    o_first = send_first(outs, o_nears)
    down_f0 = swap(down[2], "x")
    g_hid = total([[near_0], f0, came], near_0.shape, BF16)
    out_n0, out_n1, out_f0, out_f1 = out_grads(o.info, dbs, mixed, True)
    later, o_first, down_f0, g_hid, out_f0, out_f1 = o.at(later, o_first, down_f0, g_hid, out_f0, out_f1)
    down_go = plus(down[1], down_f1)
    down_came = [swap(down_go[:96], "h")]
    g_hid = exchange(g_hid)
    e, p = back(o.info, tile, values, d_num, d_den, before, later, maps, w_qkv)
    e, p, down_came, g_hid = o.at(e, p, down_came, g_hid)
    nears, fars = near_cores(p), far_cores(p)
    nears, fars = o.at(nears, fars)
    via = send_far(p, fars)
    down_came.append(swap(down_go[96:], "h"))
    out_f1, out_f0 = swap(out_f1, "x"), swap(out_f0, "x")
    head_n0, head_n1, head_f0, head_f1 = qkv_grads(o.info, xs, e, True)
    via, down_came, out_f1, out_f0, head_f0, head_f1 = o.at(via, down_came, out_f1, out_f0, head_f0, head_f1)
    first = send_first(p, nears)
    head_f1 = swap(head_f1, "x")
    out_came = swap(plus(out_n1, out_f1), "h")
    first, head_f1, out_came = o.at(first, head_f1, out_came)
    second = send_second(p, nears, via)
    head_came = swap(plus(head_n1, head_f1), "h")
    head_f0 = swap(head_f0, "x")
    g_down = total([[down[0]], [down_f0], down_came], w_down.shape, F32)
    g_out = total([[out_n0], [out_f0], [out_came]], w_out.shape, F32)
    second, head_came, head_f0 = o.at(second, head_came, head_f0)
    g_heads = exchange(total([[head_n0], [head_f0], [head_came]], head_n0.shape, BF16))
    o_second = send_second(outs, o_nears, o_via)
    input_grad = finish_input(x, d_resid, terms(p, nears, first, second))
    block_out = finish_output(resid, terms(outs, o_nears, o_first, o_second))
    return block_out, input_grad, g_heads, g_out, g_hid, g_down


def solution(mesh):
    seq, fsdp = mesh.shape["seq"], mesh.shape["fsdp"]
    fine = Mesh(mesh.devices.reshape(seq // 8, 2, 2, 2, fsdp), ("h", "l", "y", "c", "x"))
    along = ("h", "l", "y", "c")
    token, vec, mat = P("x", along, None), P(along + ("x",)), P(along + ("x",), None)
    return jax.shard_map(
        on_device,
        mesh=fine,
        in_specs=(token, P("x", None), vec, mat, mat, mat, mat, vec, mat, mat, mat, token),
        out_specs=(token, token, vec, mat, mat, mat, mat, vec, mat, mat, mat),
        check_vma=False,
    )
```

```python
import functools

import jax
import jax.numpy as jnp
import numpy as np
from jax import lax
from jax.experimental import pallas as pl
from jax.experimental.pallas import tpu as pltpu
from jax.sharding import Mesh
from jax.sharding import PartitionSpec as P

H = 16
FD = 16
DV = 128
HP = 2
ROWS = DV + 2 * FD
WIDE = 384
QK = 2 * DV
LANE_R, LANE_ONE = 64, 65
FEAT = 256
SENT = 160
SEQS = 4
TP = ("l", "y", "c")
DP = ("h", "x")
EPS = 1e-5
F32, BF16 = jnp.float32, jnp.bfloat16


def dot(a, b, dims):
    return lax.dot_general(a, b, (dims, ((), ())), preferred_element_type=F32)


def mm(a, b):
    return dot(a, b, ((1,), (0,)))


def mm_nt(a, b):
    return dot(a, b, ((1,), (1,)))


def mm_tn(a, b):
    return dot(a, b, ((0,), (0,)))


def swap(a, axis):
    return lax.ppermute(a, axis, [(0, 1), (1, 0)])


class Order:
    def __init__(self, mark):
        self.mark = mark

    def at(self, *values):
        flat, tree = jax.tree.flatten(values)
        got = lax.optimization_barrier((self.mark, *flat))
        self.mark = got[0]
        return jax.tree.unflatten(tree, got[1:])


SLOTS = ((0, 0, 256), (1, 0, 256), (2, 0, 256), (3, 0, 256), (4, 0, 256), (5, 0, 256))
SLOTS += ((6, 0, 128), (6, 128, 128), (7, 0, 128), (7, 128, 128))


def near_tokens(own, a):
    return [own, swap(own, a), swap(own, "y"), swap(own, "c")]


def chips_near(own, a):
    return [own, swap(own, a), swap(own, "y"), None]


def chip_far(near, a):
    _, from_a, from_y, _ = near
    half = from_a.shape[0] // 2
    return [swap(from_y[:half], a), swap(from_a[half:], "y")]


def cores_of(near):
    return [swap(near[2], "c"), swap(near[1], "c")]


def far_tokens(near, a):
    return chip_far(near, a) + cores_of(near)


def last_tokens(far):
    return [swap(far[0], "c"), swap(far[1], "c")]


def in_slots(near, far, last):
    return [near[0], near[3], near[2], far[2], near[1], far[3], far[0], far[1], *last]


def far_cores(p):
    return [swap(p[8], "c"), swap(p[9], "c")]


def near_cores(p):
    return [swap(p[1], "c"), swap(p[3], "c"), swap(p[5], "c")]


def plus(*terms):
    return functools.reduce(jnp.add, [t.astype(F32) for t in terms]).astype(BF16)


def send_far(p, fars, a):
    return [swap(plus(p[6], fars[0]), a), swap(plus(p[7], fars[1]), "y")]


def send_first(p, nears, a):
    half = p[6].shape[0]
    return [swap(plus(p[2][half:], nears[1][half:]), "y"), swap(plus(p[4][:half], nears[2][:half]), a)]


def send_second(p, nears, via, a):
    half = p[6].shape[0]
    y_a = plus(p[2][:half], nears[1][:half], via[0])
    a_b = plus(p[4][half:], nears[2][half:], via[1])
    return [swap(y_a, "y"), swap(a_b, a)]


def terms(p, nears, first, second):
    return [p[0], nears[0], second[0], first[1], first[0], second[1]]


def over_both(a):
    full = lax.all_gather(a, DP)
    return full.reshape((lax.axis_size("h"), lax.axis_size("x")) + a.shape)


def sum_both(parts):
    flat = parts.reshape((-1,) + parts.shape[2:])
    return lax.psum_scatter(flat, DP, scatter_dimension=0, tiled=False).astype(F32)


def sub_head():
    return lax.axis_size(DP + TP) // H == 2 * lax.axis_size("x")


def split_heads(w, width):
    rows = w.shape[0]
    w = w.T
    if sub_head():
        w = w.reshape(2, HP, 2, 2, width, rows).transpose(2, 3, 0, 1, 4, 5)
    else:
        w = w.reshape(HP, 8, width, rows).transpose(1, 0, 2, 3)
    return w.reshape(8, HP, width, rows)


def join_heads(w, width):
    rows = w.shape[-1]
    if sub_head():
        w = w.reshape(2, 2, 2, HP, width, rows).transpose(2, 3, 0, 1, 4, 5)
    else:
        w = w.transpose(1, 0, 2, 3)
    return w.reshape(H * width, rows).T


def split_hidden(first, second):
    h, x = lax.axis_size("h"), lax.axis_size("x")
    w = jnp.concatenate([first, second], 0).T
    cols = w.shape[1]
    return w.reshape(h, 8, x, -1, cols).transpose(1, 0, 2, 3, 4).reshape(8, -1, cols)


def join_hidden(w):
    h, x = lax.axis_size("h"), lax.axis_size("x")
    cols = w.shape[-1]
    w = w.reshape(8, h, x, -1, cols).transpose(1, 0, 2, 3, 4).reshape(-1, cols).T
    return w[: cols // 2], w[cols // 2 :]


LAYOUT_HEADS = ((0, 0, 0, DV), (1, 0, DV, DV), (0, DV, QK, FD), (1, DV, QK + FD, FD))
LAYOUT_HEADS += ((0, DV + FD, QK + 2 * FD, FD), (1, DV + FD, QK + 3 * FD, FD))


def layout_hidden(n):
    return ((0, 0, 0, n), (1, 0, n, n))


def slabs_to_rows(full, layout, height):
    h, x, _, n, cols = full.shape
    pair = full.reshape(h, x, 8, n, 2, cols // 2).transpose(4, 3, 0, 2, 1, 5).reshape(2, n, -1)
    rows = [pair[m, src : src + count] for m, src, _, count in layout]
    have = sum(count for *_, count in layout)
    return jnp.concatenate(rows + [jnp.zeros((height - have, pair.shape[2]), BF16)], 0)


def rows_to_slabs(rows, layout):
    h, x = lax.axis_size("h"), lax.axis_size("x")
    pair = [jnp.concatenate([rows[dst : dst + c] for m, _, dst, c in layout if m == k], 0) for k in (0, 1)]
    n = pair[0].shape[0]
    parts = jnp.stack(pair).reshape(2, n, h, 8, x, -1).transpose(2, 4, 3, 1, 0, 5)
    return parts.reshape(h, x, 8, n, -1)


def exchange(slabs, axes):
    return lax.all_to_all(slabs, axes, 0, 0, tiled=True)


def out_rows_in(full):
    if sub_head():
        h, x, rows, d = full.shape
        full = lax.all_to_all(full.reshape(2, h // 2, x, rows, d), "c", 0, 0, tiled=True)
        full = full.transpose(1, 0, 2, 3, 4)
    return full.reshape(HP * DV, -1)


def out_rows_out(grad):
    h, x = lax.axis_size("h"), lax.axis_size("x")
    d = grad.shape[1]
    if sub_head():
        grad = grad.reshape(HP, 2, x, -1, d).transpose(1, 0, 2, 3, 4)
        grad = lax.all_to_all(grad, "c", 0, 0, tiled=True)
    return grad.reshape(h, x, -1, d)


def turn(a, k):
    return lax.ppermute(a, "z", [(i, (i + k) % 4) for i in range(4)])


def ring(a):
    return [a] + [turn(a, k) for k in (1, 2, 3)]


def ring_sum(pieces):
    return [pieces[0]] + [turn(pieces[k], k) for k in (1, 2, 3)]


def line_gather(a):
    return lax.all_gather(a, "z")


def line_sum(parts):
    return lax.psum_scatter(parts, "z", scatter_dimension=0, tiled=False)


def entering(total, reverse):
    n = lax.axis_size("h")
    got = jnp.zeros_like(total)
    for s in range(1, n):
        route = [(i + s, i) if reverse else (i, i + s) for i in range(n - s)]
        came = lax.ppermute(total, "h", route)
        got = came if s == 1 else (got.astype(F32) + came.astype(F32)).astype(BF16)
    return got


def entering_line(total, reverse):
    return [turn(total, -k if reverse else k) for k in (1, 2, 3)]


def feature_maps():
    maps = np.zeros((4, 2, 128, FEAT), np.float32)
    for kind in range(4):
        where = [kind * FD + i for i in range(FD)] + [LANE_ONE]
        size = [0.5] * FD + [1.0]
        col = 0
        for i in range(FD + 1):
            for j in range(i, FD + 1):
                maps[kind, 0, where[i], col] = size[i]
                maps[kind, 1, where[j], col] = size[j] * (0.5 if kind >= 2 and i == j < FD else 1.0)
                col += 1
    return maps


MAPS = feature_maps()


def lanes(shape):
    return lax.broadcasted_iota(jnp.int32, shape, len(shape) - 1)


def where_is(info, groups, p):
    each = 8 // groups
    g = p // each if groups > 1 else 0
    return g, info[1] + (p - g * each) * 256


def lengths_of(info, g):
    return [info[4 + SEQS * g + i] for i in range(SEQS)]


def segments(info, g, places):
    end, found = 0, jnp.zeros(places.shape, jnp.int32)
    for length in lengths_of(info, g):
        end = end + length
        found = found + (places >= end).astype(jnp.int32)
    return found


def crossing(info, g, base):
    lengths = lengths_of(info, g)
    start, end, best, total = 0, lengths[0], lengths[0], lengths[0]
    for length in lengths[1:]:
        more = length > best
        start = jnp.where(more, total, start)
        total = total + length
        end = jnp.where(more, total, end)
        best = jnp.where(more, length, best)
    places = base + lax.broadcasted_iota(jnp.int32, (256, 1), 0)
    return ((places >= start) & (places < end)).astype(F32)


def pair_mask(info, g, base):
    row = lax.broadcasted_iota(jnp.int32, (256, 256), 0)
    col = lax.broadcasted_iota(jnp.int32, (256, 256), 1)
    down = segments(info, g, base + lax.broadcasted_iota(jnp.int32, (256, 1), 0))
    across = segments(info, g, base + lax.broadcasted_iota(jnp.int32, (1, 256), 1))
    return ((down == across) & (row >= col)).astype(F32)


def to_send(total):
    row = total[:, DV:].T[:1]
    at = lax.broadcasted_iota(jnp.int32, (SENT, DV), 0)
    return jnp.where(at == 156, row[:, :DV], jnp.where(at == 157, row[:, DV:], total[:SENT, :DV]))


def from_sent(sent):
    at = lax.broadcasted_iota(jnp.int32, (SENT, DV), 0)
    state = jnp.concatenate([jnp.where(at < 153, sent, 0.0), jnp.zeros((FEAT - SENT, DV), F32)], 0)
    row = jnp.concatenate([sent[156:157], sent[157:158]], 1)
    den = jnp.broadcast_to(row, (DV, FEAT)).T
    return jnp.concatenate([state, jnp.where(lanes((FEAT, DV)) == 0, den, 0.0)], 1)


def send_sums(sums, state_ref, groups, before):
    for g in range(groups):
        for h in range(HP):
            total = to_send(sums[g, h])
            if before is not None:
                total = total + before[g, h].astype(F32)
            state_ref[g, h] = total.astype(BF16)


def start_sums(info, sums, enter, groups, reverse):
    count = enter.shape[0] // groups
    for g in range(groups):
        for h in range(HP):
            came = 0.0
            for i in range(count):
                there = (info[2] + i + 1 <= 3 if reverse else info[2] - i - 1 >= 0) if count > 1 else True
                came = came + jnp.where(there, enter[i * groups + g, h].astype(F32), 0.0)
            sums[g, h] = from_sent(came)


def maps_of(tile, maps, kind):
    return mm(tile, maps[kind, 0]), mm(tile, maps[kind, 1])


def feats_t(tile, maps_t, kind):
    return (mm_nt(maps_t[kind, 0], tile) * mm_nt(maps_t[kind, 1], tile)).astype(BF16)


def feats(tile, maps, kind):
    a, b = maps_of(tile, maps, kind)
    return (a * b).astype(BF16)


def with_ones(values):
    one = (lanes((256, 128)) == 0).astype(BF16)
    return jnp.concatenate([values, one], 1)


def head_mask(h):
    at = lanes((256, 128))
    return ((at >= h * FD) & (at < (h + 1) * FD)).astype(F32)


def keys_on_queries(tile):
    return pltpu.roll(tile, 128 - HP * FD, 1)


def store(refs, r, value):
    if r < 6:
        refs[r][...] = value
        refs[r].leave()
    else:
        for i in range(2):
            refs[2 * r - 6 + i][...] = value[i * 128 : (i + 1) * 128]
            refs[2 * r - 6 + i].leave()


NEAR, FAR = tuple(range(6)), (6, 7)


def project_kernel(groups, slots, info, w, xs, maps_t, *refs):
    before = refs[0] if len(refs) == 5 else None
    tile_ref, val_ref, state_ref, sums = refs[-4:]
    sums[...] = jnp.zeros_like(sums)
    at = lanes((256, 128))
    for i, r in enumerate(slots):
        g, base = where_is(info, groups, jnp.bitwise_xor(info[0], r))
        x = xs.rows(i * 256, 256)
        wide = x.astype(F32)
        scale = lax.rsqrt(jnp.mean(wide * wide, 1, keepdims=True) + EPS)
        y = mm_nt(x, w[...]) * scale
        values = y[:, :QK].astype(BF16)
        tile = jnp.where(at == LANE_R, scale, jnp.where(at == LANE_ONE, 1.0, y[:, QK:]))
        tile_ref[i] = tile
        val_ref[i] = values
        cross = crossing(info, g, base).astype(BF16)
        low = tile.astype(BF16)
        for h in range(HP):
            feat = feats_t(low, maps_t, 2 + h)
            sums[g, h] += mm(feat, with_ones(values[:, h * DV : (h + 1) * DV]) * cross)
    tile_ref.leave()
    val_ref.leave()
    send_sums(sums, state_ref, groups, before)


def attend_kernel(groups, info, tile_ref, val_ref, enter, maps, maps_t, w, *refs):
    mixed_ref, den_ref, before_ref = refs[:3]
    outs, sums = refs[3:13], refs[13]
    start_sums(info, sums, enter, groups, False)
    for arrival in (tile_ref, val_ref, maps, maps_t):
        arrival.ready()

    def step(p, carry):
        r = jnp.bitwise_xor(info[0], p)
        tile = tile_ref[r]
        low = tile.astype(BF16)
        keys = keys_on_queries(tile).astype(BF16)
        g, base = where_is(info, groups, p)
        cross = crossing(info, g, base)
        cross_low = cross.astype(BF16)
        mask = pair_mask(info, g, base)
        den = jnp.zeros((256, 128), F32)
        for h in range(HP):
            flat = mm_nt((tile * (head_mask(h) * 0.25)).astype(BF16), keys)
            low_scores = ((1.0 + flat + 0.5 * flat * flat) * mask).astype(BF16)
            values = with_ones(val_ref[r, :, h * DV : (h + 1) * DV])
            state = sums[g, h].astype(BF16)
            before_ref[r, h] = state
            both = mm(low_scores, values) + cross * mm(feats(low, maps, h), state)
            here = both[:, DV : DV + 1]
            mixed_ref[r, :, h * DV : (h + 1) * DV] = (both[:, :DV] / here).astype(BF16)
            den = jnp.where(lanes((256, 128)) == h, here, den)
            sums[g, h] += mm(feats_t(low, maps_t, 2 + h), values * cross_low)
        den_ref[r] = den
        return carry

    lax.fori_loop(0, 8, step, 0, unroll=True)
    for out in refs[:3]:
        out.leave()
    for r in range(8):
        store(outs, r, mm(mixed_ref[r], w[...]).astype(BF16))


def back_state_kernel(groups, slots, info, w, tile_ref, den_ref, mixed_ref, maps_t, dbs, *refs):
    before = refs[0] if len(refs) == 5 else None
    d_num_ref, d_den_ref, state_ref, sums = refs[-4:]
    sums[...] = jnp.zeros_like(sums)
    at = lanes((256, 128))
    for i, r in enumerate(slots):
        g, base = where_is(info, groups, jnp.bitwise_xor(info[0], r))
        d_attn = mm_nt(dbs.rows(i * 256, 256), w[...])
        low = tile_ref[r].astype(BF16)
        cross = crossing(info, g, base).astype(BF16)
        den = den_ref[r]
        d_den = jnp.zeros((256, 128), F32)
        for h in range(HP):
            cols = slice(h * DV, (h + 1) * DV)
            inv = 1.0 / den[:, h : h + 1]
            d_num = (d_attn[:, cols] * inv).astype(BF16)
            d_num_ref[i, :, cols] = d_num
            total = -jnp.sum(d_attn[:, cols] * mixed_ref[r, :, cols].astype(F32), 1, keepdims=True) * inv
            d_den = jnp.where(at == h, total, d_den)
            grad = jnp.concatenate([d_num, jnp.where(at == 0, total, 0.0).astype(BF16)], 1)
            sums[g, h] += mm(feats_t(low, maps_t, h), grad * cross)
        d_den_ref[i] = d_den
    d_num_ref.leave()
    d_den_ref.leave()
    send_sums(sums, state_ref, groups, before)


def back_kernel(groups, info, tile_ref, val_ref, d_num_ref, d_den_ref, before_ref, enter, maps, w, *refs):
    e_ref, outs, sums = refs[0], refs[1:11], refs[11]
    start_sums(info, sums, enter, groups, True)
    for arrival in (tile_ref, val_ref, d_num_ref, d_den_ref, before_ref, maps):
        arrival.ready()
    at = lanes((256, 128))

    def through(d_feat, a, b, kind):
        return mm_nt((d_feat * b).astype(BF16), maps[kind, 0]) + mm_nt((d_feat * a).astype(BF16), maps[kind, 1])

    def step(i, carry):
        p = 7 - i
        r = jnp.bitwise_xor(info[0], p)
        tile = tile_ref[r]
        low = tile.astype(BF16)
        keys = keys_on_queries(tile)
        keys_low = keys.astype(BF16)
        g, base = where_is(info, groups, p)
        cross = crossing(info, g, base)
        cross_low = cross.astype(BF16)
        mask = pair_mask(info, g, base)
        d_tile = jnp.zeros((256, 128), F32)
        d_keys = jnp.zeros((256, 128), F32)
        scale = tile[:, LANE_R : LANE_R + 1]
        for h in range(HP):
            cols = slice(h * DV, (h + 1) * DV)
            here = head_mask(h)
            flat = mm_nt((tile * (here * 0.25)).astype(BF16), keys_low)
            low_scores = ((1.0 + flat + 0.5 * flat * flat) * mask).astype(BF16)
            values = val_ref[r, :, cols]
            d_num = d_num_ref[r, :, cols]
            d_den = d_den_ref[r][:, h : h + 1]
            back = sums[g, h].astype(BF16)
            d_flat = ((mm_nt(d_num, values) + d_den) * mask * (0.25 + 0.25 * flat)).astype(BF16)
            qa, qb = maps_of(low, maps, h)
            ka, kb = maps_of(low, maps, 2 + h)
            grad = jnp.concatenate([d_num, jnp.where(at == 0, d_den, 0.0).astype(BF16)], 1)
            d_feat_q = mm_nt(grad, before_ref[r, h]) * cross
            d_feat_k = mm_nt(with_ones(values), back) * cross
            d_tile += mm(d_flat, (keys * here).astype(BF16)) + through(d_feat_q, qa, qb, h)
            d_tile += through(d_feat_k, ka, kb, 2 + h)
            d_keys += mm_tn(d_flat, (tile * here).astype(BF16))
            d_val = mm_tn(low_scores, d_num) + cross * mm((ka * kb).astype(BF16), back[:, :DV])
            e_ref[r, :, cols] = (d_val * scale).astype(BF16)
            sums[g, h] += mm_tn((qa * qb).astype(BF16), grad * cross_low)
        d_tile = jnp.where(at < 2 * HP * FD, d_tile + pltpu.roll(d_keys, HP * FD, 1), 0.0)
        e_ref[r, :, QK:] = (d_tile * scale).astype(BF16)
        return carry

    lax.fori_loop(0, 8, step, 0)
    e_ref.leave()
    for r in range(8):
        store(outs, r, mm(e_ref[r], w[...]).astype(BF16))


def unpack_kernel(layout, turned_by, info, *refs):
    out = refs[-1]
    have = sum(count for *_, count in layout)
    if have < out.shape[0]:
        out[have:] = jnp.zeros((out.shape[0] - have, out.shape[1]), BF16)
    for k in range(4):
        z = jnp.bitwise_and(info[2] - k, 3) if turned_by else k
        for yc in range(4):
            first, second = (refs[k][yc], refs[k][4 + yc]) if turned_by else (refs[0][k, yc], refs[0][k, 4 + yc])
            pair = pack_tile(first, second)
            at = pl.multiple_of((z * 4 + yc) * 128, 128) if turned_by else (k * 4 + yc) * 128
            for m, src, dst, count in layout:
                out[dst : dst + count, pl.ds(at, 128)] = pair[m][src : src + count]


def sort_heads_kernel(info, halves, mine, other):
    halves.ready()
    for k in range(HP):
        mine[k] = halves[info[3] * 2 + k]
        other[k] = halves[(1 - info[3]) * 2 + k]


def join_halves_kernel(info, mine, other, out):
    for k in range(HP):
        out[pl.ds(pl.multiple_of(k * DV + info[3] * 64, 64), 64)] = mine[k]
        out[pl.ds(pl.multiple_of(k * DV + (1 - info[3]) * 64, 64), 64)] = other[k]


def by_step_kernel(info, mine, other, out):
    mine.ready(), other.ready()
    for k in range(4):
        z = jnp.bitwise_and(info[2] + k, 3)
        out[k] = lax.select(z // 2 == info[3], mine[z % 2], other[z % 2])


def total_kernel(groups, *refs):
    total, at = 0.0, 0
    for k in groups:
        term = [refs[at + c][...].astype(F32) for c in range(k)]
        total = total + (term[0] if k == 1 else jnp.concatenate(term, 0))
        at += k
    refs[-1][...] = total.astype(refs[-1].dtype)


def summed(pieces):
    total = pieces[0][...].astype(F32) + pieces[1][...].astype(F32)
    upper = pieces[2][...].astype(F32) + pieces[3][...].astype(F32)
    lower = pieces[4][...].astype(F32) + pieces[5][...].astype(F32)
    return total + jnp.concatenate([upper, lower], 0)


def scale_of(v):
    return lax.rsqrt(jnp.mean(v * v, 1, keepdims=True) + EPS)


def residual_kernel(x, *refs):
    resid = x[...].astype(F32) + summed(refs[:6])
    refs[6][...] = resid
    refs[7][...] = (resid * scale_of(resid)).astype(BF16)


def d_residual_kernel(dy, resid_ref, *refs):
    resid, d_n = resid_ref[...], summed(refs[:6])
    r = scale_of(resid)
    n = resid * r
    d = dy[...].astype(F32) + r * (d_n - n * jnp.mean(d_n * n, 1, keepdims=True))
    refs[6][...] = d
    refs[7][...] = d.astype(BF16)


def input_kernel(x_ref, d_resid, *refs):
    x, d_x = x_ref[...].astype(F32), summed(refs[:6])
    n = x * scale_of(x)
    refs[6][0] = d_resid[...] + d_x - n * jnp.mean(d_x * n, 1, keepdims=True)


def output_kernel(resid, *refs):
    refs[6][0] = resid[...] + summed(refs[:6])


def pack_tile(first, second):
    return [jnp.concatenate([first[:, c : c + 64], second[:, c : c + 64]], 1) for c in (0, 64)]


def over_blocks(info, left, rights, total):
    for r in range(8):
        more = mm_tn(left[r], rights.rows(r * 256, 256))
        total[...] = more if r == 0 else total[...] + more


def qkv_grads_kernel(info, e_ref, xs, out, total):
    over_blocks(info, e_ref, xs, total)
    if len(out.shape) == 2:
        out[...] = total[...].astype(BF16)
        return
    for k in range(4):
        z = jnp.bitwise_and(info[2] + k, 3)
        for yc in range(4):
            tile = total[:, pl.ds(pl.multiple_of((z * 4 + yc) * 128, 128), 128)].astype(BF16)
            pair = [
                jnp.concatenate([tile[dst : dst + c] for m, _, dst, c in LAYOUT_HEADS if m == i], 0) for i in (0, 1)
            ]
            out[k, yc], out[k, 4 + yc] = pack_tile(*pair)


def out_grads_kernel(info, mixed_ref, dbs, *refs):
    outs, total = refs[:-1], refs[-1]
    over_blocks(info, mixed_ref, dbs, total)
    if len(outs) == 1:
        outs[0][...] = total[...].astype(BF16)
        return
    for i in range(HP):
        for out, half in ((outs[0], info[3]), (outs[1], 1 - info[3])):
            out[i] = total[pl.ds(pl.multiple_of(i * DV + half * 64, 64), 64), :].astype(BF16)


def mlp_kernel(sizes, info, ns, w_gu, dys, wd, *refs):
    k = len(sizes)
    outs, dns, (hid_ref, dg_ref, du_ref) = refs[:k], refs[k : 2 * k], refs[2 * k :]
    ff, rows = wd.shape[0], 256
    starts = [sum(sizes[:i]) for i in range(len(sizes))]

    def put(refs, at, value):
        for ref, start, size in zip(refs, starts, sizes):
            if at <= start < at + rows:
                ref[...] = value[start - at : start - at + size]
                ref.leave()

    for at in range(0, sum(sizes), rows):
        n, dy = ns.rows(at, rows), dys.rows(at, rows)
        gate, up, d_hid = mm_nt(n, w_gu[:ff]), mm_nt(n, w_gu[ff:]), mm_nt(dy, wd[...])
        sig = 1.0 / (1.0 + jnp.exp(-gate))
        silu = gate * sig
        hid = (silu * up).astype(BF16)
        dg = (d_hid * up * sig * (1.0 + gate * (1.0 - sig))).astype(BF16)
        du = (d_hid * silu).astype(BF16)
        hid_ref[at : at + rows] = hid
        dg_ref[at : at + rows] = dg
        du_ref[at : at + rows] = du
        if at + rows == sum(sizes):
            for ref in (hid_ref, dg_ref, du_ref):
                ref.leave()
        put(dns, at, (mm(dg, w_gu[:ff]) + mm(du, w_gu[ff:])).astype(BF16))
        put(outs, at, mm(hid, wd[...]).astype(BF16))


def turn_over(left, scratch):
    for q in range(0, 2048, 512):
        scratch[:, q : q + 512] = left.rows(q, 512).T


def hidden_grads_kernel(info, dgs, dus, ns, out, dg_t, du_t):
    turn_over(dgs, dg_t)
    turn_over(dus, du_t)
    right = ns.ready()

    def step(i, carry):
        tile = right[:, pl.ds(pl.multiple_of(i * 256, 256), 256)]
        gate, up = mm(dg_t[...], tile).astype(BF16), mm(du_t[...], tile).astype(BF16)
        for j in range(2):
            cols = slice(j * 128, (j + 1) * 128)
            for x, slab in enumerate(pack_tile(gate[:, cols], up[:, cols])):
                out[(i // 2) * 8 + x * 4 + (i % 2) * 2 + j] = slab
        return carry

    lax.fori_loop(0, 8, step, 0)


def plain_grads_kernel(info, lefts, rights, out, left_t):
    turn_over(lefts, left_t)
    right = rights.ready()

    def step(i, carry):
        cols = pl.ds(pl.multiple_of(i * 256, 256), 256)
        out[:, cols] = mm(left_t[...], right[:, cols]).astype(BF16)
        return carry

    lax.fori_loop(0, out.shape[1] // 256, step, 0)


class Arriving:
    def __init__(self, parts, buf, sems, first):
        self.buf, self.shape, self.copies, row = buf, buf.shape, [], 0
        for i, part in enumerate(parts):
            rows = buf if len(parts) == 1 else buf.at[pl.ds(row, part.shape[0])]
            copy = pltpu.make_async_copy(part, rows, sems.at[first + i])
            copy.start()
            self.copies.append([row, part.shape[0], copy])
            row += part.shape[0]

    def ready(self, start=None, stop=None):
        for entry in list(self.copies):
            if start is None or (entry[0] < stop and start < entry[0] + entry[1]):
                entry[2].wait()
                self.copies.remove(entry)
        return self.buf

    def rows(self, start, count):
        return self.ready(start, start + count)[start : start + count]

    def __getitem__(self, at):
        return self.ready()[at]


class Leaving:
    def __init__(self, out, buf, sem):
        self.buf, self.shape, self.dtype = buf, buf.shape, buf.dtype
        self.copy, self.left = pltpu.make_async_copy(buf, out, sem), False

    def __getitem__(self, at):
        return self.buf[at]

    def __setitem__(self, at, value):
        self.buf[at] = value

    def leave(self):
        if not self.left:
            self.copy.start()
            self.left = True


def call(kernel, args, outs, scratch=(), flops=0, vmem=40):
    shapes = tuple(jax.ShapeDtypeStruct(s, t) for s, t in outs)
    flat = [a for arg in args for a in (arg if isinstance(arg, list) else [arg])]
    moved = sum(a.size * a.dtype.itemsize for a in flat) + sum(s.size * s.dtype.itemsize for s in shapes)
    groups = [arg if isinstance(arg, list) else [arg] for arg in args]
    large = [g for g in groups if g[0].dtype != jnp.int32]
    bufs = [pltpu.VMEM((sum(a.shape[0] for a in g),) + g[0].shape[1:], g[0].dtype) for g in large]
    n_in = sum(len(g) for g in large)

    def body(*refs):
        refs = list(refs)
        take = lambda n: [refs.pop(0) for _ in range(n)]
        ins, results, in_bufs, out_bufs = take(len(flat)), take(len(outs)), take(len(large)), take(len(outs))
        mine, (in_sems, out_sems) = take(len(scratch)), refs
        given, at, sem, buf = [], 0, 0, 0
        for g in groups:
            parts = ins[at : at + len(g)]
            at += len(g)
            if g[0].dtype == jnp.int32:
                given.append(parts[0])
                continue
            given.append(Arriving(parts, in_bufs[buf], in_sems, sem))
            sem, buf = sem + len(g), buf + 1
        going = [Leaving(r, b, out_sems.at[i]) for i, (r, b) in enumerate(zip(results, out_bufs))]
        kernel(*given, *going, *mine)
        for out in going:
            out.leave()
        for out in going:
            out.copy.wait()
        for arrival in given:
            if isinstance(arrival, Arriving):
                arrival.ready()

    return pl.pallas_call(
        body,
        out_shape=tuple(pltpu.HBM(s, t) for s, t in outs),
        in_specs=[pl.BlockSpec(memory_space=pltpu.SMEM if a.dtype == jnp.int32 else pltpu.HBM) for a in flat],
        out_specs=[pl.BlockSpec(memory_space=pltpu.HBM)] * len(outs),
        scratch_shapes=[
            *bufs,
            *[pltpu.VMEM(s, t) for s, t in outs],
            *scratch,
            pltpu.SemaphoreType.DMA((max(n_in, 1),)),
            pltpu.SemaphoreType.DMA((len(outs),)),
        ],
        compiler_params=pltpu.CompilerParams(vmem_limit_bytes=vmem << 20),
        cost_estimate=pl.CostEstimate(flops=flops, bytes_accessed=moved, transcendentals=0),
    )(*[a if a.dtype == jnp.int32 else pltpu.with_memory_space_constraint(a, pltpu.HBM) for a in flat])


def state_scratch(groups):
    return pltpu.VMEM((groups, HP, FEAT, 2 * DV), F32)


TOKENS = [((n, 2048), BF16) for _, _, n in SLOTS]


OWN, NEXT, LAST = slice(0, 2), slice(2, 6), slice(6, 10)


def mlp(info, ns, dys, w_gu, wd):
    ff, d = wd.shape
    sizes = [n.shape[0] for n in ns]
    blocks = [((n, d), BF16) for n in sizes]
    rows, k = sum(sizes), len(ns)
    got = call(
        functools.partial(mlp_kernel, sizes),
        [info, list(ns), w_gu, list(dys), wd],
        blocks + blocks + [((rows, ff), BF16)] * 3,
        flops=12 * rows * ff * d,
    )
    return got[:k], got[k : 2 * k], got[2 * k :]


def turned(ff):
    return pltpu.VMEM((ff, 2048), BF16)


def plain_grads(info, rights, lefts):
    ff, d = lefts[0].shape[1], rights[0].shape[1]
    shapes, flops = [((ff, d), BF16)], 2 * 2048 * ff * d
    return call(plain_grads_kernel, [info, list(lefts), list(rights)], shapes, [turned(ff)], flops, 32)[0]


def hidden_grads(info, ns, dgs, dus):
    ff, d = dgs[0].shape[1], ns[0].shape[1]
    args, shapes = [info, list(dgs), list(dus), list(ns)], [((d // 64, ff, 128), BF16)]
    got = call(hidden_grads_kernel, args, shapes, [turned(ff)] * 2, 4 * 2048 * ff * d, 36)[0]
    return got.reshape(4, 8, ff, 128)


def down_grads(info, dys, hids):
    return plain_grads(info, dys, hids).reshape(4, -1, dys[0].shape[1])


def gained(gain, w):
    return (gain * w.astype(F32)).astype(BF16)


def head_slabs(split, gain, w_query, w_key, w_value):
    parts = [split(gained(gain, w), n) for w, n in ((w_value, DV), (w_query, FD), (w_key, FD))]
    return jnp.concatenate(parts, 2).transpose(0, 2, 1, 3).reshape(8, ROWS, -1)


def project(groups, slots, info, xs, w_qkv, maps_t, before=None):
    size, d, n = 256, w_qkv.shape[1], len(slots)
    return call(
        functools.partial(project_kernel, groups, slots),
        [info, w_qkv, list(xs), maps_t] + ([] if before is None else [before]),
        [((n, size, 128), F32), ((n, size, QK), BF16), ((groups, HP, SENT, DV), BF16)],
        [state_scratch(groups)],
        flops=2 * n * size * d * WIDE,
    )


def attend(groups, info, tile, values, enter, maps, maps_t, w_out):
    size, d = 256, w_out.shape[1]
    got = call(
        functools.partial(attend_kernel, groups),
        [info, tile, values, enter, maps, maps_t, w_out],
        [((8, size, QK), BF16), ((8, size, 128), F32), ((8, HP, FEAT, 2 * DV), BF16)] + TOKENS,
        [state_scratch(groups)],
        flops=2 * 8 * size * d * QK,
    )
    return got[:3], got[3:]


def back_state(groups, slots, info, dbs, w_out, mixed, den, tile, maps_t, before=None):
    size, d, n = 256, w_out.shape[1], len(slots)
    return call(
        functools.partial(back_state_kernel, groups, slots),
        [info, w_out, tile, den, mixed, maps_t, list(dbs)] + ([] if before is None else [before]),
        [((n, size, QK), BF16), ((n, size, 128), F32), ((groups, HP, SENT, DV), BF16)],
        [state_scratch(groups)],
        flops=2 * n * size * d * QK,
    )


def back(groups, info, tile, values, d_num, d_den, before, later, maps, w_qkv):
    size, d = 256, w_qkv.shape[1]
    got = call(
        functools.partial(back_kernel, groups),
        [info, tile, values, d_num, d_den, before, later, maps, w_qkv],
        [((8, size, WIDE), BF16)] + TOKENS,
        [state_scratch(groups)],
        flops=2 * 8 * size * d * WIDE,
        vmem=28,
    )
    return got[0], got[1:]


def qkv_grads(info, xs, e, packed):
    d = xs[0].shape[1]
    outs = [((4, 8, ROWS, 128) if packed else (WIDE, d), BF16)]
    return call(qkv_grads_kernel, [info, e, list(xs)], outs, [pltpu.VMEM((WIDE, d), F32)], flops=2 * 2048 * d * WIDE)[0]


def out_grads(info, dbs, mixed, packed):
    d = dbs[0].shape[1]
    outs = [((HP, 64, d), BF16)] * 2 if packed else [((QK, d), BF16)]
    return call(out_grads_kernel, [info, mixed, list(dbs)], outs, [pltpu.VMEM((QK, d), F32)], flops=2 * 2048 * d * QK)


def unpack(info, pieces, layout, height):
    turned_by = len(pieces) > 1
    kernel = functools.partial(unpack_kernel, layout, turned_by)
    return call(kernel, [info, *pieces], [((height, 16 * 128), BF16)])[0]


def total(groups, shape, dtype):
    args = [c for g in groups for c in g]
    return call(functools.partial(total_kernel, [len(g) for g in groups]), args, [(shape, dtype)])[0]


def finish_residual(x, pieces):
    return call(residual_kernel, [x, *pieces], [(x.shape, F32), (x.shape, BF16)])


def finish_d_residual(dy, resid, pieces):
    return call(d_residual_kernel, [dy, resid, *pieces], [(dy.shape, F32), (dy.shape, BF16)])


def finish_input(x, d_resid, pieces):
    return call(input_kernel, [x, d_resid, *pieces], [((1,) + x.shape, F32)])[0]


def finish_output(resid, pieces):
    return call(output_kernel, [resid, *pieces], [((1,) + resid.shape, F32)])[0]


def gather_all(own, a):
    near = near_tokens(own, a)
    far = far_tokens(near, a)
    return in_slots(near, far, last_tokens(far))


def scatter_all(p, a):
    nears = near_cores(p)
    via = send_far(p, far_cores(p), a)
    return terms(p, nears, send_first(p, nears, a), send_second(p, nears, via, a))


def weight_grads(weights, gains, grads):
    g_query, g_key, g_value, g_gate, g_up = grads
    along = [jnp.sum(w.astype(F32) * g, -1) for w, g in zip(weights, grads)]
    one, two = along[0] + along[1] + along[2], along[3] + along[4]
    return one, gains[0] * g_query, gains[0] * g_key, gains[0] * g_value, two, gains[1] * g_gate, gains[1] * g_up


def split_of_heads(join, g_heads):
    g = g_heads.astype(F32).reshape(8, ROWS, HP, -1).transpose(0, 2, 1, 3)
    return join(g[:, :, DV : DV + FD], FD), join(g[:, :, DV + FD :], FD), join(g[:, :, :DV], DV)


def on_device(
    run, tokens, seq_lengths, norm_gain, w_query, w_key, w_value, w_out, mlp_gain, w_gate, w_up, w_down, cotangent
):
    gains = [g.astype(F32)[:, None] for g in (norm_gain, mlp_gain)]
    maps, maps_t = jnp.asarray(MAPS, BF16), jnp.asarray(MAPS.transpose(0, 1, 3, 2), BF16)
    weights = (w_query, w_key, w_value, w_gate, w_up)
    block_out, input_grad, grads, g_out, g_down = run(
        tokens[0], cotangent[0], seq_lengths, gains, weights, w_out, w_down, maps, maps_t
    )
    g = weight_grads(weights, gains, grads)
    return block_out, input_grad, *g[:4], g_out, *g[4:], g_down


def plain(x, dy, lengths, gains, weights, w_out, w_down, maps, maps_t):
    w_query, w_key, w_value, w_gate, w_up = weights
    place = jnp.stack([lax.axis_index(TP), lax.axis_index("h") * 8 * x.shape[0], 0, 0])
    info = jnp.concatenate([place.astype(jnp.int32), lengths[0]])
    heads = over_both(exchange(head_slabs(split_heads, gains[0], w_query, w_key, w_value), TP))
    w_qkv = slabs_to_rows(heads, LAYOUT_HEADS, WIDE)
    w_out_mine = out_rows_in(over_both(w_out))
    hid = over_both(exchange(split_hidden(gained(gains[1], w_gate), gained(gains[1], w_up)), TP))
    wd = over_both(w_down).reshape(-1, x.shape[1])
    ff = wd.shape[0]
    w_gu = slabs_to_rows(hid, layout_hidden(ff), 2 * ff)
    xs = gather_all(x, "l")
    tile, values, state = project(1, NEAR + FAR, info, xs, w_qkv, maps_t)
    (mixed, den, before), p = attend(1, info, tile, values, entering(state, False), maps, maps_t, w_out_mine)
    resid, n_low = finish_residual(x, scatter_all(p, "l"))
    ns, dys = gather_all(n_low, "l"), gather_all(dy, "l")
    ran = [mlp(info, ns[c], dys[c], w_gu, wd) for c in (OWN, NEXT, LAST)]
    hids, dgs, dus = [[r[2][i] for r in ran] for i in range(3)]
    block_out = finish_output(resid, scatter_all([b for r in ran for b in r[0]], "l"))
    d_resid, d_low = finish_d_residual(dy, resid, scatter_all([b for r in ran for b in r[1]], "l"))
    grads = jnp.concatenate([plain_grads(info, ns, dgs), plain_grads(info, ns, dus)], 0)
    g_hid = exchange(sum_both(rows_to_slabs(grads, layout_hidden(ff))).astype(BF16), TP)
    g_down = sum_both(plain_grads(info, dys, hids).reshape(*hid.shape[:2], -1, x.shape[1]))
    dbs = gather_all(d_low, "l")
    d_num, d_den, use = back_state(1, NEAR + FAR, info, dbs, w_out_mine, mixed, den, tile, maps_t)
    e, p = back(1, info, tile, values, d_num, d_den, before, entering(use, True), maps, w_qkv)
    input_grad = finish_input(x, d_resid, scatter_all(p, "l"))
    g_out = sum_both(out_rows_out(out_grads(info, dbs, mixed, False)[0]))
    g_heads = exchange(sum_both(rows_to_slabs(qkv_grads(info, xs, e, False), LAYOUT_HEADS)).astype(BF16), TP)
    grads = (*split_of_heads(join_heads, g_heads), *join_hidden(g_hid.astype(F32)))
    return block_out, input_grad, grads, g_out, g_down


EIGHT = ("x", "y", "c")


def split_heads_z(w, width):
    rows = w.shape[0]
    return w.T.reshape(2, HP, 4, width, rows).transpose(0, 2, 1, 3, 4).reshape(8, HP, width, rows)


def join_heads_z(w, width):
    rows = w.shape[-1]
    return w.reshape(2, 4, HP, width, rows).transpose(0, 2, 1, 3, 4).reshape(H * width, rows).T


def split_hidden_z(first, second):
    w = jnp.concatenate([first, second], 0).T.reshape(4, 4, 2, -1, 128)
    return w.transpose(2, 1, 0, 3, 4).reshape(8, -1, 128)


def join_hidden_z(w):
    w = w.reshape(2, 4, 4, -1, 128).transpose(2, 1, 0, 3, 4).reshape(-1, 128).T
    return w[:64], w[64:]


def scheduled(x, dy, lengths, gains, weights, w_out, w_down, maps, maps_t):
    w_query, w_key, w_value, w_gate, w_up = weights
    d_model = x.shape[1]
    z, my_x = lax.axis_index("z"), lax.axis_index("x")
    place = jnp.stack([lax.axis_index(EIGHT), z * 4 * x.shape[0], z, my_x]).astype(jnp.int32)
    o = Order(place)
    ax = "x"

    low = jnp.concatenate([lengths[0] % 256, lengths[0] // 256]).astype(BF16)
    low = jnp.broadcast_to(jnp.pad(low, (0, 120)), (8, 16, 128))
    heads = jnp.concatenate([head_slabs(split_heads_z, gains[0], w_query, w_key, w_value), low], 1)
    halves = line_gather(w_out)
    heads = exchange(heads, EIGHT)
    heads, x_sent, w_gate, w_up = o.at(heads, x, w_gate, w_up)
    near = chips_near(x_sent, ax)
    sent = heads[::4, ROWS, :8].astype(jnp.int32)
    info = jnp.concatenate([place, (sent[:, :4] + 256 * sent[:, 4:]).reshape(-1)])
    heads = ring(heads)
    hid = split_hidden_z(gained(gains[1], w_gate), gained(gains[1], w_up))
    heads, near, hid, x_sent, halves = o.at(heads, near, hid, x_sent, halves)
    cores = cores_of(near)
    near[3] = swap(x_sent, "c")
    wd = line_gather(w_down)
    w_qkv = unpack(info, heads, LAYOUT_HEADS, WIDE)
    near[3], cores, w_qkv = o.at(near[3], cores, w_qkv)
    far = chip_far(near, ax)
    xs = in_slots(near, far + cores, [None] * 2)
    one = project(2, NEAR, info, xs[:6], w_qkv, maps_t)
    one, far, hid = o.at(one, far, hid)
    last = last_tokens(far)
    hid = exchange(hid, EIGHT)
    w_out_near, w_out_far = call(sort_heads_kernel, [info, halves], [((HP, 64, d_model), BF16)] * 2)
    last, w_out_near, w_out_far = o.at(last, w_out_near, w_out_far)
    xs = in_slots(near, far + cores, last)

    two = project(2, FAR, info, xs[6:], w_qkv, maps_t, one[2])
    two, = o.at(two)
    tile, values = [one[0], two[0]], [one[1], two[1]]
    enter = entering_line(two[2], False)
    w_out_other = swap(w_out_far, "x")
    enter, w_out_other, wd, hid = o.at(enter, w_out_other, wd, hid)
    hid = line_gather(hid)
    w_out_mine = call(join_halves_kernel, [info, w_out_near, w_out_other], [((QK, d_model), BF16)])[0]
    (mixed, den, before), p = attend(2, info, tile, values, enter, maps, maps_t, w_out_mine)
    p, mixed, den, before = o.at(p, mixed, den, before)
    fars, nears = far_cores(p), near_cores(p)
    fars, nears = o.at(fars, nears)
    via = send_far(p, fars, ax)
    via, = o.at(via)
    first = send_first(p, nears, ax)
    first, = o.at(first)
    second = send_second(p, nears, via, ax)
    second, = o.at(second)
    resid, n_low = finish_residual(x, terms(p, nears, first, second))
    resid, n_low = o.at(resid, n_low)

    near = near_tokens(n_low, ax)
    dy_core = swap(dy, "c")
    near, dy_core = o.at(near, dy_core)
    far = chip_far(near, ax)
    wd = wd.reshape(-1, d_model)
    ff = wd.shape[0]
    w_gu = unpack(info, [hid], layout_hidden(ff), 2 * ff)
    ns, dys = in_slots(near, [None] * 4, [None] * 2), [dy, dy_core]
    run = lambda c: mlp(info, ns[c], dys[c], w_gu, wd)
    far, w_gu, dy, wd = o.at(far, w_gu, dy, wd)
    dy_near = chips_near(dy, ax)
    ran = [run(OWN)]
    cores = cores_of(near)
    ran, cores, dy_near = o.at(ran, cores, dy_near)
    dy_near[3] = dy_core
    dy_cores = cores_of(dy_near)
    last = last_tokens(far)
    dy_cores, last = o.at(dy_cores, last)
    dy_far = chip_far(dy_near, ax)
    ns, dys = in_slots(near, far + cores, last), in_slots(dy_near, dy_far + dy_cores, [None] * 2)
    ran.append(run(NEXT))
    ran, dy_far = o.at(ran, dy_far)
    dy_last = last_tokens(dy_far)
    dy_last, = o.at(dy_last)
    p = [b for r in ran for b in r[1]]
    nears = near_cores(p)
    ns, dys = in_slots(near, far + cores, last), in_slots(dy_near, dy_far + dy_cores, dy_last)
    ran.append(run(LAST))
    ran, nears = o.at(ran, nears)
    p = [b for r in ran for b in r[1]]
    outs = [b for r in ran for b in r[0]]
    parts = lambda i: [r[2][i] for r in ran]
    fars = far_cores(p)
    fars, outs = o.at(fars, outs)
    via = send_far(p, fars, ax)
    g_down = down_grads(info, dys, parts(0))
    via, g_down = o.at(via, g_down)
    g_down = line_sum(g_down)
    first = send_first(p, nears, ax)
    first, = o.at(first)
    second = send_second(p, nears, via, ax)
    second, = o.at(second)
    d_resid, d_low = finish_d_residual(dy, resid, terms(p, nears, first, second))
    d_resid, d_low = o.at(d_resid, d_low)

    near = near_tokens(d_low, ax)
    g_hid = hidden_grads(info, ns, parts(1), parts(2))
    near, g_hid = o.at(near, g_hid)
    cores = cores_of(near)
    cores, g_down, g_hid = o.at(cores, g_down, g_hid)
    g_hid = line_sum(g_hid)
    far = chip_far(near, ax)
    dbs = in_slots(near, far + cores, [None] * 2)
    one = back_state(2, NEAR, info, dbs[:6], w_out_mine, mixed, den, tile, maps_t)
    one, far = o.at(one, far)
    last = last_tokens(far)
    last, outs = o.at(last, outs)
    o_nears, o_fars = near_cores(outs), far_cores(outs)
    dbs = in_slots(near, far + cores, last)
    two = back_state(2, FAR, info, dbs[6:], w_out_mine, mixed, den, tile, maps_t, one[2])
    two, o_nears, o_fars = o.at(two, o_nears, o_fars)
    d_num, d_den = [one[0], two[0]], [one[1], two[1]]
    later = entering_line(two[2], True)
    out_near, out_far = out_grads(info, dbs, mixed, True)
    o_via = send_far(outs, o_fars, ax)
    later, out_far, o_via = o.at(later, out_far, o_via)
    out_other = swap(out_far, "x")
    o_first = send_first(outs, o_nears, ax)
    o_second = send_second(outs, o_nears, o_via, ax)
    e, p = back(2, info, tile, values, d_num, d_den, before, later, maps, w_qkv)
    e, p, out_other, o_first, o_second = o.at(e, p, out_other, o_first, o_second)
    steps = lambda a: [a[i] for i in range(4)]
    nears, fars = near_cores(p), far_cores(p)
    head_g = qkv_grads(info, xs, e, True)
    nears, fars, head_g = o.at(nears, fars, head_g)
    heads = ring_sum(steps(head_g))
    via = send_far(p, fars, ax)
    op = call(by_step_kernel, [info, out_near, out_other], [((4, 64, d_model), BF16)])[0]
    via, heads[1], heads[3], op, g_hid = o.at(via, heads[1], heads[3], op, g_hid)
    first = send_first(p, nears, ax)
    g_hid = exchange(g_hid, EIGHT)
    block_out = finish_output(resid, terms(outs, o_nears, o_first, o_second))
    first, heads[2], block_out = o.at(first, heads[2], block_out)
    second = send_second(p, nears, via, ax)
    g_heads = exchange(total([[a] for a in heads], heads[0].shape, BF16), EIGHT)
    op = ring_sum(steps(op))
    g_hid = join_hidden_z(g_hid.astype(F32))
    second, g_heads, g_hid = o.at(second, g_heads, g_hid)
    input_grad = finish_input(x, d_resid, terms(p, nears, first, second))
    g_out = total([[a] for a in op], w_out.shape, F32)
    grads = (*split_of_heads(join_heads_z, g_heads), *g_hid)
    return block_out, input_grad, grads, g_out, g_down.astype(F32)


def solution(mesh):
    seq, fsdp = mesh.shape["seq"], mesh.shape["fsdp"]
    if (seq, fsdp) == (16, 2):
        shape, along, run = (4, 2, 2, 2), ("z", "y", "c"), scheduled
    else:
        shape, along, run = (seq // 8, 2, 2, 2, fsdp), ("h", "l", "y", "c"), plain
    fine = Mesh(mesh.devices.reshape(shape), along + ("x",))
    token, vec, mat = P("x", along, None), P(along + ("x",)), P(along + ("x",), None)
    return jax.shard_map(
        functools.partial(on_device, run),
        mesh=fine,
        in_specs=(token, P("x", None), vec, mat, mat, mat, mat, vec, mat, mat, mat, token),
        out_specs=(token, token, vec, mat, mat, mat, mat, vec, mat, mat, mat),
        check_vma=False,
    )
```

```python
import functools

import jax
import jax.numpy as jnp
import numpy as np
from jax import lax
from jax.experimental import pallas as pl
from jax.experimental.pallas import tpu as pltpu
from jax.sharding import Mesh
from jax.sharding import PartitionSpec as P

H = 16
FD = 16
DV = 128
HP = 2
ROWS = DV + 2 * FD
WIDE = 384
QK = 2 * DV
LANE_R, LANE_ONE = 64, 65
FEAT = 256
SENT = 160
SEQS = 4
TP = ("l", "y", "c")
DP = ("h", "x")
EPS = 1e-5
F32, BF16 = jnp.float32, jnp.bfloat16


def dot(a, b, dims):
    return lax.dot_general(a, b, (dims, ((), ())), preferred_element_type=F32)


def mm(a, b):
    return dot(a, b, ((1,), (0,)))


def mm_nt(a, b):
    return dot(a, b, ((1,), (1,)))


def mm_tn(a, b):
    return dot(a, b, ((0,), (0,)))


def swap(a, axis):
    return lax.ppermute(a, axis, [(0, 1), (1, 0)])


class Order:
    def __init__(self, mark):
        self.mark = mark

    def at(self, *values):
        flat, tree = jax.tree.flatten(values)
        got = lax.optimization_barrier((self.mark, *flat))
        self.mark = got[0]
        return jax.tree.unflatten(tree, got[1:])


SLOTS = ((0, 0, 256), (1, 0, 256), (2, 0, 256), (3, 0, 256), (4, 0, 256), (5, 0, 256))
SLOTS += ((6, 0, 128), (6, 128, 128), (7, 0, 128), (7, 128, 128))


def near_tokens(own, a):
    return [own, swap(own, a), swap(own, "y"), swap(own, "c")]


def chips_near(own, a):
    return [own, swap(own, a), swap(own, "y"), None]


def chip_far(near, a):
    _, from_a, from_y, _ = near
    half = from_a.shape[0] // 2
    return [swap(from_y[:half], a), swap(from_a[half:], "y")]


def cores_of(near):
    return [swap(near[2], "c"), swap(near[1], "c")]


def far_tokens(near, a):
    return chip_far(near, a) + cores_of(near)


def last_tokens(far):
    return [swap(far[0], "c"), swap(far[1], "c")]


def in_slots(near, far, last):
    return [near[0], near[3], near[2], far[2], near[1], far[3], far[0], far[1], *last]


def far_cores(p):
    return [swap(p[8], "c"), swap(p[9], "c")]


def near_cores(p):
    return [swap(p[1], "c"), swap(p[3], "c"), swap(p[5], "c")]


def plus(*terms):
    return functools.reduce(jnp.add, [t.astype(F32) for t in terms]).astype(BF16)


def send_far(p, fars, a):
    return [swap(plus(p[6], fars[0]), a), swap(plus(p[7], fars[1]), "y")]


def send_first(p, nears, a):
    half = p[6].shape[0]
    return [swap(plus(p[2][half:], nears[1][half:]), "y"), swap(plus(p[4][:half], nears[2][:half]), a)]


def send_second(p, nears, via, a):
    half = p[6].shape[0]
    y_a = plus(p[2][:half], nears[1][:half], via[0])
    a_b = plus(p[4][half:], nears[2][half:], via[1])
    return [swap(y_a, "y"), swap(a_b, a)]


def terms(p, nears, first, second):
    return [p[0], nears[0], second[0], first[1], first[0], second[1]]


def over_both(a):
    full = lax.all_gather(a, DP)
    return full.reshape((lax.axis_size("h"), lax.axis_size("x")) + a.shape)


def sum_both(parts):
    flat = parts.reshape((-1,) + parts.shape[2:])
    return lax.psum_scatter(flat, DP, scatter_dimension=0, tiled=False).astype(F32)


def sub_head():
    return lax.axis_size(DP + TP) // H == 2 * lax.axis_size("x")


def split_heads(w, width):
    rows = w.shape[0]
    w = w.T
    if sub_head():
        w = w.reshape(2, HP, 2, 2, width, rows).transpose(2, 3, 0, 1, 4, 5)
    else:
        w = w.reshape(HP, 8, width, rows).transpose(1, 0, 2, 3)
    return w.reshape(8, HP, width, rows)


def join_heads(w, width):
    rows = w.shape[-1]
    if sub_head():
        w = w.reshape(2, 2, 2, HP, width, rows).transpose(2, 3, 0, 1, 4, 5)
    else:
        w = w.transpose(1, 0, 2, 3)
    return w.reshape(H * width, rows).T


def split_hidden(first, second):
    h, x = lax.axis_size("h"), lax.axis_size("x")
    w = jnp.concatenate([first, second], 0).T
    cols = w.shape[1]
    return w.reshape(h, 8, x, -1, cols).transpose(1, 0, 2, 3, 4).reshape(8, -1, cols)


def join_hidden(w):
    h, x = lax.axis_size("h"), lax.axis_size("x")
    cols = w.shape[-1]
    w = w.reshape(8, h, x, -1, cols).transpose(1, 0, 2, 3, 4).reshape(-1, cols).T
    return w[: cols // 2], w[cols // 2 :]


LAYOUT_HEADS = ((0, 0, 0, DV), (1, 0, DV, DV), (0, DV, QK, FD), (1, DV, QK + FD, FD))
LAYOUT_HEADS += ((0, DV + FD, QK + 2 * FD, FD), (1, DV + FD, QK + 3 * FD, FD))


def layout_hidden(n):
    return ((0, 0, 0, n), (1, 0, n, n))


def slabs_to_rows(full, layout, height):
    h, x, _, n, cols = full.shape
    pair = full.reshape(h, x, 8, n, 2, cols // 2).transpose(4, 3, 0, 2, 1, 5).reshape(2, n, -1)
    rows = [pair[m, src : src + count] for m, src, _, count in layout]
    have = sum(count for *_, count in layout)
    return jnp.concatenate(rows + [jnp.zeros((height - have, pair.shape[2]), BF16)], 0)


def rows_to_slabs(rows, layout):
    h, x = lax.axis_size("h"), lax.axis_size("x")
    pair = [jnp.concatenate([rows[dst : dst + c] for m, _, dst, c in layout if m == k], 0) for k in (0, 1)]
    n = pair[0].shape[0]
    parts = jnp.stack(pair).reshape(2, n, h, 8, x, -1).transpose(2, 4, 3, 1, 0, 5)
    return parts.reshape(h, x, 8, n, -1)


def exchange(slabs, axes):
    return lax.all_to_all(slabs, axes, 0, 0, tiled=True)


def out_rows_in(full):
    if sub_head():
        h, x, rows, d = full.shape
        full = lax.all_to_all(full.reshape(2, h // 2, x, rows, d), "c", 0, 0, tiled=True)
        full = full.transpose(1, 0, 2, 3, 4)
    return full.reshape(HP * DV, -1)


def out_rows_out(grad):
    h, x = lax.axis_size("h"), lax.axis_size("x")
    d = grad.shape[1]
    if sub_head():
        grad = grad.reshape(HP, 2, x, -1, d).transpose(1, 0, 2, 3, 4)
        grad = lax.all_to_all(grad, "c", 0, 0, tiled=True)
    return grad.reshape(h, x, -1, d)


def turn(a, k):
    return lax.ppermute(a, "z", [(i, (i + k) % 4) for i in range(4)])


def ring(a):
    return [a] + [turn(a, k) for k in (1, 2, 3)]


def ring_sum(pieces):
    return [pieces[0]] + [turn(pieces[k], k) for k in (1, 2, 3)]


def line_gather(a):
    return lax.all_gather(a, "z")


def line_sum(parts):
    return lax.psum_scatter(parts, "z", scatter_dimension=0, tiled=False)


def entering(total, reverse):
    n = lax.axis_size("h")
    got = jnp.zeros_like(total)
    for s in range(1, n):
        route = [(i + s, i) if reverse else (i, i + s) for i in range(n - s)]
        came = lax.ppermute(total, "h", route)
        got = came if s == 1 else (got.astype(F32) + came.astype(F32)).astype(BF16)
    return got


def entering_line(total, reverse):
    return [turn(total, -k if reverse else k) for k in (1, 2, 3)]


def feature_maps():
    maps = np.zeros((4, 2, 128, FEAT), np.float32)
    for kind in range(4):
        where = [kind * FD + i for i in range(FD)] + [LANE_ONE]
        size = [0.5] * FD + [1.0]
        col = 0
        for i in range(FD + 1):
            for j in range(i, FD + 1):
                maps[kind, 0, where[i], col] = size[i]
                maps[kind, 1, where[j], col] = size[j] * (0.5 if kind >= 2 and i == j < FD else 1.0)
                col += 1
    return maps


MAPS = feature_maps()


def lanes(shape):
    return lax.broadcasted_iota(jnp.int32, shape, len(shape) - 1)


def where_is(info, groups, p):
    each = 8 // groups
    g = p // each if groups > 1 else 0
    return g, info[1] + (p - g * each) * 256


def lengths_of(info, g):
    return [info[4 + SEQS * g + i] for i in range(SEQS)]


def segments(info, g, places):
    end, found = 0, jnp.zeros(places.shape, jnp.int32)
    for length in lengths_of(info, g):
        end = end + length
        found = found + (places >= end).astype(jnp.int32)
    return found


def crossing(info, g, base):
    lengths = lengths_of(info, g)
    start, end, best, total = 0, lengths[0], lengths[0], lengths[0]
    for length in lengths[1:]:
        more = length > best
        start = jnp.where(more, total, start)
        total = total + length
        end = jnp.where(more, total, end)
        best = jnp.where(more, length, best)
    places = base + lax.broadcasted_iota(jnp.int32, (256, 1), 0)
    return ((places >= start) & (places < end)).astype(F32)


def pair_mask(info, g, base):
    row = lax.broadcasted_iota(jnp.int32, (256, 256), 0)
    col = lax.broadcasted_iota(jnp.int32, (256, 256), 1)
    down = segments(info, g, base + lax.broadcasted_iota(jnp.int32, (256, 1), 0))
    across = segments(info, g, base + lax.broadcasted_iota(jnp.int32, (1, 256), 1))
    return ((down == across) & (row >= col)).astype(F32)


def to_send(total):
    row = total[:, DV:].T[:1]
    at = lax.broadcasted_iota(jnp.int32, (SENT, DV), 0)
    return jnp.where(at == 156, row[:, :DV], jnp.where(at == 157, row[:, DV:], total[:SENT, :DV]))


def from_sent(sent):
    at = lax.broadcasted_iota(jnp.int32, (SENT, DV), 0)
    state = jnp.concatenate([jnp.where(at < 153, sent, 0.0), jnp.zeros((FEAT - SENT, DV), F32)], 0)
    row = jnp.concatenate([sent[156:157], sent[157:158]], 1)
    den = jnp.broadcast_to(row, (DV, FEAT)).T
    return jnp.concatenate([state, jnp.where(lanes((FEAT, DV)) == 0, den, 0.0)], 1)


def send_sums(sums, state_ref, groups, before):
    for g in range(groups):
        for h in range(HP):
            total = to_send(sums[g, h])
            if before is not None:
                total = total + before[g, h].astype(F32)
            state_ref[g, h] = total.astype(BF16)


def start_sums(info, sums, enter, groups, reverse):
    count = enter.shape[0] // groups
    for g in range(groups):
        for h in range(HP):
            came = 0.0
            for i in range(count):
                there = (info[2] + i + 1 <= 3 if reverse else info[2] - i - 1 >= 0) if count > 1 else True
                came = came + jnp.where(there, enter[i * groups + g, h].astype(F32), 0.0)
            sums[g, h] = from_sent(came)


def maps_of(tile, maps, kind):
    return mm(tile, maps[kind, 0]), mm(tile, maps[kind, 1])


def feats_t(tile, maps_t, kind):
    return (mm_nt(maps_t[kind, 0], tile) * mm_nt(maps_t[kind, 1], tile)).astype(BF16)


def feats(tile, maps, kind):
    a, b = maps_of(tile, maps, kind)
    return (a * b).astype(BF16)


def with_ones(values):
    one = (lanes((256, 128)) == 0).astype(BF16)
    return jnp.concatenate([values, one], 1)


def head_mask(h):
    at = lanes((256, 128))
    return ((at >= h * FD) & (at < (h + 1) * FD)).astype(F32)


def keys_on_queries(tile):
    return pltpu.roll(tile, 128 - HP * FD, 1)


def store(refs, r, value):
    if r < 6:
        refs[r][...] = value
        refs[r].leave()
    else:
        for i in range(2):
            refs[2 * r - 6 + i][...] = value[i * 128 : (i + 1) * 128]
            refs[2 * r - 6 + i].leave()


NEAR, FAR = tuple(range(6)), (6, 7)


def project_kernel(groups, slots, info, w, xs, maps_t, *refs):
    before = refs[0] if len(refs) == 5 else None
    tile_ref, val_ref, state_ref, sums = refs[-4:]
    sums[...] = jnp.zeros_like(sums)
    at = lanes((256, 128))
    for i, r in enumerate(slots):
        g, base = where_is(info, groups, jnp.bitwise_xor(info[0], r))
        x = xs.rows(i * 256, 256)
        wide = x.astype(F32)
        scale = lax.rsqrt(jnp.mean(wide * wide, 1, keepdims=True) + EPS)
        y = mm_nt(x, w[...]) * scale
        values = y[:, :QK].astype(BF16)
        tile = jnp.where(at == LANE_R, scale, jnp.where(at == LANE_ONE, 1.0, y[:, QK:]))
        tile_ref[i] = tile
        val_ref[i] = values
        cross = crossing(info, g, base).astype(BF16)
        low = tile.astype(BF16)
        for h in range(HP):
            feat = feats_t(low, maps_t, 2 + h)
            sums[g, h] += mm(feat, with_ones(values[:, h * DV : (h + 1) * DV]) * cross)
    tile_ref.leave()
    val_ref.leave()
    send_sums(sums, state_ref, groups, before)


def attend_kernel(groups, info, tile_ref, val_ref, enter, maps, maps_t, w, *refs):
    mixed_ref, den_ref, before_ref = refs[:3]
    outs, sums = refs[3:13], refs[13]
    start_sums(info, sums, enter, groups, False)
    for arrival in (tile_ref, val_ref, maps, maps_t):
        arrival.ready()

    def step(p, carry):
        r = jnp.bitwise_xor(info[0], p)
        tile = tile_ref[r]
        low = tile.astype(BF16)
        keys = keys_on_queries(tile).astype(BF16)
        g, base = where_is(info, groups, p)
        cross = crossing(info, g, base)
        cross_low = cross.astype(BF16)
        mask = pair_mask(info, g, base)
        den = jnp.zeros((256, 128), F32)
        for h in range(HP):
            flat = mm_nt((tile * (head_mask(h) * 0.25)).astype(BF16), keys)
            low_scores = ((1.0 + flat + 0.5 * flat * flat) * mask).astype(BF16)
            values = with_ones(val_ref[r, :, h * DV : (h + 1) * DV])
            state = sums[g, h].astype(BF16)
            before_ref[r, h] = state
            both = mm(low_scores, values) + cross * mm(feats(low, maps, h), state)
            here = both[:, DV : DV + 1]
            mixed_ref[r, :, h * DV : (h + 1) * DV] = (both[:, :DV] / here).astype(BF16)
            den = jnp.where(lanes((256, 128)) == h, here, den)
            sums[g, h] += mm(feats_t(low, maps_t, 2 + h), values * cross_low)
        den_ref[r] = den
        return carry

    lax.fori_loop(0, 8, step, 0, unroll=True)
    for out in refs[:3]:
        out.leave()
    for r in range(8):
        store(outs, r, mm(mixed_ref[r], w[...]).astype(BF16))


def back_state_kernel(groups, slots, info, w, tile_ref, den_ref, mixed_ref, maps_t, dbs, *refs):
    before = refs[0] if len(refs) == 5 else None
    d_num_ref, d_den_ref, state_ref, sums = refs[-4:]
    sums[...] = jnp.zeros_like(sums)
    at = lanes((256, 128))
    for i, r in enumerate(slots):
        g, base = where_is(info, groups, jnp.bitwise_xor(info[0], r))
        d_attn = mm_nt(dbs.rows(i * 256, 256), w[...])
        low = tile_ref[r].astype(BF16)
        cross = crossing(info, g, base).astype(BF16)
        den = den_ref[r]
        d_den = jnp.zeros((256, 128), F32)
        for h in range(HP):
            cols = slice(h * DV, (h + 1) * DV)
            inv = 1.0 / den[:, h : h + 1]
            d_num = (d_attn[:, cols] * inv).astype(BF16)
            d_num_ref[i, :, cols] = d_num
            total = -jnp.sum(d_attn[:, cols] * mixed_ref[r, :, cols].astype(F32), 1, keepdims=True) * inv
            d_den = jnp.where(at == h, total, d_den)
            grad = jnp.concatenate([d_num, jnp.where(at == 0, total, 0.0).astype(BF16)], 1)
            sums[g, h] += mm(feats_t(low, maps_t, h), grad * cross)
        d_den_ref[i] = d_den
    d_num_ref.leave()
    d_den_ref.leave()
    send_sums(sums, state_ref, groups, before)


def back_kernel(groups, info, tile_ref, val_ref, d_num_ref, d_den_ref, before_ref, enter, maps, w, *refs):
    e_ref, outs, sums = refs[0], refs[1:11], refs[11]
    start_sums(info, sums, enter, groups, True)
    for arrival in (tile_ref, val_ref, d_num_ref, d_den_ref, before_ref, maps):
        arrival.ready()
    at = lanes((256, 128))

    def through(d_feat, a, b, kind):
        return mm_nt((d_feat * b).astype(BF16), maps[kind, 0]) + mm_nt((d_feat * a).astype(BF16), maps[kind, 1])

    def step(i, carry):
        p = 7 - i
        r = jnp.bitwise_xor(info[0], p)
        tile = tile_ref[r]
        low = tile.astype(BF16)
        keys = keys_on_queries(tile)
        keys_low = keys.astype(BF16)
        g, base = where_is(info, groups, p)
        cross = crossing(info, g, base)
        cross_low = cross.astype(BF16)
        mask = pair_mask(info, g, base)
        d_tile = jnp.zeros((256, 128), F32)
        d_keys = jnp.zeros((256, 128), F32)
        scale = tile[:, LANE_R : LANE_R + 1]
        for h in range(HP):
            cols = slice(h * DV, (h + 1) * DV)
            here = head_mask(h)
            flat = mm_nt((tile * (here * 0.25)).astype(BF16), keys_low)
            low_scores = ((1.0 + flat + 0.5 * flat * flat) * mask).astype(BF16)
            values = val_ref[r, :, cols]
            d_num = d_num_ref[r, :, cols]
            d_den = d_den_ref[r][:, h : h + 1]
            back = sums[g, h].astype(BF16)
            d_flat = ((mm_nt(d_num, values) + d_den) * mask * (0.25 + 0.25 * flat)).astype(BF16)
            qa, qb = maps_of(low, maps, h)
            ka, kb = maps_of(low, maps, 2 + h)
            grad = jnp.concatenate([d_num, jnp.where(at == 0, d_den, 0.0).astype(BF16)], 1)
            d_feat_q = mm_nt(grad, before_ref[r, h]) * cross
            d_feat_k = mm_nt(with_ones(values), back) * cross
            d_tile += mm(d_flat, (keys * here).astype(BF16)) + through(d_feat_q, qa, qb, h)
            d_tile += through(d_feat_k, ka, kb, 2 + h)
            d_keys += mm_tn(d_flat, (tile * here).astype(BF16))
            d_val = mm_tn(low_scores, d_num) + cross * mm((ka * kb).astype(BF16), back[:, :DV])
            e_ref[r, :, cols] = (d_val * scale).astype(BF16)
            sums[g, h] += mm_tn((qa * qb).astype(BF16), grad * cross_low)
        d_tile = jnp.where(at < 2 * HP * FD, d_tile + pltpu.roll(d_keys, HP * FD, 1), 0.0)
        e_ref[r, :, QK:] = (d_tile * scale).astype(BF16)
        return carry

    lax.fori_loop(0, 8, step, 0)
    e_ref.leave()
    for r in range(8):
        store(outs, r, mm(e_ref[r], w[...]).astype(BF16))


def unpack_kernel(layout, turned_by, info, *refs):
    out = refs[-1]
    have = sum(count for *_, count in layout)
    if have < out.shape[0]:
        out[have:] = jnp.zeros((out.shape[0] - have, out.shape[1]), BF16)
    for k in range(4):
        z = jnp.bitwise_and(info[2] - k, 3) if turned_by else k
        for yc in range(4):
            first, second = (refs[k][yc], refs[k][4 + yc]) if turned_by else (refs[0][k, yc], refs[0][k, 4 + yc])
            pair = pack_tile(first, second)
            at = pl.multiple_of((z * 4 + yc) * 128, 128) if turned_by else (k * 4 + yc) * 128
            for m, src, dst, count in layout:
                out[dst : dst + count, pl.ds(at, 128)] = pair[m][src : src + count]


def sort_heads_kernel(info, halves, mine, other):
    halves.ready()
    for k in range(HP):
        mine[k] = halves[info[3] * 2 + k]
        other[k] = halves[(1 - info[3]) * 2 + k]


def join_halves_kernel(info, mine, other, out):
    for k in range(HP):
        out[pl.ds(pl.multiple_of(k * DV + info[3] * 64, 64), 64)] = mine[k]
        out[pl.ds(pl.multiple_of(k * DV + (1 - info[3]) * 64, 64), 64)] = other[k]


def by_z_kernel(info, mine, other, out):
    mine.ready(), other.ready()
    for z in range(4):
        out[z] = lax.select(info[3] == z // 2, mine[z % 2], other[z % 2])


def hidden_out_kernel(slabs, w_gate, w_up, gain, gate_ref, up_ref, gain_ref, rows):
    part = slabs.shape[1] // 4
    for z in range(4):
        for yc in range(4):
            for x in range(2):
                at = ((z * 4 + yc) * 2 + x) * part
                rows[at : at + part] = slabs[x * 4 + yc, z * part : (z + 1) * part]
    scale, added = gain[...], jnp.zeros((64, 128), F32)
    for c in range(rows.shape[0] // 128):
        cols = slice(c * 128, (c + 1) * 128)
        both = rows[cols, :].astype(F32).T
        gate, up = both[:64], both[64:]
        added += gate * w_gate[:, cols].astype(F32) + up * w_up[:, cols].astype(F32)
        gate_ref[:, cols] = gate * scale
        up_ref[:, cols] = up * scale
    gain_ref[...] = jnp.broadcast_to(jnp.sum(added, 1, keepdims=True), (64, 128))


def heads_out_kernel(slabs, w_query, w_key, w_value, gain, query_ref, key_ref, value_ref, gain_ref, rows):
    scale, added = gain[...], jnp.zeros((64, 128), F32)
    rows[...] = jnp.zeros_like(rows)
    for x in range(2):
        for yc in range(4):
            slab = slabs[x * 4 + yc].astype(F32)
            both = slab[:DV].T
            for k in range(HP):
                head = (x * HP + k) * 4 + yc
                lanes_of = slice(k * 64, (k + 1) * 64)
                value, cols = both[lanes_of], slice(head * DV, (head + 1) * DV)
                added += value * w_value[:, cols].astype(F32)
                value_ref[:, cols] = value * scale
                for i in range(2):
                    start = DV + i * FD
                    rows[i, head * FD : (head + 1) * FD, :64] = slab[start : start + FD, lanes_of]
    total = jnp.sum(added, 1, keepdims=True)
    for i, (out, w) in enumerate(((query_ref, w_query), (key_ref, w_key))):
        grad = rows[i].T[:64]
        total += jnp.sum(grad * w[...].astype(F32), 1, keepdims=True)
        out[...] = grad * scale
    gain_ref[...] = jnp.broadcast_to(total, (64, 128))


def total_kernel(groups, *refs):
    total, at = 0.0, 0
    for k in groups:
        term = [refs[at + c][...].astype(F32) for c in range(k)]
        total = total + (term[0] if k == 1 else jnp.concatenate(term, 0))
        at += k
    refs[-1][...] = total.astype(refs[-1].dtype)


def summed(pieces):
    total = pieces[0][...].astype(F32) + pieces[1][...].astype(F32)
    upper = pieces[2][...].astype(F32) + pieces[3][...].astype(F32)
    lower = pieces[4][...].astype(F32) + pieces[5][...].astype(F32)
    return total + jnp.concatenate([upper, lower], 0)


def scale_of(v):
    return lax.rsqrt(jnp.mean(v * v, 1, keepdims=True) + EPS)


def residual_kernel(x, *refs):
    resid = x[...].astype(F32) + summed(refs[:6])
    refs[6][...] = resid
    refs[7][...] = (resid * scale_of(resid)).astype(BF16)


def d_residual_kernel(dy, resid_ref, *refs):
    resid, d_n = resid_ref[...], summed(refs[:6])
    r = scale_of(resid)
    n = resid * r
    d = dy[...].astype(F32) + r * (d_n - n * jnp.mean(d_n * n, 1, keepdims=True))
    refs[6][...] = d
    refs[7][...] = d.astype(BF16)


def input_kernel(x_ref, d_resid, *refs):
    x, d_x = x_ref[...].astype(F32), summed(refs[:6])
    n = x * scale_of(x)
    refs[6][0] = d_resid[...] + d_x - n * jnp.mean(d_x * n, 1, keepdims=True)


def output_kernel(resid, *refs):
    refs[6][0] = resid[...] + summed(refs[:6])


def pack_tile(first, second):
    return [jnp.concatenate([first[:, c : c + 64], second[:, c : c + 64]], 1) for c in (0, 64)]


def over_blocks(info, left, rights, total):
    for r in range(8):
        more = mm_tn(left[r], rights.rows(r * 256, 256))
        total[...] = more if r == 0 else total[...] + more


def qkv_grads_kernel(info, e_ref, xs, out, total):
    over_blocks(info, e_ref, xs, total)
    if len(out.shape) == 2:
        out[...] = total[...].astype(BF16)
        return
    for k in range(4):
        z = jnp.bitwise_and(info[2] + k, 3)
        for yc in range(4):
            tile = total[:, pl.ds(pl.multiple_of((z * 4 + yc) * 128, 128), 128)].astype(BF16)
            pair = [
                jnp.concatenate([tile[dst : dst + c] for m, _, dst, c in LAYOUT_HEADS if m == i], 0) for i in (0, 1)
            ]
            out[k, yc], out[k, 4 + yc] = pack_tile(*pair)


def out_grads_kernel(info, mixed_ref, dbs, *refs):
    outs, total = refs[:-1], refs[-1]
    over_blocks(info, mixed_ref, dbs, total)
    if len(outs) == 1:
        outs[0][...] = total[...].astype(BF16)
        return
    for i in range(HP):
        for out, half in ((outs[0], info[3]), (outs[1], 1 - info[3])):
            out[i] = total[pl.ds(pl.multiple_of(i * DV + half * 64, 64), 64), :].astype(BF16)


def mlp_kernel(sizes, info, ns, w_gu, dys, wd, *refs):
    k = len(sizes)
    outs, dns, (hid_ref, dg_ref, du_ref) = refs[:k], refs[k : 2 * k], refs[2 * k :]
    ff, rows = wd.shape[0], 256
    starts = [sum(sizes[:i]) for i in range(len(sizes))]

    def put(refs, at, value):
        for ref, start, size in zip(refs, starts, sizes):
            if at <= start < at + rows:
                ref[...] = value[start - at : start - at + size]
                ref.leave()

    for at in range(0, sum(sizes), rows):
        n, dy = ns.rows(at, rows), dys.rows(at, rows)
        gate, up, d_hid = mm_nt(n, w_gu[:ff]), mm_nt(n, w_gu[ff:]), mm_nt(dy, wd[...])
        sig = 1.0 / (1.0 + jnp.exp(-gate))
        silu = gate * sig
        hid = (silu * up).astype(BF16)
        dg = (d_hid * up * sig * (1.0 + gate * (1.0 - sig))).astype(BF16)
        du = (d_hid * silu).astype(BF16)
        hid_ref[at : at + rows] = hid
        dg_ref[at : at + rows] = dg
        du_ref[at : at + rows] = du
        if at + rows == sum(sizes):
            for ref in (hid_ref, dg_ref, du_ref):
                ref.leave()
        put(dns, at, (mm(dg, w_gu[:ff]) + mm(du, w_gu[ff:])).astype(BF16))
        put(outs, at, mm(hid, wd[...]).astype(BF16))


def turn_over(left, scratch):
    for q in range(0, 2048, 512):
        scratch[:, q : q + 512] = left.rows(q, 512).T


def hidden_grads_kernel(info, dgs, dus, ns, out, dg_t, du_t):
    turn_over(dgs, dg_t)
    turn_over(dus, du_t)
    right = ns.ready()

    def step(i, carry):
        tile = right[:, pl.ds(pl.multiple_of(i * 256, 256), 256)]
        gate, up = mm(dg_t[...], tile).astype(BF16), mm(du_t[...], tile).astype(BF16)
        for j in range(2):
            cols = slice(j * 128, (j + 1) * 128)
            for x, slab in enumerate(pack_tile(gate[:, cols], up[:, cols])):
                out[(i // 2) * 8 + x * 4 + (i % 2) * 2 + j] = slab
        return carry

    lax.fori_loop(0, 8, step, 0)


def plain_grads_kernel(info, lefts, rights, out, left_t):
    turn_over(lefts, left_t)
    right = rights.ready()

    def step(i, carry):
        cols = pl.ds(pl.multiple_of(i * 256, 256), 256)
        out[:, cols] = mm(left_t[...], right[:, cols]).astype(BF16)
        return carry

    lax.fori_loop(0, out.shape[1] // 256, step, 0)


class Arriving:
    def __init__(self, parts, buf, sems, first):
        self.buf, self.shape, self.copies, row = buf, buf.shape, [], 0
        for i, part in enumerate(parts):
            rows = buf if len(parts) == 1 else buf.at[pl.ds(row, part.shape[0])]
            copy = pltpu.make_async_copy(part, rows, sems.at[first + i])
            copy.start()
            self.copies.append([row, part.shape[0], copy])
            row += part.shape[0]

    def ready(self, start=None, stop=None):
        for entry in list(self.copies):
            if start is None or (entry[0] < stop and start < entry[0] + entry[1]):
                entry[2].wait()
                self.copies.remove(entry)
        return self.buf

    def rows(self, start, count):
        return self.ready(start, start + count)[start : start + count]

    def __getitem__(self, at):
        return self.ready()[at]


class Leaving:
    def __init__(self, out, buf, sem):
        self.buf, self.shape, self.dtype = buf, buf.shape, buf.dtype
        self.copy, self.left = pltpu.make_async_copy(buf, out, sem), False

    def __getitem__(self, at):
        return self.buf[at]

    def __setitem__(self, at, value):
        self.buf[at] = value

    def leave(self):
        if not self.left:
            self.copy.start()
            self.left = True


def call(kernel, args, outs, scratch=(), flops=0, vmem=40):
    shapes = tuple(jax.ShapeDtypeStruct(s, t) for s, t in outs)
    flat = [a for arg in args for a in (arg if isinstance(arg, list) else [arg])]
    moved = sum(a.size * a.dtype.itemsize for a in flat) + sum(s.size * s.dtype.itemsize for s in shapes)
    groups = [arg if isinstance(arg, list) else [arg] for arg in args]
    large = [g for g in groups if g[0].dtype != jnp.int32]
    bufs = [pltpu.VMEM((sum(a.shape[0] for a in g),) + g[0].shape[1:], g[0].dtype) for g in large]
    n_in = sum(len(g) for g in large)

    def body(*refs):
        refs = list(refs)
        take = lambda n: [refs.pop(0) for _ in range(n)]
        ins, results, in_bufs, out_bufs = take(len(flat)), take(len(outs)), take(len(large)), take(len(outs))
        mine, (in_sems, out_sems) = take(len(scratch)), refs
        given, at, sem, buf = [], 0, 0, 0
        for g in groups:
            parts = ins[at : at + len(g)]
            at += len(g)
            if g[0].dtype == jnp.int32:
                given.append(parts[0])
                continue
            given.append(Arriving(parts, in_bufs[buf], in_sems, sem))
            sem, buf = sem + len(g), buf + 1
        going = [Leaving(r, b, out_sems.at[i]) for i, (r, b) in enumerate(zip(results, out_bufs))]
        kernel(*given, *going, *mine)
        for out in going:
            out.leave()
        for out in going:
            out.copy.wait()
        for arrival in given:
            if isinstance(arrival, Arriving):
                arrival.ready()

    return pl.pallas_call(
        body,
        out_shape=tuple(pltpu.HBM(s, t) for s, t in outs),
        in_specs=[pl.BlockSpec(memory_space=pltpu.SMEM if a.dtype == jnp.int32 else pltpu.HBM) for a in flat],
        out_specs=[pl.BlockSpec(memory_space=pltpu.HBM)] * len(outs),
        scratch_shapes=[
            *bufs,
            *[pltpu.VMEM(s, t) for s, t in outs],
            *scratch,
            pltpu.SemaphoreType.DMA((max(n_in, 1),)),
            pltpu.SemaphoreType.DMA((len(outs),)),
        ],
        compiler_params=pltpu.CompilerParams(vmem_limit_bytes=vmem << 20),
        cost_estimate=pl.CostEstimate(flops=flops, bytes_accessed=moved, transcendentals=0),
    )(*[a if a.dtype == jnp.int32 else pltpu.with_memory_space_constraint(a, pltpu.HBM) for a in flat])


def state_scratch(groups):
    return pltpu.VMEM((groups, HP, FEAT, 2 * DV), F32)


TOKENS = [((n, 2048), BF16) for _, _, n in SLOTS]


OWN, NEXT, LAST = slice(0, 2), slice(2, 6), slice(6, 10)


def mlp(info, ns, dys, w_gu, wd):
    ff, d = wd.shape
    sizes = [n.shape[0] for n in ns]
    blocks = [((n, d), BF16) for n in sizes]
    rows, k = sum(sizes), len(ns)
    got = call(
        functools.partial(mlp_kernel, sizes),
        [info, list(ns), w_gu, list(dys), wd],
        blocks + blocks + [((rows, ff), BF16)] * 3,
        flops=12 * rows * ff * d,
    )
    return got[:k], got[k : 2 * k], got[2 * k :]


def turned(ff):
    return pltpu.VMEM((ff, 2048), BF16)


def plain_grads(info, rights, lefts):
    ff, d = lefts[0].shape[1], rights[0].shape[1]
    shapes, flops = [((ff, d), BF16)], 2 * 2048 * ff * d
    return call(plain_grads_kernel, [info, list(lefts), list(rights)], shapes, [turned(ff)], flops, 32)[0]


def hidden_grads(info, ns, dgs, dus):
    ff, d = dgs[0].shape[1], ns[0].shape[1]
    args, shapes = [info, list(dgs), list(dus), list(ns)], [((d // 64, ff, 128), BF16)]
    got = call(hidden_grads_kernel, args, shapes, [turned(ff)] * 2, 4 * 2048 * ff * d, 36)[0]
    return got.reshape(4, 8, ff, 128)


def down_grads(info, dys, hids):
    return plain_grads(info, dys, hids).reshape(4, -1, dys[0].shape[1])


def gained(gain, w):
    return (gain * w.astype(F32)).astype(BF16)


def head_slabs(split, gain, w_query, w_key, w_value):
    parts = [split(gained(gain, w), n) for w, n in ((w_value, DV), (w_query, FD), (w_key, FD))]
    return jnp.concatenate(parts, 2).transpose(0, 2, 1, 3).reshape(8, ROWS, -1)


def project(groups, slots, info, xs, w_qkv, maps_t, before=None):
    size, d, n = 256, w_qkv.shape[1], len(slots)
    return call(
        functools.partial(project_kernel, groups, slots),
        [info, w_qkv, list(xs), maps_t] + ([] if before is None else [before]),
        [((n, size, 128), F32), ((n, size, QK), BF16), ((groups, HP, SENT, DV), BF16)],
        [state_scratch(groups)],
        flops=2 * n * size * d * WIDE,
    )


def attend(groups, info, tile, values, enter, maps, maps_t, w_out):
    size, d = 256, w_out.shape[1]
    got = call(
        functools.partial(attend_kernel, groups),
        [info, tile, values, enter, maps, maps_t, w_out],
        [((8, size, QK), BF16), ((8, size, 128), F32), ((8, HP, FEAT, 2 * DV), BF16)] + TOKENS,
        [state_scratch(groups)],
        flops=2 * 8 * size * d * QK,
    )
    return got[:3], got[3:]


def back_state(groups, slots, info, dbs, w_out, mixed, den, tile, maps_t, before=None):
    size, d, n = 256, w_out.shape[1], len(slots)
    return call(
        functools.partial(back_state_kernel, groups, slots),
        [info, w_out, tile, den, mixed, maps_t, list(dbs)] + ([] if before is None else [before]),
        [((n, size, QK), BF16), ((n, size, 128), F32), ((groups, HP, SENT, DV), BF16)],
        [state_scratch(groups)],
        flops=2 * n * size * d * QK,
    )


def back(groups, info, tile, values, d_num, d_den, before, later, maps, w_qkv):
    size, d = 256, w_qkv.shape[1]
    got = call(
        functools.partial(back_kernel, groups),
        [info, tile, values, d_num, d_den, before, later, maps, w_qkv],
        [((8, size, WIDE), BF16)] + TOKENS,
        [state_scratch(groups)],
        flops=2 * 8 * size * d * WIDE,
        vmem=28,
    )
    return got[0], got[1:]


def qkv_grads(info, xs, e, packed):
    d = xs[0].shape[1]
    outs = [((4, 8, ROWS, 128) if packed else (WIDE, d), BF16)]
    return call(qkv_grads_kernel, [info, e, list(xs)], outs, [pltpu.VMEM((WIDE, d), F32)], flops=2 * 2048 * d * WIDE)[0]


def out_grads(info, dbs, mixed, packed):
    d = dbs[0].shape[1]
    outs = [((HP, 64, d), BF16)] * 2 if packed else [((QK, d), BF16)]
    return call(out_grads_kernel, [info, mixed, list(dbs)], outs, [pltpu.VMEM((QK, d), F32)], flops=2 * 2048 * d * QK)


def unpack(info, pieces, layout, height):
    turned_by = len(pieces) > 1
    kernel = functools.partial(unpack_kernel, layout, turned_by)
    return call(kernel, [info, *pieces], [((height, 16 * 128), BF16)])[0]


def total(groups, shape, dtype):
    args = [c for g in groups for c in g]
    return call(functools.partial(total_kernel, [len(g) for g in groups]), args, [(shape, dtype)])[0]


def finish_residual(x, pieces):
    return call(residual_kernel, [x, *pieces], [(x.shape, F32), (x.shape, BF16)])


def finish_d_residual(dy, resid, pieces):
    return call(d_residual_kernel, [dy, resid, *pieces], [(dy.shape, F32), (dy.shape, BF16)])


def finish_input(x, d_resid, pieces):
    return call(input_kernel, [x, d_resid, *pieces], [((1,) + x.shape, F32)])[0]


def finish_output(resid, pieces):
    return call(output_kernel, [resid, *pieces], [((1,) + resid.shape, F32)])[0]


def hidden_out(slabs, w_gate, w_up, gain):
    ff = w_gate.shape[1]
    outs = [((64, ff), F32), ((64, ff), F32), ((64, 128), F32)]
    gate, up, one = call(hidden_out_kernel, [slabs, w_gate, w_up, gain], outs, [pltpu.VMEM((ff, 128), BF16)])
    return one[:, 0], gate, up


def heads_out(slabs, w_query, w_key, w_value, gain):
    outs = [(w.shape, F32) for w in (w_query, w_key, w_value)] + [((64, 128), F32)]
    scratch = [pltpu.VMEM((2, H * FD, 128), F32)]
    query, key, value, one = call(heads_out_kernel, [slabs, w_query, w_key, w_value, gain], outs, scratch)
    return one[:, 0], query, key, value


def gather_all(own, a):
    near = near_tokens(own, a)
    far = far_tokens(near, a)
    return in_slots(near, far, last_tokens(far))


def scatter_all(p, a):
    nears = near_cores(p)
    via = send_far(p, far_cores(p), a)
    return terms(p, nears, send_first(p, nears, a), send_second(p, nears, via, a))


def weight_grads(weights, gains, grads):
    g_query, g_key, g_value, g_gate, g_up = grads
    along = [jnp.sum(w.astype(F32) * g, -1) for w, g in zip(weights, grads)]
    one, two = along[0] + along[1] + along[2], along[3] + along[4]
    return one, gains[0] * g_query, gains[0] * g_key, gains[0] * g_value, two, gains[1] * g_gate, gains[1] * g_up


def split_of_heads(join, g_heads):
    g = g_heads.astype(F32).reshape(8, ROWS, HP, -1).transpose(0, 2, 1, 3)
    return join(g[:, :, DV : DV + FD], FD), join(g[:, :, DV + FD :], FD), join(g[:, :, :DV], DV)


def on_device(
    run, tokens, seq_lengths, norm_gain, w_query, w_key, w_value, w_out, mlp_gain, w_gate, w_up, w_down, cotangent
):
    gains = [g.astype(F32)[:, None] for g in (norm_gain, mlp_gain)]
    maps, maps_t = jnp.asarray(MAPS, BF16), jnp.asarray(MAPS.transpose(0, 1, 3, 2), BF16)
    weights = (w_query, w_key, w_value, w_gate, w_up)
    block_out, input_grad, g, g_out, g_down = run(
        tokens[0], cotangent[0], seq_lengths, gains, weights, w_out, w_down, maps, maps_t
    )
    return block_out, input_grad, *g[:4], g_out, *g[4:], g_down


def plain(x, dy, lengths, gains, weights, w_out, w_down, maps, maps_t):
    w_query, w_key, w_value, w_gate, w_up = weights
    place = jnp.stack([lax.axis_index(TP), lax.axis_index("h") * 8 * x.shape[0], 0, 0])
    info = jnp.concatenate([place.astype(jnp.int32), lengths[0]])
    heads = over_both(exchange(head_slabs(split_heads, gains[0], w_query, w_key, w_value), TP))
    w_qkv = slabs_to_rows(heads, LAYOUT_HEADS, WIDE)
    w_out_mine = out_rows_in(over_both(w_out))
    hid = over_both(exchange(split_hidden(gained(gains[1], w_gate), gained(gains[1], w_up)), TP))
    wd = over_both(w_down).reshape(-1, x.shape[1])
    ff = wd.shape[0]
    w_gu = slabs_to_rows(hid, layout_hidden(ff), 2 * ff)
    xs = gather_all(x, "l")
    tile, values, state = project(1, NEAR + FAR, info, xs, w_qkv, maps_t)
    (mixed, den, before), p = attend(1, info, tile, values, entering(state, False), maps, maps_t, w_out_mine)
    resid, n_low = finish_residual(x, scatter_all(p, "l"))
    ns, dys = gather_all(n_low, "l"), gather_all(dy, "l")
    ran = [mlp(info, ns[c], dys[c], w_gu, wd) for c in (OWN, NEXT, LAST)]
    hids, dgs, dus = [[r[2][i] for r in ran] for i in range(3)]
    block_out = finish_output(resid, scatter_all([b for r in ran for b in r[0]], "l"))
    d_resid, d_low = finish_d_residual(dy, resid, scatter_all([b for r in ran for b in r[1]], "l"))
    grads = jnp.concatenate([plain_grads(info, ns, dgs), plain_grads(info, ns, dus)], 0)
    g_hid = exchange(sum_both(rows_to_slabs(grads, layout_hidden(ff))).astype(BF16), TP)
    g_down = sum_both(plain_grads(info, dys, hids).reshape(*hid.shape[:2], -1, x.shape[1]))
    dbs = gather_all(d_low, "l")
    d_num, d_den, use = back_state(1, NEAR + FAR, info, dbs, w_out_mine, mixed, den, tile, maps_t)
    e, p = back(1, info, tile, values, d_num, d_den, before, entering(use, True), maps, w_qkv)
    input_grad = finish_input(x, d_resid, scatter_all(p, "l"))
    g_out = sum_both(out_rows_out(out_grads(info, dbs, mixed, False)[0]))
    g_heads = exchange(sum_both(rows_to_slabs(qkv_grads(info, xs, e, False), LAYOUT_HEADS)).astype(BF16), TP)
    grads = (*split_of_heads(join_heads, g_heads), *join_hidden(g_hid.astype(F32)))
    return block_out, input_grad, weight_grads(weights, gains, grads), g_out, g_down


EIGHT = ("x", "y", "c")


def split_heads_z(w, width):
    rows = w.shape[0]
    return w.T.reshape(2, HP, 4, width, rows).transpose(0, 2, 1, 3, 4).reshape(8, HP, width, rows)


def split_hidden_z(first, second):
    w = jnp.concatenate([first, second], 0).T.reshape(4, 4, 2, -1, 128)
    return w.transpose(2, 1, 0, 3, 4).reshape(8, -1, 128)


def scheduled(x, dy, lengths, gains, weights, w_out, w_down, maps, maps_t):
    w_query, w_key, w_value, w_gate, w_up = weights
    d_model = x.shape[1]
    z, my_x = lax.axis_index("z"), lax.axis_index("x")
    place = jnp.stack([lax.axis_index(EIGHT), z * 4 * x.shape[0], z, my_x]).astype(jnp.int32)
    o = Order(place)
    ax = "x"

    low = jnp.concatenate([lengths[0] % 256, lengths[0] // 256]).astype(BF16)
    low = jnp.broadcast_to(jnp.pad(low, (0, 120)), (8, 16, 128))
    heads = jnp.concatenate([head_slabs(split_heads_z, gains[0], w_query, w_key, w_value), low], 1)
    halves = line_gather(w_out)
    heads = exchange(heads, EIGHT)
    heads, x_sent, w_gate, w_up = o.at(heads, x, w_gate, w_up)
    near = chips_near(x_sent, ax)
    sent = heads[::4, ROWS, :8].astype(jnp.int32)
    info = jnp.concatenate([place, (sent[:, :4] + 256 * sent[:, 4:]).reshape(-1)])
    heads = ring(heads)
    hid = split_hidden_z(gained(gains[1], w_gate), gained(gains[1], w_up))
    heads, near, hid, x_sent, halves = o.at(heads, near, hid, x_sent, halves)
    cores = cores_of(near)
    near[3] = swap(x_sent, "c")
    wd = line_gather(w_down)
    w_qkv = unpack(info, heads, LAYOUT_HEADS, WIDE)
    near[3], cores, w_qkv = o.at(near[3], cores, w_qkv)
    far = chip_far(near, ax)
    xs = in_slots(near, far + cores, [None] * 2)
    one = project(2, NEAR, info, xs[:6], w_qkv, maps_t)
    one, far, hid = o.at(one, far, hid)
    last = last_tokens(far)
    hid = exchange(hid, EIGHT)
    w_out_near, w_out_far = call(sort_heads_kernel, [info, halves], [((HP, 64, d_model), BF16)] * 2)
    last, w_out_near, w_out_far = o.at(last, w_out_near, w_out_far)
    xs = in_slots(near, far + cores, last)

    two = project(2, FAR, info, xs[6:], w_qkv, maps_t, one[2])
    two, = o.at(two)
    tile, values = [one[0], two[0]], [one[1], two[1]]
    enter = entering_line(two[2], False)
    w_out_other = swap(w_out_far, "x")
    enter, w_out_other, wd, hid, dy = o.at(enter, w_out_other, wd, hid, dy)
    hid = line_gather(hid)
    w_out_mine = call(join_halves_kernel, [info, w_out_near, w_out_other], [((QK, d_model), BF16)])[0]
    dy_near = near_tokens(dy, ax)
    (mixed, den, before), p = attend(2, info, tile, values, enter, maps, maps_t, w_out_mine)
    p, mixed, den, before = o.at(p, mixed, den, before)
    fars = far_cores(p)
    fars, dy_near = o.at(fars, dy_near)
    via = send_far(p, fars, ax)
    nears = near_cores(p)
    via, nears = o.at(via, nears)
    first = send_first(p, nears, ax)
    first, = o.at(first)
    second = send_second(p, nears, via, ax)
    dy_cores = cores_of(dy_near)
    second, dy_cores = o.at(second, dy_cores)
    resid, n_low = finish_residual(x, terms(p, nears, first, second))
    resid, n_low = o.at(resid, n_low)

    near = near_tokens(n_low, ax)
    near, = o.at(near)
    far, cores = chip_far(near, ax), cores_of(near)
    wd = wd.reshape(-1, d_model)
    ff = wd.shape[0]
    w_gu = unpack(info, [hid], layout_hidden(ff), 2 * ff)
    ns, dys = in_slots(near, far + cores, [None] * 2), [dy_near[0], dy_near[3]]
    run = lambda c: mlp(info, ns[c], dys[c], w_gu, wd)
    far, cores, w_gu, dy_near = o.at(far, cores, w_gu, dy_near)
    last, dy_far = last_tokens(far), chip_far(dy_near, ax)
    ran = [run(OWN)]
    ran, last, dy_far = o.at(ran, last, dy_far)
    ns, dys = in_slots(near, far + cores, last), in_slots(dy_near, dy_far + dy_cores, [None] * 2)
    dy_last = last_tokens(dy_far)
    ran.append(run(NEXT))
    ran, dy_last = o.at(ran, dy_last)
    ns, dys = in_slots(near, far + cores, last), in_slots(dy_near, dy_far + dy_cores, dy_last)
    p = [b for r in ran for b in r[1]]
    nears = near_cores(p)
    ran.append(run(LAST))
    ran, nears = o.at(ran, nears)
    p = [b for r in ran for b in r[1]]
    outs = [b for r in ran for b in r[0]]
    parts = lambda i: [r[2][i] for r in ran]
    fars = far_cores(p)
    fars, outs = o.at(fars, outs)
    via = send_far(p, fars, ax)
    g_down = down_grads(info, dys, parts(0))
    via, g_down = o.at(via, g_down)
    g_down = line_sum(g_down)
    first = send_first(p, nears, ax)
    first, = o.at(first)
    second = send_second(p, nears, via, ax)
    second, = o.at(second)
    d_resid, d_low = finish_d_residual(dy, resid, terms(p, nears, first, second))
    d_resid, d_low = o.at(d_resid, d_low)

    near = near_tokens(d_low, ax)
    g_hid = hidden_grads(info, ns, parts(1), parts(2))
    near, g_hid = o.at(near, g_hid)
    cores = cores_of(near)
    cores, g_down, g_hid = o.at(cores, g_down, g_hid)
    g_hid = line_sum(g_hid)
    far = chip_far(near, ax)
    dbs = in_slots(near, far + cores, [None] * 2)
    one = back_state(2, NEAR, info, dbs[:6], w_out_mine, mixed, den, tile, maps_t)
    one, far = o.at(one, far)
    last = last_tokens(far)
    last, outs = o.at(last, outs)
    o_nears, o_fars = near_cores(outs), far_cores(outs)
    dbs = in_slots(near, far + cores, last)
    two = back_state(2, FAR, info, dbs[6:], w_out_mine, mixed, den, tile, maps_t, one[2])
    two, o_nears, o_fars = o.at(two, o_nears, o_fars)
    d_num, d_den = [one[0], two[0]], [one[1], two[1]]
    later = entering_line(two[2], True)
    out_near, out_far = out_grads(info, dbs, mixed, True)
    o_via = send_far(outs, o_fars, ax)
    later, out_far, o_via = o.at(later, out_far, o_via)
    out_other = swap(out_far, "x")
    o_first = send_first(outs, o_nears, ax)
    o_second = send_second(outs, o_nears, o_via, ax)
    e, p = back(2, info, tile, values, d_num, d_den, before, later, maps, w_qkv)
    e, p, out_other, o_first, o_second = o.at(e, p, out_other, o_first, o_second)
    steps = lambda a: [a[i] for i in range(4)]
    nears, fars = near_cores(p), far_cores(p)
    head_g = qkv_grads(info, xs, e, True)
    nears, fars, head_g = o.at(nears, fars, head_g)
    heads = ring_sum(steps(head_g))
    via = send_far(p, fars, ax)
    g_hid = exchange(g_hid, EIGHT)
    g_out = call(by_z_kernel, [info, out_near, out_other], [((4, 64, d_model), BF16)])[0]
    via, heads[1:3], g_hid, g_out = o.at(via, heads[1:3], g_hid, g_out)
    first = send_first(p, nears, ax)
    hid_out = hidden_out(g_hid, w_gate, w_up, gains[1])
    first, heads[3], hid_out, g_out = o.at(first, heads[3], hid_out, g_out)
    g_out = line_sum(g_out)
    g_heads = exchange(total([[a] for a in heads], heads[0].shape, BF16), EIGHT)
    second = send_second(p, nears, via, ax)
    block_out = finish_output(resid, terms(outs, o_nears, o_first, o_second))
    second, g_heads, block_out = o.at(second, g_heads, block_out)
    input_grad = finish_input(x, d_resid, terms(p, nears, first, second))
    head_out = heads_out(g_heads, w_query, w_key, w_value, gains[0])
    return block_out, input_grad, (*head_out, *hid_out), g_out.astype(F32), g_down.astype(F32)


def solution(mesh):
    seq, fsdp = mesh.shape["seq"], mesh.shape["fsdp"]
    if (seq, fsdp) == (16, 2):
        shape, along, run = (4, 2, 2, 2), ("z", "y", "c"), scheduled
    else:
        shape, along, run = (seq // 8, 2, 2, 2, fsdp), ("h", "l", "y", "c"), plain
    fine = Mesh(mesh.devices.reshape(shape), along + ("x",))
    token, vec, mat = P("x", along, None), P(along + ("x",)), P(along + ("x",), None)
    return jax.shard_map(
        functools.partial(on_device, run),
        mesh=fine,
        in_specs=(token, P("x", None), vec, mat, mat, mat, mat, vec, mat, mat, mat, token),
        out_specs=(token, token, vec, mat, mat, mat, mat, vec, mat, mat, mat),
        check_vma=False,
    )
```

```python
import functools

import jax
import jax.numpy as jnp
import numpy as np
from jax import lax
from jax.experimental import pallas as pl
from jax.experimental.pallas import tpu as pltpu
from jax.sharding import Mesh
from jax.sharding import PartitionSpec as P

H = 16
FD = 16
DV = 128
HP = 2
ROWS = DV + 2 * FD
WIDE = 384
QK = 2 * DV
LANE_R, LANE_ONE = 64, 65
FEAT = 256
SENT = 160
SEQS = 4
TP = ("l", "y", "c")
DP = ("h", "x")
EPS = 1e-5
F32, BF16 = jnp.float32, jnp.bfloat16


def dot(a, b, dims):
    return lax.dot_general(a, b, (dims, ((), ())), preferred_element_type=F32)


def mm(a, b):
    return dot(a, b, ((1,), (0,)))


def mm_nt(a, b):
    return dot(a, b, ((1,), (1,)))


def mm_tn(a, b):
    return dot(a, b, ((0,), (0,)))


def swap(a, axis):
    return lax.ppermute(a, axis, [(0, 1), (1, 0)])


class Order:
    def __init__(self, mark):
        self.mark = mark

    def at(self, *values):
        flat, tree = jax.tree.flatten(values)
        got = lax.optimization_barrier((self.mark, *flat))
        self.mark = got[0]
        return jax.tree.unflatten(tree, got[1:])


SLOTS = ((0, 0, 256), (1, 0, 256), (2, 0, 256), (3, 0, 256), (4, 0, 256), (5, 0, 256))
SLOTS += ((6, 0, 128), (6, 128, 128), (7, 0, 128), (7, 128, 128))


def near_tokens(own, a):
    return [own, swap(own, a), swap(own, "y"), swap(own, "c")]


def chips_near(own, a):
    return [own, swap(own, a), swap(own, "y"), None]


def chip_far(near, a):
    _, from_a, from_y, _ = near
    half = from_a.shape[0] // 2
    return [swap(from_y[:half], a), swap(from_a[half:], "y")]


def cores_of(near):
    return [swap(near[2], "c"), swap(near[1], "c")]


def far_tokens(near, a):
    return chip_far(near, a) + cores_of(near)


def last_tokens(far):
    return [swap(far[0], "c"), swap(far[1], "c")]


def in_slots(near, far, last):
    return [near[0], near[3], near[2], far[2], near[1], far[3], far[0], far[1], *last]


def far_cores(p):
    return [swap(p[8], "c"), swap(p[9], "c")]


def near_cores(p):
    return [swap(p[1], "c"), swap(p[3], "c"), swap(p[5], "c")]


def plus(*terms):
    return functools.reduce(jnp.add, [t.astype(F32) for t in terms]).astype(BF16)


def send_far(p, fars, a):
    return [swap(plus(p[6], fars[0]), a), swap(plus(p[7], fars[1]), "y")]


def send_first(p, nears, a):
    half = p[6].shape[0]
    return [swap(plus(p[2][half:], nears[1][half:]), "y"), swap(plus(p[4][:half], nears[2][:half]), a)]


def send_second(p, nears, via, a):
    half = p[6].shape[0]
    y_a = plus(p[2][:half], nears[1][:half], via[0])
    a_b = plus(p[4][half:], nears[2][half:], via[1])
    return [swap(y_a, "y"), swap(a_b, a)]


def terms(p, nears, first, second):
    return [p[0], nears[0], second[0], first[1], first[0], second[1]]


def over_both(a):
    full = lax.all_gather(a, DP)
    return full.reshape((lax.axis_size("h"), lax.axis_size("x")) + a.shape)


def sum_both(parts):
    flat = parts.reshape((-1,) + parts.shape[2:])
    return lax.psum_scatter(flat, DP, scatter_dimension=0, tiled=False).astype(F32)


def sub_head():
    return lax.axis_size(DP + TP) // H == 2 * lax.axis_size("x")


def split_heads(w, width):
    rows = w.shape[0]
    w = w.T
    if sub_head():
        w = w.reshape(2, HP, 2, 2, width, rows).transpose(2, 3, 0, 1, 4, 5)
    else:
        w = w.reshape(HP, 8, width, rows).transpose(1, 0, 2, 3)
    return w.reshape(8, HP, width, rows)


def join_heads(w, width):
    rows = w.shape[-1]
    if sub_head():
        w = w.reshape(2, 2, 2, HP, width, rows).transpose(2, 3, 0, 1, 4, 5)
    else:
        w = w.transpose(1, 0, 2, 3)
    return w.reshape(H * width, rows).T


def split_hidden(first, second):
    h, x = lax.axis_size("h"), lax.axis_size("x")
    w = jnp.concatenate([first, second], 0).T
    cols = w.shape[1]
    return w.reshape(h, 8, x, -1, cols).transpose(1, 0, 2, 3, 4).reshape(8, -1, cols)


def join_hidden(w):
    h, x = lax.axis_size("h"), lax.axis_size("x")
    cols = w.shape[-1]
    w = w.reshape(8, h, x, -1, cols).transpose(1, 0, 2, 3, 4).reshape(-1, cols).T
    return w[: cols // 2], w[cols // 2 :]


LAYOUT_HEADS = ((0, 0, 0, DV), (1, 0, DV, DV), (0, DV, QK, FD), (1, DV, QK + FD, FD))
LAYOUT_HEADS += ((0, DV + FD, QK + 2 * FD, FD), (1, DV + FD, QK + 3 * FD, FD))


def layout_hidden(n):
    return ((0, 0, 0, n), (1, 0, n, n))


def slabs_to_rows(full, layout, height):
    h, x, _, n, cols = full.shape
    pair = full.reshape(h, x, 8, n, 2, cols // 2).transpose(4, 3, 0, 2, 1, 5).reshape(2, n, -1)
    rows = [pair[m, src : src + count] for m, src, _, count in layout]
    have = sum(count for *_, count in layout)
    return jnp.concatenate(rows + [jnp.zeros((height - have, pair.shape[2]), BF16)], 0)


def rows_to_slabs(rows, layout):
    h, x = lax.axis_size("h"), lax.axis_size("x")
    pair = [jnp.concatenate([rows[dst : dst + c] for m, _, dst, c in layout if m == k], 0) for k in (0, 1)]
    n = pair[0].shape[0]
    parts = jnp.stack(pair).reshape(2, n, h, 8, x, -1).transpose(2, 4, 3, 1, 0, 5)
    return parts.reshape(h, x, 8, n, -1)


def exchange(slabs, axes):
    return lax.all_to_all(slabs, axes, 0, 0, tiled=True)


def out_rows_in(full):
    if sub_head():
        h, x, rows, d = full.shape
        full = lax.all_to_all(full.reshape(2, h // 2, x, rows, d), "c", 0, 0, tiled=True)
        full = full.transpose(1, 0, 2, 3, 4)
    return full.reshape(HP * DV, -1)


def out_rows_out(grad):
    h, x = lax.axis_size("h"), lax.axis_size("x")
    d = grad.shape[1]
    if sub_head():
        grad = grad.reshape(HP, 2, x, -1, d).transpose(1, 0, 2, 3, 4)
        grad = lax.all_to_all(grad, "c", 0, 0, tiled=True)
    return grad.reshape(h, x, -1, d)


def turn(a, k):
    return lax.ppermute(a, "z", [(i, (i + k) % 4) for i in range(4)])


def ring(a):
    return [a] + [turn(a, k) for k in (1, 2, 3)]


def ring_sum(pieces):
    return [pieces[0]] + [turn(pieces[k], k) for k in (1, 2, 3)]


def line_gather(a):
    return lax.all_gather(a, "z")


def line_sum(parts):
    return lax.psum_scatter(parts, "z", scatter_dimension=0, tiled=False)


def entering(total, reverse):
    n = lax.axis_size("h")
    got = jnp.zeros_like(total)
    for s in range(1, n):
        route = [(i + s, i) if reverse else (i, i + s) for i in range(n - s)]
        came = lax.ppermute(total, "h", route)
        got = came if s == 1 else (got.astype(F32) + came.astype(F32)).astype(BF16)
    return got


def entering_line(total, reverse):
    z, sign = lax.axis_index("z"), -1 if reverse else 1
    one = turn(total, sign)
    there = z < 3 if reverse else z > 0
    return [one, turn(plus(total, jnp.where(there, one, 0)), 2 * sign)]


def feature_maps():
    maps = np.zeros((4, 2, 128, FEAT), np.float32)
    for kind in range(4):
        where = [kind * FD + i for i in range(FD)] + [LANE_ONE]
        size = [0.5] * FD + [1.0]
        col = 0
        for i in range(FD + 1):
            for j in range(i, FD + 1):
                maps[kind, 0, where[i], col] = size[i]
                maps[kind, 1, where[j], col] = size[j] * (0.5 if kind >= 2 and i == j < FD else 1.0)
                col += 1
    return maps


MAPS = feature_maps()


def lanes(shape):
    return lax.broadcasted_iota(jnp.int32, shape, len(shape) - 1)


def where_is(info, groups, p):
    each = 8 // groups
    g = p // each if groups > 1 else 0
    return g, info[1] + (p - g * each) * 256


def lengths_of(info, g):
    return [info[4 + SEQS * g + i] for i in range(SEQS)]


def segments(info, g, places):
    end, found = 0, jnp.zeros(places.shape, jnp.int32)
    for length in lengths_of(info, g):
        end = end + length
        found = found + (places >= end).astype(jnp.int32)
    return found


def crossing(info, g, base):
    lengths = lengths_of(info, g)
    start, end, best, total = 0, lengths[0], lengths[0], lengths[0]
    for length in lengths[1:]:
        more = length > best
        start = jnp.where(more, total, start)
        total = total + length
        end = jnp.where(more, total, end)
        best = jnp.where(more, length, best)
    places = base + lax.broadcasted_iota(jnp.int32, (256, 1), 0)
    return ((places >= start) & (places < end)).astype(F32)


def pair_mask(info, g, base):
    row = lax.broadcasted_iota(jnp.int32, (256, 256), 0)
    col = lax.broadcasted_iota(jnp.int32, (256, 256), 1)
    down = segments(info, g, base + lax.broadcasted_iota(jnp.int32, (256, 1), 0))
    across = segments(info, g, base + lax.broadcasted_iota(jnp.int32, (1, 256), 1))
    return ((down == across) & (row >= col)).astype(F32)


def to_send(total):
    row = total[:, DV:].T[:1]
    at = lax.broadcasted_iota(jnp.int32, (SENT, DV), 0)
    return jnp.where(at == 156, row[:, :DV], jnp.where(at == 157, row[:, DV:], total[:SENT, :DV]))


def from_sent(sent):
    at = lax.broadcasted_iota(jnp.int32, (SENT, DV), 0)
    state = jnp.concatenate([jnp.where(at < 153, sent, 0.0), jnp.zeros((FEAT - SENT, DV), F32)], 0)
    row = jnp.concatenate([sent[156:157], sent[157:158]], 1)
    den = jnp.broadcast_to(row, (DV, FEAT)).T
    return jnp.concatenate([state, jnp.where(lanes((FEAT, DV)) == 0, den, 0.0)], 1)


def send_sums(sums, state_ref, groups, before):
    for g in range(groups):
        for h in range(HP):
            total = to_send(sums[g, h])
            if before is not None:
                total = total + before[g, h].astype(F32)
            state_ref[g, h] = total.astype(BF16)


def start_sums(info, sums, enter, groups, reverse):
    count = enter.shape[0] // groups
    for g in range(groups):
        for h in range(HP):
            came = 0.0
            for i in range(count):
                there = (info[2] + i + 1 <= 3 if reverse else info[2] - i - 1 >= 0) if count > 1 else True
                came = came + jnp.where(there, enter[i * groups + g, h].astype(F32), 0.0)
            sums[g, h] = from_sent(came)


def maps_of(tile, maps, kind):
    return mm(tile, maps[kind, 0]), mm(tile, maps[kind, 1])


def feats_t(tile, maps_t, kind):
    return (mm_nt(maps_t[kind, 0], tile) * mm_nt(maps_t[kind, 1], tile)).astype(BF16)


def feats(tile, maps, kind):
    a, b = maps_of(tile, maps, kind)
    return (a * b).astype(BF16)


def with_ones(values):
    one = (lanes((256, 128)) == 0).astype(BF16)
    return jnp.concatenate([values, one], 1)


def head_mask(h):
    at = lanes((256, 128))
    return ((at >= h * FD) & (at < (h + 1) * FD)).astype(F32)


def keys_on_queries(tile):
    return pltpu.roll(tile, 128 - HP * FD, 1)


def store(refs, r, value):
    if r < 6:
        refs[r][...] = value
        refs[r].leave()
    else:
        for i in range(2):
            refs[2 * r - 6 + i][...] = value[i * 128 : (i + 1) * 128]
            refs[2 * r - 6 + i].leave()


NEAR, FAR = tuple(range(6)), (6, 7)


def project_kernel(groups, slots, info, w, xs, maps_t, *refs):
    before = refs[0] if len(refs) == 5 else None
    tile_ref, val_ref, state_ref, sums = refs[-4:]
    sums[...] = jnp.zeros_like(sums)
    at = lanes((256, 128))
    for i, r in enumerate(slots):
        g, base = where_is(info, groups, jnp.bitwise_xor(info[0], r))
        x = xs.rows(i * 256, 256)
        wide = x.astype(F32)
        scale = lax.rsqrt(jnp.mean(wide * wide, 1, keepdims=True) + EPS)
        y = mm_nt(x, w[...]) * scale
        values = y[:, :QK].astype(BF16)
        tile = jnp.where(at == LANE_R, scale, jnp.where(at == LANE_ONE, 1.0, y[:, QK:]))
        tile_ref[i] = tile
        val_ref[i] = values
        cross = crossing(info, g, base).astype(BF16)
        low = tile.astype(BF16)
        for h in range(HP):
            feat = feats_t(low, maps_t, 2 + h)
            sums[g, h] += mm(feat, with_ones(values[:, h * DV : (h + 1) * DV]) * cross)
    tile_ref.leave()
    val_ref.leave()
    send_sums(sums, state_ref, groups, before)


def attend_kernel(groups, info, tile_ref, val_ref, enter, maps, maps_t, w, *refs):
    mixed_ref, den_ref, before_ref = refs[:3]
    outs, sums = refs[3:13], refs[13]
    start_sums(info, sums, enter, groups, False)
    for arrival in (tile_ref, val_ref, maps, maps_t):
        arrival.ready()

    def step(p, carry):
        r = jnp.bitwise_xor(info[0], p)
        tile = tile_ref[r]
        low = tile.astype(BF16)
        keys = keys_on_queries(tile).astype(BF16)
        g, base = where_is(info, groups, p)
        cross = crossing(info, g, base)
        cross_low = cross.astype(BF16)
        mask = pair_mask(info, g, base)
        den = jnp.zeros((256, 128), F32)
        for h in range(HP):
            flat = mm_nt((tile * (head_mask(h) * 0.25)).astype(BF16), keys)
            low_scores = ((1.0 + flat + 0.5 * flat * flat) * mask).astype(BF16)
            values = with_ones(val_ref[r, :, h * DV : (h + 1) * DV])
            state = sums[g, h].astype(BF16)
            before_ref[r, h] = state
            both = mm(low_scores, values) + cross * mm(feats(low, maps, h), state)
            here = both[:, DV : DV + 1]
            mixed_ref[r, :, h * DV : (h + 1) * DV] = (both[:, :DV] / here).astype(BF16)
            den = jnp.where(lanes((256, 128)) == h, here, den)
            sums[g, h] += mm(feats_t(low, maps_t, 2 + h), values * cross_low)
        den_ref[r] = den
        return carry

    lax.fori_loop(0, 8, step, 0, unroll=True)
    for out in refs[:3]:
        out.leave()
    for r in range(8):
        store(outs, r, mm(mixed_ref[r], w[...]).astype(BF16))


def back_state_kernel(groups, slots, info, w, tile_ref, den_ref, mixed_ref, maps_t, dbs, *refs):
    before = refs[0] if len(refs) == 5 else None
    d_num_ref, d_den_ref, state_ref, sums = refs[-4:]
    sums[...] = jnp.zeros_like(sums)
    at = lanes((256, 128))
    for i, r in enumerate(slots):
        g, base = where_is(info, groups, jnp.bitwise_xor(info[0], r))
        d_attn = mm_nt(dbs.rows(i * 256, 256), w[...])
        low = tile_ref[r].astype(BF16)
        cross = crossing(info, g, base).astype(BF16)
        den = den_ref[r]
        d_den = jnp.zeros((256, 128), F32)
        for h in range(HP):
            cols = slice(h * DV, (h + 1) * DV)
            inv = 1.0 / den[:, h : h + 1]
            d_num = (d_attn[:, cols] * inv).astype(BF16)
            d_num_ref[i, :, cols] = d_num
            total = -jnp.sum(d_attn[:, cols] * mixed_ref[r, :, cols].astype(F32), 1, keepdims=True) * inv
            d_den = jnp.where(at == h, total, d_den)
            grad = jnp.concatenate([d_num, jnp.where(at == 0, total, 0.0).astype(BF16)], 1)
            sums[g, h] += mm(feats_t(low, maps_t, h), grad * cross)
        d_den_ref[i] = d_den
    d_num_ref.leave()
    d_den_ref.leave()
    send_sums(sums, state_ref, groups, before)


def back_kernel(groups, info, tile_ref, val_ref, d_num_ref, d_den_ref, before_ref, enter, maps, w, *refs):
    e_ref, outs, sums = refs[0], refs[1:11], refs[11]
    start_sums(info, sums, enter, groups, True)
    for arrival in (tile_ref, val_ref, d_num_ref, d_den_ref, before_ref, maps):
        arrival.ready()
    at = lanes((256, 128))

    def through(d_feat, a, b, kind):
        return mm_nt((d_feat * b).astype(BF16), maps[kind, 0]) + mm_nt((d_feat * a).astype(BF16), maps[kind, 1])

    def step(i, carry):
        p = 7 - i
        r = jnp.bitwise_xor(info[0], p)
        tile = tile_ref[r]
        low = tile.astype(BF16)
        keys = keys_on_queries(tile)
        keys_low = keys.astype(BF16)
        g, base = where_is(info, groups, p)
        cross = crossing(info, g, base)
        cross_low = cross.astype(BF16)
        mask = pair_mask(info, g, base)
        d_tile = jnp.zeros((256, 128), F32)
        d_keys = jnp.zeros((256, 128), F32)
        scale = tile[:, LANE_R : LANE_R + 1]
        for h in range(HP):
            cols = slice(h * DV, (h + 1) * DV)
            here = head_mask(h)
            flat = mm_nt((tile * (here * 0.25)).astype(BF16), keys_low)
            low_scores = ((1.0 + flat + 0.5 * flat * flat) * mask).astype(BF16)
            values = val_ref[r, :, cols]
            d_num = d_num_ref[r, :, cols]
            d_den = d_den_ref[r][:, h : h + 1]
            back = sums[g, h].astype(BF16)
            d_flat = ((mm_nt(d_num, values) + d_den) * mask * (0.25 + 0.25 * flat)).astype(BF16)
            qa, qb = maps_of(low, maps, h)
            ka, kb = maps_of(low, maps, 2 + h)
            grad = jnp.concatenate([d_num, jnp.where(at == 0, d_den, 0.0).astype(BF16)], 1)
            d_feat_q = mm_nt(grad, before_ref[r, h]) * cross
            d_feat_k = mm_nt(with_ones(values), back) * cross
            d_tile += mm(d_flat, (keys * here).astype(BF16)) + through(d_feat_q, qa, qb, h)
            d_tile += through(d_feat_k, ka, kb, 2 + h)
            d_keys += mm_tn(d_flat, (tile * here).astype(BF16))
            d_val = mm_tn(low_scores, d_num) + cross * mm((ka * kb).astype(BF16), back[:, :DV])
            e_ref[r, :, cols] = (d_val * scale).astype(BF16)
            sums[g, h] += mm_tn((qa * qb).astype(BF16), grad * cross_low)
        d_tile = jnp.where(at < 2 * HP * FD, d_tile + pltpu.roll(d_keys, HP * FD, 1), 0.0)
        e_ref[r, :, QK:] = (d_tile * scale).astype(BF16)
        return carry

    lax.fori_loop(0, 8, step, 0)
    e_ref.leave()
    for r in range(8):
        store(outs, r, mm(e_ref[r], w[...]).astype(BF16))


def unpack_kernel(layout, turned_by, info, *refs):
    out = refs[-1]
    have = sum(count for *_, count in layout)
    if have < out.shape[0]:
        out[have:] = jnp.zeros((out.shape[0] - have, out.shape[1]), BF16)
    for k in range(4):
        z = jnp.bitwise_and(info[2] - k, 3) if turned_by else k
        for yc in range(4):
            first, second = (refs[k][yc], refs[k][4 + yc]) if turned_by else (refs[0][k, yc], refs[0][k, 4 + yc])
            pair = pack_tile(first, second)
            at = pl.multiple_of((z * 4 + yc) * 128, 128) if turned_by else (k * 4 + yc) * 128
            for m, src, dst, count in layout:
                out[dst : dst + count, pl.ds(at, 128)] = pair[m][src : src + count]


def sort_heads_kernel(info, halves, mine, other):
    halves.ready()
    for k in range(HP):
        mine[k] = halves[info[3] * 2 + k]
        other[k] = halves[(1 - info[3]) * 2 + k]


def join_halves_kernel(info, mine, other, out):
    for k in range(HP):
        out[pl.ds(pl.multiple_of(k * DV + info[3] * 64, 64), 64)] = mine[k]
        out[pl.ds(pl.multiple_of(k * DV + (1 - info[3]) * 64, 64), 64)] = other[k]


def by_z_kernel(info, mine, other, out):
    mine.ready(), other.ready()
    for z in range(4):
        out[z] = lax.select(info[3] == z // 2, mine[z % 2], other[z % 2])


def hidden_out_kernel(slabs, w_gate, w_up, gain, gate_ref, up_ref, gain_ref, rows):
    part = slabs.shape[1] // 4
    for z in range(4):
        for yc in range(4):
            for x in range(2):
                at = ((z * 4 + yc) * 2 + x) * part
                rows[at : at + part] = slabs[x * 4 + yc, z * part : (z + 1) * part]
    scale, added = gain[...], jnp.zeros((64, 128), F32)
    for c in range(rows.shape[0] // 128):
        cols = slice(c * 128, (c + 1) * 128)
        both = rows[cols, :].astype(F32).T
        gate, up = both[:64], both[64:]
        added += gate * w_gate[:, cols].astype(F32) + up * w_up[:, cols].astype(F32)
        gate_ref[:, cols] = gate * scale
        up_ref[:, cols] = up * scale
    gain_ref[...] = jnp.broadcast_to(jnp.sum(added, 1, keepdims=True), (64, 128))


def heads_out_kernel(slabs, w_query, w_key, w_value, gain, query_ref, key_ref, value_ref, gain_ref, rows):
    scale, added = gain[...], jnp.zeros((64, 128), F32)
    rows[...] = jnp.zeros_like(rows)
    for x in range(2):
        for yc in range(4):
            slab = slabs[x * 4 + yc].astype(F32)
            both = slab[:DV].T
            for k in range(HP):
                head = (x * HP + k) * 4 + yc
                lanes_of = slice(k * 64, (k + 1) * 64)
                value, cols = both[lanes_of], slice(head * DV, (head + 1) * DV)
                added += value * w_value[:, cols].astype(F32)
                value_ref[:, cols] = value * scale
                for i in range(2):
                    start = DV + i * FD
                    rows[i, head * FD : (head + 1) * FD, :64] = slab[start : start + FD, lanes_of]
    total = jnp.sum(added, 1, keepdims=True)
    for i, (out, w) in enumerate(((query_ref, w_query), (key_ref, w_key))):
        grad = rows[i].T[:64]
        total += jnp.sum(grad * w[...].astype(F32), 1, keepdims=True)
        out[...] = grad * scale
    gain_ref[...] = jnp.broadcast_to(total, (64, 128))


def total_kernel(groups, *refs):
    total, at = 0.0, 0
    for k in groups:
        term = [refs[at + c][...].astype(F32) for c in range(k)]
        total = total + (term[0] if k == 1 else jnp.concatenate(term, 0))
        at += k
    refs[-1][...] = total.astype(refs[-1].dtype)


def summed(pieces):
    total = pieces[0][...].astype(F32) + pieces[1][...].astype(F32)
    upper = pieces[2][...].astype(F32) + pieces[3][...].astype(F32)
    lower = pieces[4][...].astype(F32) + pieces[5][...].astype(F32)
    return total + jnp.concatenate([upper, lower], 0)


def scale_of(v):
    return lax.rsqrt(jnp.mean(v * v, 1, keepdims=True) + EPS)


def residual_kernel(x, *refs):
    resid = x[...].astype(F32) + summed(refs[:6])
    refs[6][...] = resid
    refs[7][...] = (resid * scale_of(resid)).astype(BF16)


def d_residual_kernel(dy, resid_ref, *refs):
    resid, d_n = resid_ref[...], summed(refs[:6])
    r = scale_of(resid)
    n = resid * r
    d = dy[...].astype(F32) + r * (d_n - n * jnp.mean(d_n * n, 1, keepdims=True))
    refs[6][...] = d
    refs[7][...] = d.astype(BF16)


def input_kernel(x_ref, d_resid, *refs):
    x, d_x = x_ref[...].astype(F32), summed(refs[:6])
    n = x * scale_of(x)
    refs[6][0] = d_resid[...] + d_x - n * jnp.mean(d_x * n, 1, keepdims=True)


def output_kernel(resid, *refs):
    refs[6][0] = resid[...] + summed(refs[:6])


def pack_tile(first, second):
    return [jnp.concatenate([first[:, c : c + 64], second[:, c : c + 64]], 1) for c in (0, 64)]


def over_blocks(info, left, rights, total):
    for r in range(8):
        more = mm_tn(left[r], rights.rows(r * 256, 256))
        total[...] = more if r == 0 else total[...] + more


def qkv_grads_kernel(info, e_ref, xs, out, total):
    over_blocks(info, e_ref, xs, total)
    if len(out.shape) == 2:
        out[...] = total[...].astype(BF16)
        return
    for k in range(4):
        z = jnp.bitwise_and(info[2] + k, 3)
        for yc in range(4):
            tile = total[:, pl.ds(pl.multiple_of((z * 4 + yc) * 128, 128), 128)].astype(BF16)
            pair = [
                jnp.concatenate([tile[dst : dst + c] for m, _, dst, c in LAYOUT_HEADS if m == i], 0) for i in (0, 1)
            ]
            out[k, yc], out[k, 4 + yc] = pack_tile(*pair)


def out_grads_kernel(info, mixed_ref, dbs, *refs):
    outs, total = refs[:-1], refs[-1]
    over_blocks(info, mixed_ref, dbs, total)
    if len(outs) == 1:
        outs[0][...] = total[...].astype(BF16)
        return
    for i in range(HP):
        for out, half in ((outs[0], info[3]), (outs[1], 1 - info[3])):
            out[i] = total[pl.ds(pl.multiple_of(i * DV + half * 64, 64), 64), :].astype(BF16)


def mlp_kernel(sizes, info, ns, w_gu, dys, wd, *refs):
    k = len(sizes)
    outs, dns, (hid_ref, dg_ref, du_ref) = refs[:k], refs[k : 2 * k], refs[2 * k :]
    ff, rows = wd.shape[0], 256
    starts = [sum(sizes[:i]) for i in range(len(sizes))]

    def put(refs, at, value):
        for ref, start, size in zip(refs, starts, sizes):
            if at <= start < at + rows:
                ref[...] = value[start - at : start - at + size]
                ref.leave()

    for at in range(0, sum(sizes), rows):
        n, dy = ns.rows(at, rows), dys.rows(at, rows)
        gate, up, d_hid = mm_nt(n, w_gu[:ff]), mm_nt(n, w_gu[ff:]), mm_nt(dy, wd[...])
        sig = 1.0 / (1.0 + jnp.exp(-gate))
        silu = gate * sig
        hid = (silu * up).astype(BF16)
        dg = (d_hid * up * sig * (1.0 + gate * (1.0 - sig))).astype(BF16)
        du = (d_hid * silu).astype(BF16)
        hid_ref[at : at + rows] = hid
        dg_ref[at : at + rows] = dg
        du_ref[at : at + rows] = du
        if at + rows == sum(sizes):
            for ref in (hid_ref, dg_ref, du_ref):
                ref.leave()
        put(dns, at, (mm(dg, w_gu[:ff]) + mm(du, w_gu[ff:])).astype(BF16))
        put(outs, at, mm(hid, wd[...]).astype(BF16))


def turn_over(left, scratch):
    for q in range(0, 2048, 512):
        scratch[:, q : q + 512] = left.rows(q, 512).T


def hidden_grads_kernel(info, dgs, dus, ns, out, dg_t, du_t):
    turn_over(dgs, dg_t)
    turn_over(dus, du_t)
    right = ns.ready()

    def step(i, carry):
        tile = right[:, pl.ds(pl.multiple_of(i * 256, 256), 256)]
        gate, up = mm(dg_t[...], tile).astype(BF16), mm(du_t[...], tile).astype(BF16)
        for j in range(2):
            cols = slice(j * 128, (j + 1) * 128)
            for x, slab in enumerate(pack_tile(gate[:, cols], up[:, cols])):
                out[(i // 2) * 8 + x * 4 + (i % 2) * 2 + j] = slab
        return carry

    lax.fori_loop(0, 8, step, 0)


def plain_grads_kernel(info, lefts, rights, out, left_t):
    turn_over(lefts, left_t)
    right = rights.ready()

    def step(i, carry):
        cols = pl.ds(pl.multiple_of(i * 256, 256), 256)
        out[:, cols] = mm(left_t[...], right[:, cols]).astype(BF16)
        return carry

    lax.fori_loop(0, out.shape[1] // 256, step, 0)


class Arriving:
    def __init__(self, parts, buf, sems, first):
        self.buf, self.shape, self.copies, row = buf, buf.shape, [], 0
        for i, part in enumerate(parts):
            rows = buf if len(parts) == 1 else buf.at[pl.ds(row, part.shape[0])]
            copy = pltpu.make_async_copy(part, rows, sems.at[first + i])
            copy.start()
            self.copies.append([row, part.shape[0], copy])
            row += part.shape[0]

    def ready(self, start=None, stop=None):
        for entry in list(self.copies):
            if start is None or (entry[0] < stop and start < entry[0] + entry[1]):
                entry[2].wait()
                self.copies.remove(entry)
        return self.buf

    def rows(self, start, count):
        return self.ready(start, start + count)[start : start + count]

    def __getitem__(self, at):
        return self.ready()[at]


class Leaving:
    def __init__(self, out, buf, sem):
        self.buf, self.shape, self.dtype = buf, buf.shape, buf.dtype
        self.copy, self.left = pltpu.make_async_copy(buf, out, sem), False

    def __getitem__(self, at):
        return self.buf[at]

    def __setitem__(self, at, value):
        self.buf[at] = value

    def leave(self):
        if not self.left:
            self.copy.start()
            self.left = True


def call(kernel, args, outs, scratch=(), flops=0, vmem=40):
    shapes = tuple(jax.ShapeDtypeStruct(s, t) for s, t in outs)
    flat = [a for arg in args for a in (arg if isinstance(arg, list) else [arg])]
    moved = sum(a.size * a.dtype.itemsize for a in flat) + sum(s.size * s.dtype.itemsize for s in shapes)
    groups = [arg if isinstance(arg, list) else [arg] for arg in args]
    large = [g for g in groups if g[0].dtype != jnp.int32]
    bufs = [pltpu.VMEM((sum(a.shape[0] for a in g),) + g[0].shape[1:], g[0].dtype) for g in large]
    n_in = sum(len(g) for g in large)

    def body(*refs):
        refs = list(refs)
        take = lambda n: [refs.pop(0) for _ in range(n)]
        ins, results, in_bufs, out_bufs = take(len(flat)), take(len(outs)), take(len(large)), take(len(outs))
        mine, (in_sems, out_sems) = take(len(scratch)), refs
        given, at, sem, buf = [], 0, 0, 0
        for g in groups:
            parts = ins[at : at + len(g)]
            at += len(g)
            if g[0].dtype == jnp.int32:
                given.append(parts[0])
                continue
            given.append(Arriving(parts, in_bufs[buf], in_sems, sem))
            sem, buf = sem + len(g), buf + 1
        going = [Leaving(r, b, out_sems.at[i]) for i, (r, b) in enumerate(zip(results, out_bufs))]
        kernel(*given, *going, *mine)
        for out in going:
            out.leave()
        for out in going:
            out.copy.wait()
        for arrival in given:
            if isinstance(arrival, Arriving):
                arrival.ready()

    return pl.pallas_call(
        body,
        out_shape=tuple(pltpu.HBM(s, t) for s, t in outs),
        in_specs=[pl.BlockSpec(memory_space=pltpu.SMEM if a.dtype == jnp.int32 else pltpu.HBM) for a in flat],
        out_specs=[pl.BlockSpec(memory_space=pltpu.HBM)] * len(outs),
        scratch_shapes=[
            *bufs,
            *[pltpu.VMEM(s, t) for s, t in outs],
            *scratch,
            pltpu.SemaphoreType.DMA((max(n_in, 1),)),
            pltpu.SemaphoreType.DMA((len(outs),)),
        ],
        compiler_params=pltpu.CompilerParams(vmem_limit_bytes=vmem << 20),
        cost_estimate=pl.CostEstimate(flops=flops, bytes_accessed=moved, transcendentals=0),
    )(*[a if a.dtype == jnp.int32 else pltpu.with_memory_space_constraint(a, pltpu.HBM) for a in flat])


def state_scratch(groups):
    return pltpu.VMEM((groups, HP, FEAT, 2 * DV), F32)


TOKENS = [((n, 2048), BF16) for _, _, n in SLOTS]


OWN, NEXT, LAST = slice(0, 2), slice(2, 6), slice(6, 10)


def mlp(info, ns, dys, w_gu, wd):
    ff, d = wd.shape
    sizes = [n.shape[0] for n in ns]
    blocks = [((n, d), BF16) for n in sizes]
    rows, k = sum(sizes), len(ns)
    got = call(
        functools.partial(mlp_kernel, sizes),
        [info, list(ns), w_gu, list(dys), wd],
        blocks + blocks + [((rows, ff), BF16)] * 3,
        flops=12 * rows * ff * d,
    )
    return got[:k], got[k : 2 * k], got[2 * k :]


def turned(ff):
    return pltpu.VMEM((ff, 2048), BF16)


def plain_grads(info, rights, lefts):
    ff, d = lefts[0].shape[1], rights[0].shape[1]
    shapes, flops = [((ff, d), BF16)], 2 * 2048 * ff * d
    return call(plain_grads_kernel, [info, list(lefts), list(rights)], shapes, [turned(ff)], flops, 32)[0]


def hidden_grads(info, ns, dgs, dus):
    ff, d = dgs[0].shape[1], ns[0].shape[1]
    args, shapes = [info, list(dgs), list(dus), list(ns)], [((d // 64, ff, 128), BF16)]
    got = call(hidden_grads_kernel, args, shapes, [turned(ff)] * 2, 4 * 2048 * ff * d, 36)[0]
    return got.reshape(4, 8, ff, 128)


def down_grads(info, dys, hids):
    return plain_grads(info, dys, hids).reshape(4, -1, dys[0].shape[1])


def gained(gain, w):
    return (gain * w.astype(F32)).astype(BF16)


def head_slabs(split, gain, w_query, w_key, w_value):
    parts = [split(gained(gain, w), n) for w, n in ((w_value, DV), (w_query, FD), (w_key, FD))]
    return jnp.concatenate(parts, 2).transpose(0, 2, 1, 3).reshape(8, ROWS, -1)


def project(groups, slots, info, xs, w_qkv, maps_t, before=None):
    size, d, n = 256, w_qkv.shape[1], len(slots)
    return call(
        functools.partial(project_kernel, groups, slots),
        [info, w_qkv, list(xs), maps_t] + ([] if before is None else [before]),
        [((n, size, 128), F32), ((n, size, QK), BF16), ((groups, HP, SENT, DV), BF16)],
        [state_scratch(groups)],
        flops=2 * n * size * d * WIDE,
    )


def attend(groups, info, tile, values, enter, maps, maps_t, w_out):
    size, d = 256, w_out.shape[1]
    got = call(
        functools.partial(attend_kernel, groups),
        [info, tile, values, enter, maps, maps_t, w_out],
        [((8, size, QK), BF16), ((8, size, 128), F32), ((8, HP, FEAT, 2 * DV), BF16)] + TOKENS,
        [state_scratch(groups)],
        flops=2 * 8 * size * d * QK,
    )
    return got[:3], got[3:]


def back_state(groups, slots, info, dbs, w_out, mixed, den, tile, maps_t, before=None):
    size, d, n = 256, w_out.shape[1], len(slots)
    return call(
        functools.partial(back_state_kernel, groups, slots),
        [info, w_out, tile, den, mixed, maps_t, list(dbs)] + ([] if before is None else [before]),
        [((n, size, QK), BF16), ((n, size, 128), F32), ((groups, HP, SENT, DV), BF16)],
        [state_scratch(groups)],
        flops=2 * n * size * d * QK,
    )


def back(groups, info, tile, values, d_num, d_den, before, later, maps, w_qkv):
    size, d = 256, w_qkv.shape[1]
    got = call(
        functools.partial(back_kernel, groups),
        [info, tile, values, d_num, d_den, before, later, maps, w_qkv],
        [((8, size, WIDE), BF16)] + TOKENS,
        [state_scratch(groups)],
        flops=2 * 8 * size * d * WIDE,
        vmem=28,
    )
    return got[0], got[1:]


def qkv_grads(info, xs, e, packed):
    d = xs[0].shape[1]
    outs = [((4, 8, ROWS, 128) if packed else (WIDE, d), BF16)]
    return call(qkv_grads_kernel, [info, e, list(xs)], outs, [pltpu.VMEM((WIDE, d), F32)], flops=2 * 2048 * d * WIDE)[0]


def out_grads(info, dbs, mixed, packed):
    d = dbs[0].shape[1]
    outs = [((HP, 64, d), BF16)] * 2 if packed else [((QK, d), BF16)]
    return call(out_grads_kernel, [info, mixed, list(dbs)], outs, [pltpu.VMEM((QK, d), F32)], flops=2 * 2048 * d * QK)


def unpack(info, pieces, layout, height):
    turned_by = len(pieces) > 1
    kernel = functools.partial(unpack_kernel, layout, turned_by)
    return call(kernel, [info, *pieces], [((height, 16 * 128), BF16)])[0]


def total(groups, shape, dtype):
    args = [c for g in groups for c in g]
    return call(functools.partial(total_kernel, [len(g) for g in groups]), args, [(shape, dtype)])[0]


def finish_residual(x, pieces):
    return call(residual_kernel, [x, *pieces], [(x.shape, F32), (x.shape, BF16)])


def finish_d_residual(dy, resid, pieces):
    return call(d_residual_kernel, [dy, resid, *pieces], [(dy.shape, F32), (dy.shape, BF16)])


def finish_input(x, d_resid, pieces):
    return call(input_kernel, [x, d_resid, *pieces], [((1,) + x.shape, F32)])[0]


def finish_output(resid, pieces):
    return call(output_kernel, [resid, *pieces], [((1,) + resid.shape, F32)])[0]


def hidden_out(slabs, w_gate, w_up, gain):
    ff = w_gate.shape[1]
    outs = [((64, ff), F32), ((64, ff), F32), ((64, 128), F32)]
    gate, up, one = call(hidden_out_kernel, [slabs, w_gate, w_up, gain], outs, [pltpu.VMEM((ff, 128), BF16)])
    return one[:, 0], gate, up


def heads_out(slabs, w_query, w_key, w_value, gain):
    outs = [(w.shape, F32) for w in (w_query, w_key, w_value)] + [((64, 128), F32)]
    scratch = [pltpu.VMEM((2, H * FD, 128), F32)]
    query, key, value, one = call(heads_out_kernel, [slabs, w_query, w_key, w_value, gain], outs, scratch)
    return one[:, 0], query, key, value


def gather_all(own, a):
    near = near_tokens(own, a)
    far = far_tokens(near, a)
    return in_slots(near, far, last_tokens(far))


def scatter_all(p, a):
    nears = near_cores(p)
    via = send_far(p, far_cores(p), a)
    return terms(p, nears, send_first(p, nears, a), send_second(p, nears, via, a))


def weight_grads(weights, gains, grads):
    g_query, g_key, g_value, g_gate, g_up = grads
    along = [jnp.sum(w.astype(F32) * g, -1) for w, g in zip(weights, grads)]
    one, two = along[0] + along[1] + along[2], along[3] + along[4]
    return one, gains[0] * g_query, gains[0] * g_key, gains[0] * g_value, two, gains[1] * g_gate, gains[1] * g_up


def split_of_heads(join, g_heads):
    g = g_heads.astype(F32).reshape(8, ROWS, HP, -1).transpose(0, 2, 1, 3)
    return join(g[:, :, DV : DV + FD], FD), join(g[:, :, DV + FD :], FD), join(g[:, :, :DV], DV)


def on_device(
    run, tokens, seq_lengths, norm_gain, w_query, w_key, w_value, w_out, mlp_gain, w_gate, w_up, w_down, cotangent
):
    gains = [g.astype(F32)[:, None] for g in (norm_gain, mlp_gain)]
    maps, maps_t = jnp.asarray(MAPS, BF16), jnp.asarray(MAPS.transpose(0, 1, 3, 2), BF16)
    weights = (w_query, w_key, w_value, w_gate, w_up)
    block_out, input_grad, g, g_out, g_down = run(
        tokens[0], cotangent[0], seq_lengths, gains, weights, w_out, w_down, maps, maps_t
    )
    return block_out, input_grad, *g[:4], g_out, *g[4:], g_down


def plain(x, dy, lengths, gains, weights, w_out, w_down, maps, maps_t):
    w_query, w_key, w_value, w_gate, w_up = weights
    place = jnp.stack([lax.axis_index(TP), lax.axis_index("h") * 8 * x.shape[0], 0, 0])
    info = jnp.concatenate([place.astype(jnp.int32), lengths[0]])
    heads = over_both(exchange(head_slabs(split_heads, gains[0], w_query, w_key, w_value), TP))
    w_qkv = slabs_to_rows(heads, LAYOUT_HEADS, WIDE)
    w_out_mine = out_rows_in(over_both(w_out))
    hid = over_both(exchange(split_hidden(gained(gains[1], w_gate), gained(gains[1], w_up)), TP))
    wd = over_both(w_down).reshape(-1, x.shape[1])
    ff = wd.shape[0]
    w_gu = slabs_to_rows(hid, layout_hidden(ff), 2 * ff)
    xs = gather_all(x, "l")
    tile, values, state = project(1, NEAR + FAR, info, xs, w_qkv, maps_t)
    (mixed, den, before), p = attend(1, info, tile, values, entering(state, False), maps, maps_t, w_out_mine)
    resid, n_low = finish_residual(x, scatter_all(p, "l"))
    ns, dys = gather_all(n_low, "l"), gather_all(dy, "l")
    ran = [mlp(info, ns[c], dys[c], w_gu, wd) for c in (OWN, NEXT, LAST)]
    hids, dgs, dus = [[r[2][i] for r in ran] for i in range(3)]
    block_out = finish_output(resid, scatter_all([b for r in ran for b in r[0]], "l"))
    d_resid, d_low = finish_d_residual(dy, resid, scatter_all([b for r in ran for b in r[1]], "l"))
    grads = jnp.concatenate([plain_grads(info, ns, dgs), plain_grads(info, ns, dus)], 0)
    g_hid = exchange(sum_both(rows_to_slabs(grads, layout_hidden(ff))).astype(BF16), TP)
    g_down = sum_both(plain_grads(info, dys, hids).reshape(*hid.shape[:2], -1, x.shape[1]))
    dbs = gather_all(d_low, "l")
    d_num, d_den, use = back_state(1, NEAR + FAR, info, dbs, w_out_mine, mixed, den, tile, maps_t)
    e, p = back(1, info, tile, values, d_num, d_den, before, entering(use, True), maps, w_qkv)
    input_grad = finish_input(x, d_resid, scatter_all(p, "l"))
    g_out = sum_both(out_rows_out(out_grads(info, dbs, mixed, False)[0]))
    g_heads = exchange(sum_both(rows_to_slabs(qkv_grads(info, xs, e, False), LAYOUT_HEADS)).astype(BF16), TP)
    grads = (*split_of_heads(join_heads, g_heads), *join_hidden(g_hid.astype(F32)))
    return block_out, input_grad, weight_grads(weights, gains, grads), g_out, g_down


EIGHT = ("x", "y", "c")


def split_heads_z(w, width):
    rows = w.shape[0]
    return w.T.reshape(2, HP, 4, width, rows).transpose(0, 2, 1, 3, 4).reshape(8, HP, width, rows)


def split_hidden_z(first, second):
    w = jnp.concatenate([first, second], 0).T.reshape(4, 4, 2, -1, 128)
    return w.transpose(2, 1, 0, 3, 4).reshape(8, -1, 128)


def scheduled(x, dy, lengths, gains, weights, w_out, w_down, maps, maps_t):
    w_query, w_key, w_value, w_gate, w_up = weights
    d_model = x.shape[1]
    z, my_x = lax.axis_index("z"), lax.axis_index("x")
    place = jnp.stack([lax.axis_index(EIGHT), z * 4 * x.shape[0], z, my_x]).astype(jnp.int32)
    o = Order(place)
    ax = "x"

    low = jnp.concatenate([lengths[0] % 256, lengths[0] // 256]).astype(BF16)
    low = jnp.broadcast_to(jnp.pad(low, (0, 120)), (8, 16, 128))
    heads = jnp.concatenate([head_slabs(split_heads_z, gains[0], w_query, w_key, w_value), low], 1)
    halves = line_gather(w_out)
    heads = exchange(heads, EIGHT)
    heads, x_sent, w_gate, w_up = o.at(heads, x, w_gate, w_up)
    near = chips_near(x_sent, ax)
    sent = heads[::4, ROWS, :8].astype(jnp.int32)
    info = jnp.concatenate([place, (sent[:, :4] + 256 * sent[:, 4:]).reshape(-1)])
    heads = ring(heads)
    hid = split_hidden_z(gained(gains[1], w_gate), gained(gains[1], w_up))
    heads, near, hid, x_sent, halves = o.at(heads, near, hid, x_sent, halves)
    cores = cores_of(near)
    near[3] = swap(x_sent, "c")
    wd = line_gather(w_down)
    w_qkv = unpack(info, heads, LAYOUT_HEADS, WIDE)
    near[3], cores, w_qkv = o.at(near[3], cores, w_qkv)
    far = chip_far(near, ax)
    xs = in_slots(near, far + cores, [None] * 2)
    one = project(2, NEAR, info, xs[:6], w_qkv, maps_t)
    one, far, hid = o.at(one, far, hid)
    last = last_tokens(far)
    hid = exchange(hid, EIGHT)
    w_out_near, w_out_far = call(sort_heads_kernel, [info, halves], [((HP, 64, d_model), BF16)] * 2)
    last, w_out_near, w_out_far = o.at(last, w_out_near, w_out_far)
    xs = in_slots(near, far + cores, last)

    two = project(2, FAR, info, xs[6:], w_qkv, maps_t, one[2])
    two, = o.at(two)
    tile, values = [one[0], two[0]], [one[1], two[1]]
    enter = entering_line(two[2], False)
    w_out_other = swap(w_out_far, "x")
    enter, w_out_other, wd, hid, dy = o.at(enter, w_out_other, wd, hid, dy)
    hid = line_gather(hid)
    w_out_mine = call(join_halves_kernel, [info, w_out_near, w_out_other], [((QK, d_model), BF16)])[0]
    dy_near = near_tokens(dy, ax)
    (mixed, den, before), p = attend(2, info, tile, values, enter, maps, maps_t, w_out_mine)
    p, mixed, den, before = o.at(p, mixed, den, before)
    fars = far_cores(p)
    fars, dy_near = o.at(fars, dy_near)
    via = send_far(p, fars, ax)
    nears = near_cores(p)
    via, nears = o.at(via, nears)
    first = send_first(p, nears, ax)
    first, = o.at(first)
    second = send_second(p, nears, via, ax)
    dy_cores = cores_of(dy_near)
    second, dy_cores = o.at(second, dy_cores)
    resid, n_low = finish_residual(x, terms(p, nears, first, second))
    resid, n_low = o.at(resid, n_low)

    near = near_tokens(n_low, ax)
    near, = o.at(near)
    far, cores = chip_far(near, ax), cores_of(near)
    wd = wd.reshape(-1, d_model)
    ff = wd.shape[0]
    w_gu = unpack(info, [hid], layout_hidden(ff), 2 * ff)
    ns, dys = in_slots(near, far + cores, [None] * 2), [dy_near[0], dy_near[3]]
    run = lambda c: mlp(info, ns[c], dys[c], w_gu, wd)
    far, cores, w_gu, dy_near = o.at(far, cores, w_gu, dy_near)
    last, dy_far = last_tokens(far), chip_far(dy_near, ax)
    ran = [run(OWN)]
    ran, last, dy_far = o.at(ran, last, dy_far)
    ns, dys = in_slots(near, far + cores, last), in_slots(dy_near, dy_far + dy_cores, [None] * 2)
    dy_last = last_tokens(dy_far)
    ran.append(run(NEXT))
    ran, dy_last = o.at(ran, dy_last)
    ns, dys = in_slots(near, far + cores, last), in_slots(dy_near, dy_far + dy_cores, dy_last)
    p = [b for r in ran for b in r[1]]
    nears = near_cores(p)
    ran.append(run(LAST))
    ran, nears = o.at(ran, nears)
    p = [b for r in ran for b in r[1]]
    outs = [b for r in ran for b in r[0]]
    parts = lambda i: [r[2][i] for r in ran]
    fars = far_cores(p)
    fars, outs = o.at(fars, outs)
    via = send_far(p, fars, ax)
    g_down = down_grads(info, dys, parts(0))
    via, g_down = o.at(via, g_down)
    g_down = line_sum(g_down)
    first = send_first(p, nears, ax)
    first, = o.at(first)
    second = send_second(p, nears, via, ax)
    second, = o.at(second)
    d_resid, d_low = finish_d_residual(dy, resid, terms(p, nears, first, second))
    d_resid, d_low = o.at(d_resid, d_low)

    near = near_tokens(d_low, ax)
    g_hid = hidden_grads(info, ns, parts(1), parts(2))
    near, g_hid = o.at(near, g_hid)
    cores = cores_of(near)
    cores, g_down, g_hid = o.at(cores, g_down, g_hid)
    g_hid = line_sum(g_hid)
    far = chip_far(near, ax)
    dbs = in_slots(near, far + cores, [None] * 2)
    one = back_state(2, NEAR, info, dbs[:6], w_out_mine, mixed, den, tile, maps_t)
    one, far = o.at(one, far)
    last = last_tokens(far)
    last, outs = o.at(last, outs)
    o_nears, o_fars = near_cores(outs), far_cores(outs)
    dbs = in_slots(near, far + cores, last)
    two = back_state(2, FAR, info, dbs[6:], w_out_mine, mixed, den, tile, maps_t, one[2])
    two, o_nears, o_fars = o.at(two, o_nears, o_fars)
    d_num, d_den = [one[0], two[0]], [one[1], two[1]]
    later = entering_line(two[2], True)
    out_near, out_far = out_grads(info, dbs, mixed, True)
    o_via = send_far(outs, o_fars, ax)
    later, out_far, o_via = o.at(later, out_far, o_via)
    out_other = swap(out_far, "x")
    o_first = send_first(outs, o_nears, ax)
    o_second = send_second(outs, o_nears, o_via, ax)
    e, p = back(2, info, tile, values, d_num, d_den, before, later, maps, w_qkv)
    e, p, out_other, o_first, o_second = o.at(e, p, out_other, o_first, o_second)
    steps = lambda a: [a[i] for i in range(4)]
    nears, fars = near_cores(p), far_cores(p)
    head_g = qkv_grads(info, xs, e, True)
    nears, fars, head_g = o.at(nears, fars, head_g)
    heads = ring_sum(steps(head_g))
    via = send_far(p, fars, ax)
    g_hid = exchange(g_hid, EIGHT)
    g_out = call(by_z_kernel, [info, out_near, out_other], [((4, 64, d_model), BF16)])[0]
    via, heads[1:3], g_hid, g_out = o.at(via, heads[1:3], g_hid, g_out)
    first = send_first(p, nears, ax)
    hid_out = hidden_out(g_hid, w_gate, w_up, gains[1])
    first, heads[3], hid_out, g_out = o.at(first, heads[3], hid_out, g_out)
    g_out = line_sum(g_out)
    g_heads = exchange(total([[a] for a in heads], heads[0].shape, BF16), EIGHT)
    second = send_second(p, nears, via, ax)
    block_out = finish_output(resid, terms(outs, o_nears, o_first, o_second))
    second, g_heads, block_out = o.at(second, g_heads, block_out)
    input_grad = finish_input(x, d_resid, terms(p, nears, first, second))
    head_out = heads_out(g_heads, w_query, w_key, w_value, gains[0])
    return block_out, input_grad, (*head_out, *hid_out), g_out.astype(F32), g_down.astype(F32)


def solution(mesh):
    seq, fsdp = mesh.shape["seq"], mesh.shape["fsdp"]
    if (seq, fsdp) == (16, 2):
        shape, along, run = (4, 2, 2, 2), ("z", "y", "c"), scheduled
    else:
        shape, along, run = (seq // 8, 2, 2, 2, fsdp), ("h", "l", "y", "c"), plain
    fine = Mesh(mesh.devices.reshape(shape), along + ("x",))
    token, vec, mat = P("x", along, None), P(along + ("x",)), P(along + ("x",), None)
    return jax.shard_map(
        functools.partial(on_device, run),
        mesh=fine,
        in_specs=(token, P("x", None), vec, mat, mat, mat, mat, vec, mat, mat, mat, token),
        out_specs=(token, token, vec, mat, mat, mat, mat, vec, mat, mat, mat),
        check_vma=False,
    )
```
